32 devices in a mesh: fsdp: 8 (over z, core), replica: 4 (over y, x).
Axes of the slice: x: 2, y: 2, z: 4, core: 2. Of those that a mesh axis runs over, the one named last changes fastest.
Arguments:
- grads: bfloat16 [4, 2304, 18432], P('replica', 'fsdp'), may hold values from -5 to 5
- slots: int32 [4, 32], replicated, may hold values from 0 to 31, each once within a row
- stats_left: float32 [4, 32, 2, 4, 72, 576], P(None, 'fsdp', None, 'replica'), may hold values from -6 to 6
- stats_right: float32 [4, 32, 2, 4, 72, 576], P(None, 'fsdp', None, 'replica'), may hold values from -6 to 6
- root_left: bfloat16 [4, 32, 2, 4, 72, 576], P(None, 'fsdp', None, 'replica'), may hold values from -0.25 to 0.25
- root_right: bfloat16 [4, 32, 2, 4, 72, 576], P(None, 'fsdp', None, 'replica'), may hold values from -0.25 to 0.25
- second_moment: float32 [4, 32, 2, 4, 72, 576], P(None, 'fsdp', None, 'replica'), may hold values from 0.25 to 60, as said below
Outputs:
- update: bfloat16 [2304, 18432], P('fsdp')
- left_new: float32 [4, 32, 2, 4, 72, 576], P(None, 'fsdp', None, 'replica')
- right_new: float32 [4, 32, 2, 4, 72, 576], P(None, 'fsdp', None, 'replica')
- moment_new: float32 [4, 32, 2, 4, 72, 576], P(None, 'fsdp', None, 'replica')
The draws below stay inside these ranges and needn't reach their ends.
Inputs may be any that keep to these rules, and one draw needn't show every extreme that they name: Each row of slots names every slot 0 to 31 once; slot s of a block row is held by fsdp index s // 4. `second_moment`: positive entries.
All inputs are finite; a program needn't handle non-finite values.
Results may differ from the reference program's by a relative error of at most 0.014.
Values may be sent and summed in bfloat16 or wider, within the bound.
No kernel may reach another device: no remote copies, remote signals or barrier semaphores. Data moves between devices by JAX's collectives and lax.ppermute only.
A program may use at most 256 MiB of HBM per device.

```python
import math
import jax
import jax.numpy as jnp
from jax import lax

D = 2304
FF = 18432
B = 576
NBR = 4
NBC = 32
NREP = 4
RD = 72
SUBF = 2


def draw_second_moment(key, part):
    key = jax.random.fold_in(key, 11)
    array_shape = (NBR, NBC, SUBF, NREP, RD, B)
    position = jnp.arange(NREP, dtype=jnp.float32) / max(NREP - 1, 1)
    base_draw = jnp.exp(jax.random.uniform(key, array_shape, jnp.float32, math.log(0.5), math.log(2.0)))
    scale_span = 9.0
    row_factor = jnp.power(scale_span, 1.0 - position).reshape(1, 1, 1, NREP, 1, 1)
    return (base_draw * row_factor).astype(jnp.float32)


def level_of(key, dims, pieces, low, top_value):
    def one(axis_at, shards_of):
        steps = jax.random.uniform(jax.random.fold_in(jax.random.fold_in(key, 6), axis_at), (shards_of,), jnp.float32, low / len(pieces), top_value / len(pieces))
        return jnp.repeat(jnp.exp(steps), dims[axis_at] // shards_of).reshape((-1,) + (1,) * (len(dims) - axis_at - 1))

    level = one(*pieces[0])
    for cut in pieces[1:]:
        level = level * one(*cut)
    return level


def scatter_about(own_key, shape, width, most, split=(), kind=jnp.bfloat16):
    result = jax.random.normal(own_key, shape, jnp.float32) * width
    if len(split) > 0:
        result = level_of(own_key, shape, split, -0.22, 0.18) * result
    return jnp.clip(result, min=-most, max=most).astype(kind)


def setup_inputs(seed: int = 0) -> dict:
    seeds = jax.random.split(jax.random.key(seed), 8)
    grads = scatter_about(seeds[0], (NREP, D, FF), 0.35, 5.0, ((0, 4), (1, 8)))
    slots = jax.vmap(lambda own: jax.random.permutation(own, NBC))(jax.random.split(seeds[1], NBR)).reshape((NBR, NBC)).astype(jnp.int32)
    stats_left = scatter_about(seeds[2], (NBR, NBC, SUBF, NREP, RD, B), 1.0, 6.0, ((1, 8), (3, 4)), jnp.float32)
    stats_right = scatter_about(seeds[3], (NBR, NBC, SUBF, NREP, RD, B), 1.0, 6.0, ((1, 8), (3, 4)), jnp.float32)
    root_left = scatter_about(seeds[4], (NBR, NBC, SUBF, NREP, RD, B), B ** -0.5, 0.25, ((1, 8), (3, 4)))
    root_right = scatter_about(seeds[5], (NBR, NBC, SUBF, NREP, RD, B), B ** -0.5, 0.25, ((1, 8), (3, 4)))
    second_moment = draw_second_moment(jax.random.fold_in(seeds[7], 71), 0)
    return {"grads": grads, "slots": slots, "stats_left": stats_left, "stats_right": stats_right, "root_left": root_left, "root_right": root_right, "second_moment": second_moment}


def as_blocks(array_in):
    return array_in.reshape(D // B, FF // B, B, B)

def reference(grads, slots, stats_left, stats_right, root_left, root_right, second_moment):
    rows_blk = D // B
    cols_blk = FF // B
    grad_total = grads[0].astype(jnp.float32)
    for replica_item in range(1, NREP):
        grad_total = grad_total + grads[replica_item].astype(jnp.float32)
    summed_grad = grad_total.astype(jnp.bfloat16)
    blocks = summed_grad.reshape(rows_blk, B, cols_blk, B).transpose(0, 2, 1, 3)
    column_ids = jnp.arange(cols_blk, dtype=jnp.int32)
    matches = slots[:, None, :] == column_ids[None, :, None]
    slot_cols = lax.optimization_barrier(jnp.sum(jnp.where(matches, column_ids[None, None, :], 0), axis=2)).astype(jnp.int32)
    owned_blocks = jax.vmap(lambda block_set, index_row: block_set[index_row])(blocks, slot_cols)
    grad_float = owned_blocks.astype(jnp.float32)
    left_new = 0.95 * as_blocks(stats_left) + 0.05 * jnp.einsum('abmk,abnk->abmn', grad_float, grad_float)
    right_new = 0.95 * as_blocks(stats_right) + 0.05 * jnp.einsum('abkm,abkn->abmn', grad_float, grad_float)
    inner_left = jnp.einsum('abmk,abkn->abmn', as_blocks(root_left).astype(jnp.float32), grad_float).astype(jnp.bfloat16)
    direction = jnp.einsum('abmk,abkn->abmn', inner_left.astype(jnp.float32), as_blocks(root_right).astype(jnp.float32))
    moment = 0.95 * as_blocks(second_moment) + 0.05 * grad_float * grad_float
    adam_step = grad_float / (jnp.sqrt(moment) + 1e-08)
    graft_scale = jnp.sqrt(lax.optimization_barrier(jnp.sum(adam_step * adam_step, axis=(2, 3)))) / jnp.sqrt(lax.optimization_barrier(jnp.sum(direction * direction, axis=(2, 3))) + 1e-06)
    stepped = direction * graft_scale[:, :, None, None]
    col_blocks = jax.vmap(lambda block_set, index_row: block_set[index_row])(stepped, slots)
    update = col_blocks.transpose(0, 2, 1, 3).reshape(D, FF).astype(jnp.bfloat16)
    return (update, left_new.reshape(stats_left.shape), right_new.reshape(stats_right.shape), moment.reshape(second_moment.shape))
```

```python
import functools

import jax
import jax.numpy as jnp
from jax import lax
from jax.experimental import pallas as pl
from jax.experimental.pallas import tpu as pltpu
from jax.sharding import PartitionSpec as P

B = 576
VMEM = 56 * 1024 * 1024


def params():
    return pltpu.CompilerParams(vmem_limit_bytes=VMEM)


def cost(flops, moved):
    return pl.CostEstimate(flops=flops, bytes_accessed=moved, transcendentals=0)


def arrange_body(n_add, halves, half, cols, grad, *refs):
    adds, outs = refs[: n_add * 2], refs[n_add * 2 :]
    i = pl.program_id(0)
    hr = outs[0].shape[1]
    parity = lax.rem(cols[i], 2)

    def emit(out, terms):
        for side in range(2):

            @pl.when(parity == side)
            def _():
                part = grad[:, side * B : side * B + B]
                out[0, :, :B] = part[:hr]
                out[0, :, B:] = part[hr:]

        if terms:
            total = out[0].astype(jnp.float32)
            for term in terms:
                total = total + term[0].astype(jnp.float32)
            out[0] = total.astype(out.dtype)

    if halves or n_add:

        @pl.when(i < half)
        def _():
            emit(outs[0], adds[0::2])

        @pl.when(i >= half)
        def _():
            emit(outs[-1], adds[1::2])
    else:
        emit(outs[0], ())


def arrange(cols, grad, adds, halves):
    n = cols.shape[0]
    half = n // 2
    rows = grad.shape[0]
    hr, w = rows // 2, 2 * B
    low = pl.BlockSpec((1, hr, w), lambda i, c: (jnp.minimum(i, half - 1), 0, 0))
    high = pl.BlockSpec((1, hr, w), lambda i, c: (jnp.maximum(i - half, 0), 0, 0))
    whole = pl.BlockSpec((1, hr, w), lambda i, c: (i, 0, 0))
    out_specs = [low, high] if halves else [whole]
    out_rows = half if halves else n
    return pl.pallas_call(
        functools.partial(arrange_body, len(adds), halves, half),
        grid_spec=pltpu.PrefetchScalarGridSpec(
            num_scalar_prefetch=1,
            grid=(n,),
            in_specs=[pl.BlockSpec((rows, w), lambda i, c: (0, c[i] // 2))]
            + [low, high] * len(adds),
            out_specs=out_specs,
        ),
        out_shape=[jax.ShapeDtypeStruct((out_rows, hr, w), grad.dtype) for _ in out_specs],
        compiler_params=params(),
        cost_estimate=cost(0, n * rows * w * 2 * (2 + len(adds))),
    )(cols, grad, *[term for pair in adds for term in pair])


def pack_roots_body(js, left, right, *outs):
    m = pl.program_id(0)
    for k, out in enumerate(outs):

        @pl.when(m == k)
        def _():
            for kind, ref in enumerate((left, right)):
                for q in range(2):
                    out[kind, 0, :, q * B : q * B + B] = ref[q, 0]


def visit(k, m, p, last):
    return jnp.where(m == k, p, jnp.where(m < k, 0, last))


def pack_roots(js, left, right):
    blocks, _, rows, _ = left.shape
    pairs, n, w = blocks // 2, js.shape[0], 2 * B
    source = pl.BlockSpec((2, 1, rows, B), lambda m, p, j: (p, j[m], 0, 0))
    return pl.pallas_call(
        pack_roots_body,
        grid_spec=pltpu.PrefetchScalarGridSpec(
            num_scalar_prefetch=1,
            grid=(n, pairs),
            in_specs=[source, source],
            out_specs=[
                pl.BlockSpec(
                    (2, 1, rows, w),
                    lambda m, p, j, k=k: (0, visit(k, m, p, pairs - 1), 0, 0),
                )
                for k in range(n)
            ],
        ),
        out_shape=[jax.ShapeDtypeStruct((2, pairs, rows, w), left.dtype)] * n,
        compiler_params=params(),
        cost_estimate=cost(0, 4 * left.size * 2),
    )(js, left, right)


def dot(x, y, dims):
    return lax.dot_general(x, y, (dims, ((), ())), preferred_element_type=jnp.float32)


def precondition_body(n, rd, js, grad, *refs):
    roots, outs = refs[:n], refs[n : 2 * n]
    direction_out, square_out, g16, g32, l32, r32 = refs[2 * n :]
    hr = grad.shape[1]
    for q in range(2):
        for h in range(2):
            for side in range(2):
                g16[h * 2 * hr + side * hr : h * 2 * hr + side * hr + hr, :] = grad[
                    2 * q + h, :, side * B : side * B + B
                ]
        for k in range(n):
            for kind, full in enumerate((l32, r32)):
                part = roots[k][kind, 0, :, q * B : q * B + B].astype(jnp.float32)
                for h in range(2):
                    start = pl.multiple_of(h * 2 * hr + js[k] * rd, 8)
                    full[pl.ds(start, rd), :] = part[h * rd : h * rd + rd]
        g = g16[...]
        inner = dot(l32[...].astype(jnp.bfloat16), g, ((1,), (0,))).astype(jnp.bfloat16)
        direction = dot(inner, r32[...].astype(jnp.bfloat16), ((1,), (0,)))
        square_out[0, q : q + 1, :] = jnp.full((1, 128), jnp.sum(direction * direction))
        direction = direction.astype(jnp.bfloat16)
        for h in range(2):
            for side in range(2):
                start = h * 2 * hr + side * hr
                direction_out[2 * q + h, :, side * B : side * B + B] = direction[start : start + hr]
        g32[...] = g.astype(jnp.float32)
        l32[...] = dot(g, g, ((1,), (1,)))
        r32[...] = dot(g, g, ((0,), (0,)))
        for k in range(n):
            for kind, full in enumerate((g32, l32, r32)):
                parts = [
                    full[pl.ds(pl.multiple_of(h * 2 * hr + js[k] * rd, 8), rd), :] for h in range(2)
                ]
                outs[k][kind, 0, :, q * B : q * B + B] = jnp.concatenate(parts, axis=0).astype(
                    jnp.bfloat16
                )


def precondition(js, grad, roots, rd):
    n = js.shape[0]
    count, hr, w = grad.shape
    pairs, rows = roots[0].shape[1], roots[0].shape[2]
    return pl.pallas_call(
        functools.partial(precondition_body, n, rd),
        grid_spec=pltpu.PrefetchScalarGridSpec(
            num_scalar_prefetch=1,
            grid=(pairs,),
            in_specs=[pl.BlockSpec((4, hr, w), lambda p, j: (p, 0, 0))]
            + [pl.BlockSpec((2, 1, rows, w), lambda p, j: (0, p, 0, 0))] * n,
            out_specs=[pl.BlockSpec((3, 1, rows, w), lambda p, j: (0, p, 0, 0))] * n
            + [
                pl.BlockSpec((4, hr, w), lambda p, j: (p, 0, 0)),
                pl.BlockSpec((1, 8, 128), lambda p, j: (p, 0, 0)),
            ],
            scratch_shapes=[pltpu.VMEM((B, B), jnp.bfloat16)] + [pltpu.VMEM((B, B), jnp.float32)] * 3,
        ),
        out_shape=[jax.ShapeDtypeStruct((3, pairs, rows, w), jnp.bfloat16)] * n
        + [
            jax.ShapeDtypeStruct((count, hr, w), jnp.bfloat16),
            jax.ShapeDtypeStruct((pairs, 8, 128), jnp.float32),
        ],
        compiler_params=params(),
        cost_estimate=cost(pairs * 16 * B**3, pairs * B * B * 2 * 14),
    )(js, grad, *roots)


def statistics_body(n, js, *refs):
    received = refs[:n]
    left, right, moment, left_out, right_out, moment_out, square_out = refs[n:]
    m = pl.program_id(0)
    for k in range(n):

        @pl.when(m == k)
        def _():
            for q in range(2):
                lanes = slice(q * B, q * B + B)
                g, left_gram, right_gram = (
                    received[k][kind, 0, :, lanes].astype(jnp.float32) for kind in range(3)
                )
                left_out[q, 0] = 0.95 * left[q, 0] + 0.05 * left_gram
                right_out[q, 0] = 0.95 * right[q, 0] + 0.05 * right_gram
                second = 0.95 * moment[q, 0] + 0.05 * g * g
                moment_out[q, 0] = second
                adam = g / (jnp.sqrt(second) + 1e-08)
                square_out[0, 0, q : q + 1, :] = jnp.full((1, 128), jnp.sum(adam * adam))


def statistics(js, received, left, right, moment):
    n = js.shape[0]
    blocks, _, rows, _ = left.shape
    pairs, w = blocks // 2, 2 * B
    own = pl.BlockSpec((2, 1, rows, B), lambda m, p, j: (p, j[m], 0, 0))
    like = jax.ShapeDtypeStruct(left.shape, jnp.float32)
    return pl.pallas_call(
        functools.partial(statistics_body, n),
        grid_spec=pltpu.PrefetchScalarGridSpec(
            num_scalar_prefetch=1,
            grid=(n, pairs),
            in_specs=[
                pl.BlockSpec(
                    (3, 1, rows, w),
                    lambda m, p, j, k=k: (0, visit(k, m, p, pairs - 1), 0, 0),
                )
                for k in range(n)
            ]
            + [own] * 3,
            out_specs=[own] * 3 + [pl.BlockSpec((1, 1, 8, 128), lambda m, p, j: (m, p, 0, 0))],
        ),
        out_shape=[like] * 3 + [jax.ShapeDtypeStruct((n, pairs, 8, 128), jnp.float32)],
        compiler_params=params(),
        cost_estimate=cost(0, left.size * 4 * 7),
    )(js, *received, left, right, moment)


def restore_body(n_src, half, src, item, scale, *refs):
    sources, out, buffer, sems = refs[:n_src], refs[n_src], refs[n_src + 1], refs[n_src + 2]
    p = pl.program_id(0)
    hr = buffer.shape[2]

    def fetch(pair, slot):
        for e in range(2):
            for k in range(n_src):

                @pl.when(src[2 * pair + e] == k)
                def _():
                    pltpu.make_async_copy(
                        sources[k].at[item[2 * pair + e]], buffer.at[slot, e], sems.at[slot, e]
                    ).start()

    @pl.when(p == 0)
    def _():
        fetch(0, 0)

    @pl.when(p + 1 < pl.num_programs(0))
    def _():
        fetch(p + 1, lax.rem(p + 1, 2))

    slot = lax.rem(p, 2)
    for e in range(2):
        pltpu.make_async_copy(sources[0].at[0], buffer.at[slot, e], sems.at[slot, e]).wait()
        scaled = (buffer[slot, e].astype(jnp.float32) * scale[2 * p + e]).astype(out.dtype)
        out[:hr, e * B : e * B + B] = scaled[:, :B]
        out[hr:, e * B : e * B + B] = scaled[:, B:]


def restore(src, item, scale, sources):
    half, hr, w = sources[0].shape
    columns = src.shape[0]
    return pl.pallas_call(
        functools.partial(restore_body, len(sources), half),
        grid_spec=pltpu.PrefetchScalarGridSpec(
            num_scalar_prefetch=3,
            grid=(columns // 2,),
            in_specs=[pl.BlockSpec(memory_space=pl.ANY)] * len(sources),
            out_specs=pl.BlockSpec((2 * hr, w), lambda p, a, b, c: (0, p)),
            scratch_shapes=[
                pltpu.VMEM((2, 2, hr, w), jnp.bfloat16),
                pltpu.SemaphoreType.DMA((2, 2)),
            ],
        ),
        out_shape=jax.ShapeDtypeStruct((2 * hr, columns * B), jnp.bfloat16),
        compiler_params=params(),
        cost_estimate=cost(0, columns * hr * w * 4),
    )(src, item, scale, *sources)


def owner_local(grads, slots, stats_left, stats_right, root_left, root_right, second_moment):
    owners = lax.axis_size("fsdp")
    replicas = lax.axis_size("replica")
    grad = grads[0]
    rows, full_width = grad.shape
    columns = full_width // B
    row_blocks = slots.shape[0]
    sub_count = B // rows
    rd = rows // replicas
    half = owners // 2
    f = lax.axis_index("fsdp")
    r = lax.axis_index("replica")
    js = r ^ jnp.arange(replicas, dtype=jnp.int32)
    row_slots = lax.dynamic_index_in_dim(slots, f // sub_count, 0, keepdims=False)
    column_ids = jnp.arange(columns, dtype=jnp.int32)
    wanted = (
        replicas * jnp.arange(owners, dtype=jnp.int32)[None, :, None] + js[:, None, None]
    )
    cols = jnp.sum(jnp.where(row_slots == wanted, column_ids, 0), axis=2)

    def swap(x, k):
        return lax.ppermute(x, "replica", [(i, i ^ k) for i in range(replicas)])

    def as_rows(x):
        return x.reshape(row_blocks, -1, sub_count * rd, B)

    far_a, far_b = arrange(cols[3], grad, (), True)
    from_x_far, from_y_far = swap(far_a, 1), swap(far_b, 2)
    x_a, y_b = arrange(jnp.concatenate([cols[1, :half], cols[2, half:]]), grad, (), True)
    from_x_a, from_y_b = swap(x_a, 1), swap(y_b, 2)
    y_a, x_b = arrange(
        jnp.concatenate([cols[2, :half], cols[1, half:]]), grad, [(from_x_far, from_y_far)], True
    )
    from_y_a, from_x_b = swap(y_a, 2), swap(x_b, 1)
    (owned,) = arrange(cols[0], grad, [(from_x_a, from_x_b), (from_y_a, from_y_b)], False)
    roots = pack_roots(js, as_rows(root_left), as_rows(root_right))
    roots = [roots[0]] + [swap(roots[k], k) for k in (1, 2, 3)]
    blocks = lax.all_to_all(owned, "fsdp", split_axis=0, concat_axis=0, tiled=True)

    *products, direction, direction_square = precondition(js, blocks, roots, rd)
    received = [products[0]] + [swap(products[k], k) for k in (1, 2, 3)]
    returned = lax.all_to_all(direction, "fsdp", split_axis=0, concat_axis=0, tiled=True)

    mine_a, mine_b = returned[:half], returned[half:]
    x_a, y_b = swap(mine_a, 1), swap(mine_b, 2)
    x_b, y_a = swap(mine_b, 1), swap(mine_a, 2)
    far_a, far_b = swap(x_a, 2), swap(y_b, 1)

    left_new, right_new, moment, adam_square = statistics(
        js, received, as_rows(stats_left), as_rows(stats_right), as_rows(second_moment)
    )
    adam_square = adam_square[:, :, :2, 0].reshape(replicas, row_blocks)
    direction_square = direction_square[:, :2, 0].reshape(row_blocks)
    place = (replicas * f + js)[:, None] == column_ids
    squares = jnp.stack(
        [
            jnp.sum(jnp.where(place[:, None, :], adam_square[:, :, None], 0.0), axis=0),
            jnp.where(place[0], direction_square[:, None], 0.0),
        ]
    )
    squares = lax.psum(squares, ("fsdp", "replica"))
    ratio = jnp.sqrt(squares[0]) / jnp.sqrt(squares[1] + 1e-06)
    row_ratio = lax.dynamic_index_in_dim(ratio, f // sub_count, 0, keepdims=False)
    scale = jnp.sum(jnp.where(row_slots[:, None] == column_ids, row_ratio, 0.0), axis=1)

    owner = row_slots // replicas
    src = 2 * (lax.rem(row_slots, replicas) ^ r) + owner // half
    update = restore(
        src, lax.rem(owner, half), scale, (mine_a, mine_b, x_a, x_b, y_a, y_b, far_a, far_b)
    )
    return (
        update,
        left_new.reshape(stats_left.shape),
        right_new.reshape(stats_right.shape),
        moment.reshape(second_moment.shape),
    )


def slot_columns(row_slots, row_count):
    column_ids = jnp.arange(row_count, dtype=jnp.int32)
    matches = row_slots[None, :] == column_ids[:, None]
    return jnp.sum(jnp.where(matches, column_ids[None, :], 0), axis=1)


def row_local(grads, slots, stats_left, stats_right, root_left, root_right, second_moment):
    fsdp_count = lax.axis_size("fsdp")
    replica_count = lax.axis_size("replica")
    local_grad = grads[0]
    shard_rows, full_width = local_grad.shape
    columns = full_width // B
    row_blocks = slots.shape[0]
    per_owner = columns // fsdp_count
    sub_count = B // shard_rows
    part_rows = shard_rows // replica_count
    mine_rows = sub_count * part_rows
    fsdp_index = lax.axis_index("fsdp")
    replica_index = lax.axis_index("replica")
    row_slots = lax.dynamic_index_in_dim(slots, fsdp_index // sub_count, 0, keepdims=False)
    slot_cols = slot_columns(row_slots, columns)
    summed = lax.psum_scatter(
        local_grad.astype(jnp.float32).astype(jnp.bfloat16),
        "replica",
        scatter_dimension=0,
        tiled=True,
    )
    row_count = summed.shape[0]
    ordered = jnp.take(summed.reshape(row_count, columns, B), slot_cols, axis=1)
    arrived = lax.all_to_all(
        ordered.reshape(row_count, fsdp_count, per_owner * B).transpose(1, 0, 2),
        "fsdp",
        split_axis=0,
        concat_axis=0,
        tiled=True,
    )
    own_split = arrived.reshape(row_blocks, sub_count, part_rows, per_owner, B).transpose(
        0, 3, 1, 2, 4
    )
    gathered = lax.all_gather(own_split[:, :, :, None], "replica", axis=3, tiled=True)
    full_grad = gathered.reshape(row_blocks, per_owner, B, B)
    own_rows = own_split.reshape(row_blocks, per_owner, mine_rows, B)

    def as_rows(array_in):
        return array_in.reshape(row_blocks, per_owner, mine_rows, B)

    column_split = full_grad.reshape(row_blocks, per_owner, B, sub_count, replica_count, part_rows)
    column_part = lax.dynamic_index_in_dim(column_split, replica_index, 4, keepdims=False).reshape(
        row_blocks, per_owner, B, mine_rows
    )
    left_gram = jnp.einsum(
        "abmk,abnk->abmn", own_rows, full_grad, preferred_element_type=jnp.float32
    )
    right_gram = jnp.einsum(
        "abkm,abkn->abmn", column_part, full_grad, preferred_element_type=jnp.float32
    )
    left_new = 0.95 * as_rows(stats_left) + 0.05 * left_gram
    right_new = 0.95 * as_rows(stats_right) + 0.05 * right_gram
    right_full = lax.all_gather(root_right, "replica", axis=3, tiled=True).reshape(
        row_blocks, per_owner, B, B
    )
    inner_left = jnp.einsum(
        "abmk,abkn->abmn", as_rows(root_left), full_grad, preferred_element_type=jnp.float32
    ).astype(jnp.bfloat16)
    direction = jnp.einsum(
        "abmk,abkn->abmn", inner_left, right_full, preferred_element_type=jnp.float32
    )
    grad_float = own_rows.astype(jnp.float32)
    moment = 0.95 * as_rows(second_moment) + 0.05 * grad_float * grad_float
    adam_step = grad_float / (jnp.sqrt(moment) + 1e-08)
    adam_square, shampoo_square = lax.psum(
        (jnp.sum(adam_step * adam_step, axis=(2, 3)), jnp.sum(direction * direction, axis=(2, 3))),
        "replica",
    )
    graft_scale = jnp.sqrt(adam_square) / jnp.sqrt(shampoo_square + 1e-06)
    update_part = (direction * graft_scale[:, :, None, None]).astype(jnp.bfloat16)
    outgoing = (
        update_part.reshape(row_blocks, per_owner, sub_count, part_rows, B)
        .transpose(0, 2, 3, 1, 4)
        .reshape(fsdp_count, part_rows, per_owner * B)
    )
    returned = lax.all_to_all(outgoing, "fsdp", split_axis=0, concat_axis=0, tiled=True)
    ordered = returned.transpose(1, 0, 2).reshape(part_rows, columns, B)
    update = lax.all_gather(
        jnp.take(ordered, row_slots, axis=1).reshape(part_rows, full_width),
        "replica",
        axis=0,
        tiled=True,
    )
    return (
        update,
        left_new.reshape(stats_left.shape),
        right_new.reshape(stats_right.shape),
        moment.reshape(second_moment.shape),
    )


def local(*arrays):
    replicas = lax.axis_size("replica")
    rows, full_width = arrays[0].shape[1:]
    per_owner = full_width // B // lax.axis_size("fsdp")
    if replicas == 4 and per_owner == replicas and 2 * rows == B:
        return owner_local(*arrays)
    return row_local(*arrays)


def solution(mesh):
    placed = (
        P("replica", "fsdp", None),
        P(),
        P(None, "fsdp", None, "replica", None, None),
        P(None, "fsdp", None, "replica", None, None),
        P(None, "fsdp", None, "replica", None, None),
        P(None, "fsdp", None, "replica", None, None),
        P(None, "fsdp", None, "replica", None, None),
    )
    return jax.shard_map(
        local,
        mesh=mesh,
        in_specs=placed,
        out_specs=(
            P("fsdp", None),
            P(None, "fsdp", None, "replica", None, None),
            P(None, "fsdp", None, "replica", None, None),
            P(None, "fsdp", None, "replica", None, None),
        ),
        check_vma=False,
    )
```

```python
import functools

import jax
import jax.numpy as jnp
from jax import lax
from jax.experimental import pallas as pl
from jax.experimental.pallas import tpu as pltpu
from jax.sharding import PartitionSpec as P

B = 576
LANES = 128
WINDOW = -(-B // LANES) * LANES
VMEM = 56 * 1024 * 1024
ANY = pl.BlockSpec(memory_space=pl.ANY)
WHOLE = pl.BlockSpec(memory_space=pltpu.VMEM)
SCALARS = pl.BlockSpec(memory_space=pltpu.SMEM)


def params():
    return pltpu.CompilerParams(vmem_limit_bytes=VMEM)


def cost(flops, moved):
    return pl.CostEstimate(flops=flops, bytes_accessed=moved, transcendentals=0)


def arrange_body(n_add, n_after, n_pass, base, halves, cols, grad, *refs):
    adds = refs[: 2 * n_add]
    n_out = 2 if halves else 1
    first = 2 * n_add + n_after + n_pass
    outs = refs[first : first + n_out]
    buffer, sems = refs[-2:]
    n = outs[0].shape[1]
    count = buffer.shape[0]
    half = count // 2

    def copy(i):
        start = pl.multiple_of(cols[i] * B // LANES * LANES, LANES)
        return pltpu.make_async_copy(
            grad.at[pl.ds(base, 2 * n), pl.ds(start, WINDOW)], buffer.at[i], sems.at[i]
        )

    for i in range(count):
        copy(i).start()
    for i in range(count):
        copy(i).wait()
        out, at = (outs[i // half], i % half) if halves else (outs[0], i)
        for shift in (0, B % LANES):

            @pl.when(lax.rem(cols[i] * B, LANES) == shift)
            def _():
                part = buffer[i, :, shift : shift + B]
                out[at, :, :B] = part[:n]
                out[at, :, B:] = part[n:]

        if n_add:
            total = out[at].astype(jnp.float32)
            for k in range(n_add):
                total = total + adds[2 * k + i // half][i % half].astype(jnp.float32)
            out[at] = total.astype(out.dtype)


def arrange(cols, grad, base, n, adds=(), halves=True, after=(), through=()):
    count = cols.shape[0]
    w = 2 * B
    shapes = [(count // 2, n, w)] * 2 if halves else [(count, n, w)]
    before = 2 + 2 * len(adds) + len(after)
    return pl.pallas_call(
        functools.partial(arrange_body, len(adds), len(after), len(through), base, halves),
        in_specs=[SCALARS, ANY]
        + [WHOLE] * (2 * len(adds))
        + [ANY] * (len(after) + len(through)),
        out_specs=[WHOLE] * len(shapes) + [ANY] * len(through),
        out_shape=[jax.ShapeDtypeStruct(s, grad.dtype) for s in shapes]
        + [jax.ShapeDtypeStruct(x.shape, x.dtype) for x in through],
        scratch_shapes=[
            pltpu.VMEM((count, 2 * n, WINDOW), grad.dtype),
            pltpu.SemaphoreType.DMA((count,)),
        ],
        input_output_aliases={before + k: len(shapes) + k for k in range(len(through))},
        compiler_params=params(),
        cost_estimate=cost(0, count * n * w * 2 * (2 + len(adds))),
    )(cols, grad, *[term for pair in adds for term in pair], *after, *through)


def visit(k, m, p, last):
    return jnp.where(m == k, p, jnp.where(m < k, 0, last))


def pack_roots_body(n, js, left, right, *refs):
    m = pl.program_id(0)
    for k, out in enumerate(refs[-n:]):

        @pl.when(m == k)
        def _():
            for kind, ref in enumerate((left, right)):
                for q in range(2):
                    out[kind, 0, :, q * B : q * B + B] = ref[q, 0]


def pack_roots(js, left, right, after):
    blocks, _, rows, _ = left.shape
    pairs, n, w = blocks // 2, js.shape[0], 2 * B
    source = pl.BlockSpec((2, 1, rows, B), lambda m, p, j: (p, j[m], 0, 0))
    return pl.pallas_call(
        functools.partial(pack_roots_body, n),
        grid_spec=pltpu.PrefetchScalarGridSpec(
            num_scalar_prefetch=1,
            grid=(n, pairs),
            in_specs=[source, source] + [ANY] * len(after),
            out_specs=[
                pl.BlockSpec(
                    (2, 1, rows, w),
                    lambda m, p, j, k=k: (0, visit(k, m, p, pairs - 1), 0, 0),
                )
                for k in range(n)
            ],
        ),
        out_shape=[jax.ShapeDtypeStruct((2, pairs, rows, w), left.dtype)] * n,
        compiler_params=params(),
        cost_estimate=cost(0, 4 * left.size * 2),
    )(js, left, right, *after)


def dot(x, y, dims):
    return lax.dot_general(x, y, (dims, ((), ())), preferred_element_type=jnp.float32)


def assemble(chunks, q, full):
    base = 0
    for chunk in chunks:
        n = chunk.shape[1]
        for h in range(2):
            for side in range(2):
                start = h * (B // 2) + base + side * n
                full[start : start + n, :] = chunk[2 * q + h, :, side * B : side * B + B]
        base += 2 * n


def own_rows(j, h, rd):
    return pl.ds(pl.multiple_of(h * (B // 2) + j * rd, 8), rd)


def gram_body(n, rd, n_chunks, js, *refs):
    chunks, refs = refs[:n_chunks], refs[n_chunks:]
    rows_out, grams_out = refs[:n], refs[n : 2 * n]
    g16, g32, l32, r32 = refs[2 * n :]
    for q in range(2):
        assemble(chunks, q, g16)
        g = g16[...]
        g32[...] = g.astype(jnp.float32)
        l32[...] = dot(g, g, ((1,), (1,)))
        r32[...] = dot(g, g, ((0,), (0,)))
        lanes = slice(q * B, q * B + B)
        for k in range(n):
            for full, out, kind in ((g32, rows_out, 0), (l32, grams_out, 0), (r32, grams_out, 1)):
                parts = [full[own_rows(js[k], h, rd), :] for h in range(2)]
                out[k][kind, 0, :, lanes] = jnp.concatenate(parts, axis=0).astype(jnp.bfloat16)


def gram(js, chunks, rd):
    n = js.shape[0]
    count, _, w = chunks[0].shape
    pairs, rows = count // 4, 2 * rd

    def outs(kinds):
        return (
            [pl.BlockSpec((kinds, 1, rows, w), lambda p, j: (0, p, 0, 0))] * n,
            [jax.ShapeDtypeStruct((kinds, pairs, rows, w), jnp.bfloat16)] * n,
        )

    (rows_specs, rows_shapes), (gram_specs, gram_shapes) = outs(1), outs(2)
    out = pl.pallas_call(
        functools.partial(gram_body, n, rd, len(chunks)),
        grid_spec=pltpu.PrefetchScalarGridSpec(
            num_scalar_prefetch=1,
            grid=(pairs,),
            in_specs=[
                pl.BlockSpec((4,) + chunk.shape[1:], lambda p, j: (p, 0, 0)) for chunk in chunks
            ],
            out_specs=rows_specs + gram_specs,
            scratch_shapes=[pltpu.VMEM((B, B), jnp.bfloat16)] + [pltpu.VMEM((B, B), jnp.float32)] * 3,
        ),
        out_shape=rows_shapes + gram_shapes,
        compiler_params=params(),
        cost_estimate=cost(pairs * 8 * B**3, pairs * B * B * 2 * 8),
    )(js, *chunks)
    return out[:n], out[n:]


def direct_body(n, rd, n_chunks, js, *refs):
    chunks, roots, refs = refs[:n_chunks], refs[n_chunks : n_chunks + n], refs[n_chunks + n :]
    outs, square_out = refs[:n_chunks], refs[n_chunks]
    g16, l32, r32 = refs[n_chunks + 1 :]
    for q in range(2):
        assemble(chunks, q, g16)
        for k in range(n):
            for kind, full in enumerate((l32, r32)):
                part = roots[k][kind, 0, :, q * B : q * B + B].astype(jnp.float32)
                for h in range(2):
                    full[own_rows(js[k], h, rd), :] = part[h * rd : h * rd + rd]
        inner = dot(l32[...].astype(jnp.bfloat16), g16[...], ((1,), (0,))).astype(jnp.bfloat16)
        direction = dot(inner, r32[...].astype(jnp.bfloat16), ((1,), (0,)))
        square_out[0, q : q + 1, :] = jnp.full((1, LANES), jnp.sum(direction * direction))
        direction = direction.astype(jnp.bfloat16)
        base = 0
        for out in outs:
            size = out.shape[1]
            for h in range(2):
                for side in range(2):
                    start = h * (B // 2) + base + side * size
                    out[2 * q + h, :, side * B : side * B + B] = direction[start : start + size]
            base += 2 * size


def direct(js, chunks, roots, rd):
    n = js.shape[0]
    count, _, w = chunks[0].shape
    pairs, rows = roots[0].shape[1], roots[0].shape[2]
    chunk_specs = [pl.BlockSpec((4,) + chunk.shape[1:], lambda p, j: (p, 0, 0)) for chunk in chunks]
    return pl.pallas_call(
        functools.partial(direct_body, n, rd, len(chunks)),
        grid_spec=pltpu.PrefetchScalarGridSpec(
            num_scalar_prefetch=1,
            grid=(pairs,),
            in_specs=chunk_specs
            + [pl.BlockSpec((2, 1, rows, w), lambda p, j: (0, p, 0, 0))] * n,
            out_specs=chunk_specs + [pl.BlockSpec((1, 8, LANES), lambda p, j: (p, 0, 0))],
            scratch_shapes=[pltpu.VMEM((B, B), jnp.bfloat16)] + [pltpu.VMEM((B, B), jnp.float32)] * 2,
        ),
        out_shape=[jax.ShapeDtypeStruct(chunk.shape, jnp.bfloat16) for chunk in chunks]
        + [jax.ShapeDtypeStruct((pairs, 8, LANES), jnp.float32)],
        compiler_params=params(),
        cost_estimate=cost(pairs * 8 * B**3, pairs * B * B * 2 * 8),
    )(js, *chunks, *roots)


def moment_body(n, js, *refs):
    received, (moment, moment_out, square_out) = refs[:n], refs[n:]
    m = pl.program_id(0)
    for k in range(n):

        @pl.when(m == k)
        def _():
            for q in range(2):
                g = received[k][0, 0, :, q * B : q * B + B].astype(jnp.float32)
                second = 0.95 * moment[q, 0] + 0.05 * g * g
                moment_out[q, 0] = second
                adam = g / (jnp.sqrt(second) + 1e-08)
                square_out[0, 0, q : q + 1, :] = jnp.full((1, LANES), jnp.sum(adam * adam))


def statistics_body(n, js, *refs):
    received, (left, right, left_out, right_out) = refs[:n], refs[n:]
    m = pl.program_id(0)
    for k in range(n):

        @pl.when(m == k)
        def _():
            for q in range(2):
                for kind, old, new in ((0, left, left_out), (1, right, right_out)):
                    product = received[k][kind, 0, :, q * B : q * B + B].astype(jnp.float32)
                    new[q, 0] = 0.95 * old[q, 0] + 0.05 * product


def by_rows(body, js, received, olds, squares):
    n = js.shape[0]
    blocks, _, rows, _ = olds[0].shape
    kinds, pairs, _, w = received[0].shape
    own = pl.BlockSpec((2, 1, rows, B), lambda m, p, j: (p, j[m], 0, 0))
    out_specs = [own] * len(olds)
    out_shape = [jax.ShapeDtypeStruct(old.shape, jnp.float32) for old in olds]
    if squares:
        out_specs.append(pl.BlockSpec((1, 1, 8, LANES), lambda m, p, j: (m, p, 0, 0)))
        out_shape.append(jax.ShapeDtypeStruct((n, pairs, 8, LANES), jnp.float32))
    return pl.pallas_call(
        functools.partial(body, n),
        grid_spec=pltpu.PrefetchScalarGridSpec(
            num_scalar_prefetch=1,
            grid=(n, pairs),
            in_specs=[
                pl.BlockSpec(
                    (kinds, 1, rows, w),
                    lambda m, p, j, k=k: (0, visit(k, m, p, pairs - 1), 0, 0),
                )
                for k in range(n)
            ]
            + [own] * len(olds),
            out_specs=out_specs,
        ),
        out_shape=out_shape,
        compiler_params=params(),
        cost_estimate=cost(0, olds[0].size * 10 * len(olds)),
    )(js, *received, *olds)


def restore_body(n_src, n_old, base, src, item, scale, *refs):
    sources = refs[:n_src]
    out, buffer, result, in_sems, out_sems = refs[n_src + n_old :]
    columns, n, w = buffer.shape
    slots = result.shape[0]

    def fetch(c, _):
        for k in range(n_src):

            @pl.when(src[c] == k)
            def _():
                pltpu.make_async_copy(sources[k].at[item[c]], buffer.at[c], in_sems.at[c]).start()

        return 0

    def store(p, slot):
        start = pl.multiple_of(p * w, LANES)
        return pltpu.make_async_copy(
            result.at[slot], out.at[pl.ds(base, 2 * n), pl.ds(start, w)], out_sems.at[slot]
        )

    def step(p, _):
        slot = lax.rem(p, slots)

        @pl.when(p >= slots)
        def _():
            store(p - slots, slot).wait()

        for e in range(2):
            c = 2 * p + e
            pltpu.make_async_copy(sources[0].at[0], buffer.at[c], in_sems.at[c]).wait()
            scaled = (buffer[c].astype(jnp.float32) * scale[c]).astype(result.dtype)
            result[slot, :n, e * B : e * B + B] = scaled[:, :B]
            result[slot, n:, e * B : e * B + B] = scaled[:, B:]
        store(p, slot).start()
        return 0

    pairs = columns // 2
    lax.fori_loop(0, columns, fetch, 0)
    lax.fori_loop(0, pairs, step, 0)
    for p in range(pairs - slots, pairs):
        store(p, p % slots).wait()


def restore(src, item, scale, sources, base, rows, old):
    _, n, w = sources[0].shape
    columns = src.shape[0]
    slots = 4
    return pl.pallas_call(
        functools.partial(restore_body, len(sources), len(old), base),
        in_specs=[SCALARS] * 3 + [ANY] * (len(sources) + len(old)),
        out_specs=ANY,
        out_shape=jax.ShapeDtypeStruct((rows, columns * B), jnp.bfloat16),
        scratch_shapes=[
            pltpu.VMEM((columns, n, w), jnp.bfloat16),
            pltpu.VMEM((slots, 2 * n, w), jnp.bfloat16),
            pltpu.SemaphoreType.DMA((columns,)),
            pltpu.SemaphoreType.DMA((slots,)),
        ],
        input_output_aliases={3 + len(sources): 0} if old else {},
        compiler_params=params(),
        cost_estimate=cost(0, columns * n * w * 4),
    )(src, item, scale, *sources, *old)


def owner_local(grads, slots, stats_left, stats_right, root_left, root_right, second_moment):
    owners = lax.axis_size("fsdp")
    replicas = lax.axis_size("replica")
    grad = grads[0]
    rows, full_width = grad.shape
    columns = full_width // B
    row_blocks = slots.shape[0]
    sub_count = B // rows
    rd = rows // replicas
    half = owners // 2
    f = lax.axis_index("fsdp")
    r = lax.axis_index("replica")
    js = r ^ jnp.arange(replicas, dtype=jnp.int32)
    row_slots = lax.dynamic_index_in_dim(slots, f // sub_count, 0, keepdims=False)
    column_ids = jnp.arange(columns, dtype=jnp.int32)
    owner_ids = replicas * jnp.arange(owners, dtype=jnp.int32)

    def columns_of(low, high):
        ids = jnp.arange(owners, dtype=jnp.int32)
        wanted = owner_ids + (r ^ jnp.where(ids < half, low, high))
        return jnp.sum(jnp.where(row_slots == wanted[:, None], column_ids, 0), axis=1)

    far, near, cross, own = (columns_of(*k) for k in ((3, 3), (1, 2), (2, 1), (0, 0)))

    def swap(x, k):
        return lax.ppermute(x, "replica", [(i, i ^ k) for i in range(replicas)])

    def as_rows(x):
        return x.reshape(row_blocks, -1, sub_count * rd, B)

    def exchange(x):
        return lax.all_to_all(x, "fsdp", split_axis=0, concat_axis=0, tiled=True)

    first = -(-rows // 64) * 16
    chunks = ((0, first), (2 * first, rows // 2 - first))

    def start_sum(base, n, after):
        far_a, far_b = arrange(far, grad, base, n, after=after)
        by_far = (swap(far_a, 1), swap(far_b, 2))
        x_a, y_b = arrange(near, grad, base, n, after=(far_a,))
        return by_far, (swap(x_a, 1), swap(y_b, 2)), x_a

    def end_sum(base, n, by_far, after):
        y_a, x_b = arrange(cross, grad, base, n, (by_far,), after=after)
        return (swap(y_a, 2), swap(x_b, 1)), y_a

    by_far, by_near, sent = start_sum(*chunks[0], ())
    roots = list(pack_roots(js, as_rows(root_left), as_rows(root_right), (sent,)))
    by_cross, sent = end_sum(*chunks[0], by_far, (roots[0],))
    by_far_1, by_near_1, sent = start_sum(*chunks[1], (sent,))
    terms = ((by_near[0], by_cross[1]), (by_cross[0], by_near[1]))
    (owned,) = arrange(own, grad, *chunks[0], terms, halves=False, after=(sent,))
    by_cross_1, sent = end_sum(*chunks[1], by_far_1, (owned,))
    blocks = [exchange(owned)]
    terms = ((by_near_1[0], by_cross_1[1]), (by_cross_1[0], by_near_1[1]))
    owned, *roots[1:] = arrange(
        own, grad, *chunks[1], terms, halves=False, through=tuple(roots[1:])
    )
    blocks.append(exchange(owned))
    roots = [roots[0]] + [swap(roots[k], k) for k in (3, 1, 2)]
    roots = [roots[0], roots[2], roots[3], roots[1]]

    grad_rows, grams = gram(js, blocks, rd)
    grad_rows = [grad_rows[0]] + [swap(grad_rows[k], k) for k in (1, 2, 3)]
    grams = [grams[0]] + [swap(grams[k], k) for k in (1, 2, 3)]
    *directions, direction_square = direct(js, blocks, roots, rd)

    gathered = []
    for direction in directions:
        mine = exchange(direction)
        x, y = swap(mine, 1), swap(mine, 2)
        gathered.append((mine, x, y, swap(x[:half], 2), swap(y[half:], 1)))

    moment, adam_square = by_rows(moment_body, js, grad_rows, [as_rows(second_moment)], True)
    left_new, right_new = by_rows(
        statistics_body, js, grams, [as_rows(stats_left), as_rows(stats_right)], False
    )

    adam_square = adam_square[:, :, :2, 0].reshape(replicas, row_blocks)
    slot_ids = jnp.arange(replicas, dtype=jnp.int32)
    adam_square = jnp.sum(
        jnp.where((js[:, None] == slot_ids)[:, :, None], adam_square[:, None, :], 0.0), axis=0
    )
    squares = jnp.concatenate([adam_square, direction_square[:, :2, 0].reshape(1, row_blocks)])
    squares = lax.all_gather(squares, ("fsdp", "replica")).reshape(
        owners, replicas, replicas + 1, row_blocks
    )
    ratio = jnp.sqrt(jnp.sum(squares[:, :, :replicas], axis=1)) / jnp.sqrt(
        squares[:, :, replicas] + 1e-06
    )
    row_ratio = lax.dynamic_index_in_dim(
        ratio.reshape(columns, row_blocks), f // sub_count, 1, keepdims=False
    )
    scale = jnp.sum(jnp.where(row_slots[:, None] == column_ids, row_ratio, 0.0), axis=1)

    owner = row_slots // replicas
    step = lax.rem(row_slots, replicas) ^ r
    src = step + jnp.where(step == 3, owner // half, 0)
    item = jnp.where(step == 3, lax.rem(owner, half), owner)
    update = ()
    for (base, _), sources in zip(chunks, gathered):
        update = (restore(src, item, scale, sources, base, rows, update),)
    return (
        update[0],
        left_new.reshape(stats_left.shape),
        right_new.reshape(stats_right.shape),
        moment.reshape(second_moment.shape),
    )


def slot_columns(row_slots, row_count):
    column_ids = jnp.arange(row_count, dtype=jnp.int32)
    matches = row_slots[None, :] == column_ids[:, None]
    return jnp.sum(jnp.where(matches, column_ids[None, :], 0), axis=1)


def row_local(grads, slots, stats_left, stats_right, root_left, root_right, second_moment):
    fsdp_count = lax.axis_size("fsdp")
    replica_count = lax.axis_size("replica")
    local_grad = grads[0]
    shard_rows, full_width = local_grad.shape
    columns = full_width // B
    row_blocks = slots.shape[0]
    per_owner = columns // fsdp_count
    sub_count = B // shard_rows
    part_rows = shard_rows // replica_count
    mine_rows = sub_count * part_rows
    fsdp_index = lax.axis_index("fsdp")
    replica_index = lax.axis_index("replica")
    row_slots = lax.dynamic_index_in_dim(slots, fsdp_index // sub_count, 0, keepdims=False)
    slot_cols = slot_columns(row_slots, columns)
    summed = lax.psum_scatter(
        local_grad.astype(jnp.float32).astype(jnp.bfloat16),
        "replica",
        scatter_dimension=0,
        tiled=True,
    )
    row_count = summed.shape[0]
    ordered = jnp.take(summed.reshape(row_count, columns, B), slot_cols, axis=1)
    arrived = lax.all_to_all(
        ordered.reshape(row_count, fsdp_count, per_owner * B).transpose(1, 0, 2),
        "fsdp",
        split_axis=0,
        concat_axis=0,
        tiled=True,
    )
    own_split = arrived.reshape(row_blocks, sub_count, part_rows, per_owner, B).transpose(
        0, 3, 1, 2, 4
    )
    gathered = lax.all_gather(own_split[:, :, :, None], "replica", axis=3, tiled=True)
    full_grad = gathered.reshape(row_blocks, per_owner, B, B)
    own_rows = own_split.reshape(row_blocks, per_owner, mine_rows, B)

    def as_rows(array_in):
        return array_in.reshape(row_blocks, per_owner, mine_rows, B)

    column_split = full_grad.reshape(row_blocks, per_owner, B, sub_count, replica_count, part_rows)
    column_part = lax.dynamic_index_in_dim(column_split, replica_index, 4, keepdims=False).reshape(
        row_blocks, per_owner, B, mine_rows
    )
    left_gram = jnp.einsum(
        "abmk,abnk->abmn", own_rows, full_grad, preferred_element_type=jnp.float32
    )
    right_gram = jnp.einsum(
        "abkm,abkn->abmn", column_part, full_grad, preferred_element_type=jnp.float32
    )
    left_new = 0.95 * as_rows(stats_left) + 0.05 * left_gram
    right_new = 0.95 * as_rows(stats_right) + 0.05 * right_gram
    right_full = lax.all_gather(root_right, "replica", axis=3, tiled=True).reshape(
        row_blocks, per_owner, B, B
    )
    inner_left = jnp.einsum(
        "abmk,abkn->abmn", as_rows(root_left), full_grad, preferred_element_type=jnp.float32
    ).astype(jnp.bfloat16)
    direction = jnp.einsum(
        "abmk,abkn->abmn", inner_left, right_full, preferred_element_type=jnp.float32
    )
    grad_float = own_rows.astype(jnp.float32)
    moment = 0.95 * as_rows(second_moment) + 0.05 * grad_float * grad_float
    adam_step = grad_float / (jnp.sqrt(moment) + 1e-08)
    adam_square, shampoo_square = lax.psum(
        (jnp.sum(adam_step * adam_step, axis=(2, 3)), jnp.sum(direction * direction, axis=(2, 3))),
        "replica",
    )
    graft_scale = jnp.sqrt(adam_square) / jnp.sqrt(shampoo_square + 1e-06)
    update_part = (direction * graft_scale[:, :, None, None]).astype(jnp.bfloat16)
    outgoing = (
        update_part.reshape(row_blocks, per_owner, sub_count, part_rows, B)
        .transpose(0, 2, 3, 1, 4)
        .reshape(fsdp_count, part_rows, per_owner * B)
    )
    returned = lax.all_to_all(outgoing, "fsdp", split_axis=0, concat_axis=0, tiled=True)
    ordered = returned.transpose(1, 0, 2).reshape(part_rows, columns, B)
    update = lax.all_gather(
        jnp.take(ordered, row_slots, axis=1).reshape(part_rows, full_width),
        "replica",
        axis=0,
        tiled=True,
    )
    return (
        update,
        left_new.reshape(stats_left.shape),
        right_new.reshape(stats_right.shape),
        moment.reshape(second_moment.shape),
    )


def local(*arrays):
    replicas = lax.axis_size("replica")
    rows, full_width = arrays[0].shape[1:]
    per_owner = full_width // B // lax.axis_size("fsdp")
    if replicas == 4 and per_owner == replicas and 2 * rows == B:
        return owner_local(*arrays)
    return row_local(*arrays)


def solution(mesh):
    placed = (
        P("replica", "fsdp", None),
        P(),
        P(None, "fsdp", None, "replica", None, None),
        P(None, "fsdp", None, "replica", None, None),
        P(None, "fsdp", None, "replica", None, None),
        P(None, "fsdp", None, "replica", None, None),
        P(None, "fsdp", None, "replica", None, None),
    )
    return jax.shard_map(
        local,
        mesh=mesh,
        in_specs=placed,
        out_specs=(
            P("fsdp", None),
            P(None, "fsdp", None, "replica", None, None),
            P(None, "fsdp", None, "replica", None, None),
            P(None, "fsdp", None, "replica", None, None),
        ),
        check_vma=False,
    )
```

```python
import functools

import jax
import jax.numpy as jnp
from jax import lax
from jax.experimental import pallas as pl
from jax.experimental.pallas import tpu as pltpu
from jax.sharding import PartitionSpec as P

B = 576
LANES = 128
WINDOW = -(-B // LANES) * LANES
VMEM = 64 * 1024 * 1024 - 4096
ANY = pl.BlockSpec(memory_space=pl.ANY)
WHOLE = pl.BlockSpec(memory_space=pltpu.VMEM)
SCALARS = pl.BlockSpec(memory_space=pltpu.SMEM)


def params():
    return pltpu.CompilerParams(vmem_limit_bytes=VMEM)


def cost(flops, moved):
    return pl.CostEstimate(flops=flops, bytes_accessed=moved, transcendentals=0)


def arrange_body(n_add, n_after, n_pass, base, halves, cols, grad, *refs):
    adds = refs[: 2 * n_add]
    n_out = 2 if halves else 1
    first = 2 * n_add + n_after + n_pass
    outs = refs[first : first + n_out]
    buffer, sems = refs[-2:]
    n = outs[0].shape[1]
    count = buffer.shape[0]
    half = count // 2

    def copy(i):
        start = pl.multiple_of(cols[i] * B // LANES * LANES, LANES)
        return pltpu.make_async_copy(
            grad.at[pl.ds(base, 2 * n), pl.ds(start, WINDOW)], buffer.at[i], sems.at[i]
        )

    for i in range(count):
        copy(i).start()
    for i in range(count):
        copy(i).wait()
        out, at = (outs[i // half], i % half) if halves else (outs[0], i)
        for shift in (0, B % LANES):

            @pl.when(lax.rem(cols[i] * B, LANES) == shift)
            def _():
                part = buffer[i, :, shift : shift + B]
                out[at, :, :B] = part[:n]
                out[at, :, B:] = part[n:]

        if n_add:
            total = out[at].astype(jnp.float32)
            for k in range(n_add):
                total = total + adds[2 * k + i // half][i % half].astype(jnp.float32)
            out[at] = total.astype(out.dtype)


def arrange(cols, grad, base, n, adds=(), halves=True, after=(), through=()):
    count = cols.shape[0]
    w = 2 * B
    shapes = [(count // 2, n, w)] * 2 if halves else [(count, n, w)]
    before = 2 + 2 * len(adds) + len(after)
    return pl.pallas_call(
        functools.partial(arrange_body, len(adds), len(after), len(through), base, halves),
        in_specs=[SCALARS, ANY]
        + [WHOLE] * (2 * len(adds))
        + [ANY] * (len(after) + len(through)),
        out_specs=[WHOLE] * len(shapes) + [ANY] * len(through),
        out_shape=[jax.ShapeDtypeStruct(s, grad.dtype) for s in shapes]
        + [jax.ShapeDtypeStruct(x.shape, x.dtype) for x in through],
        scratch_shapes=[
            pltpu.VMEM((count, 2 * n, WINDOW), grad.dtype),
            pltpu.SemaphoreType.DMA((count,)),
        ],
        input_output_aliases={before + k: len(shapes) + k for k in range(len(through))},
        compiler_params=params(),
        cost_estimate=cost(0, count * n * w * 2 * (2 + len(adds))),
    )(cols, grad, *[term for pair in adds for term in pair], *after, *through)


def visit(k, m, p, last):
    return jnp.where(m == k, p, jnp.where(m < k, 0, last))


def pack_roots_body(n, js, left, right, *refs):
    m = pl.program_id(0)
    for k, out in enumerate(refs[-n:]):

        @pl.when(m == k)
        def _():
            for kind, ref in enumerate((left, right)):
                for q in range(2):
                    out[kind, 0, :, q * B : q * B + B] = ref[q, 0]


def pack_roots(js, left, right, after):
    blocks, _, rows, _ = left.shape
    pairs, n, w = blocks // 2, js.shape[0], 2 * B
    source = pl.BlockSpec((2, 1, rows, B), lambda m, p, j: (p, j[m], 0, 0))
    return pl.pallas_call(
        functools.partial(pack_roots_body, n),
        grid_spec=pltpu.PrefetchScalarGridSpec(
            num_scalar_prefetch=1,
            grid=(n, pairs),
            in_specs=[source, source] + [ANY] * len(after),
            out_specs=[
                pl.BlockSpec(
                    (2, 1, rows, w),
                    lambda m, p, j, k=k: (0, visit(k, m, p, pairs - 1), 0, 0),
                )
                for k in range(n)
            ],
        ),
        out_shape=[jax.ShapeDtypeStruct((2, pairs, rows, w), left.dtype)] * n,
        compiler_params=params(),
        cost_estimate=cost(0, 4 * left.size * 2),
    )(js, left, right, *after)


def dot(x, y, dims):
    return lax.dot_general(x, y, (dims, ((), ())), preferred_element_type=jnp.float32)


def assemble(chunks, q, full):
    base = 0
    for chunk in chunks:
        n = chunk.shape[1]
        for h in range(2):
            for side in range(2):
                start = h * (B // 2) + base + side * n
                full[start : start + n, :] = chunk[2 * q + h, :, side * B : side * B + B]
        base += 2 * n


def own_rows(j, h, rd):
    return pl.ds(pl.multiple_of(h * (B // 2) + j * rd, 8), rd)


def gram_body(n, rd, n_chunks, js, *refs):
    chunks, refs = refs[:n_chunks], refs[n_chunks:]
    outs, (g16, g32, l32, r32) = refs[:n], refs[n:]
    for q in range(2):
        assemble(chunks, q, g16)
        g = g16[...]
        g32[...] = g.astype(jnp.float32)
        l32[...] = dot(g, g, ((1,), (1,)))
        r32[...] = dot(g, g, ((0,), (0,)))
        lanes = slice(q * B, q * B + B)
        for k in range(n):
            for kind, full in enumerate((g32, l32, r32)):
                parts = [full[own_rows(js[k], h, rd), :] for h in range(2)]
                outs[k][kind, 0, :, lanes] = jnp.concatenate(parts, axis=0).astype(jnp.bfloat16)


def gram(js, chunks, rd):
    n = js.shape[0]
    count, _, w = chunks[0].shape
    pairs, rows = count // 4, 2 * rd

    return pl.pallas_call(
        functools.partial(gram_body, n, rd, len(chunks)),
        grid_spec=pltpu.PrefetchScalarGridSpec(
            num_scalar_prefetch=1,
            grid=(pairs,),
            in_specs=[
                pl.BlockSpec((4,) + chunk.shape[1:], lambda p, j: (p, 0, 0)) for chunk in chunks
            ],
            out_specs=[pl.BlockSpec((3, 1, rows, w), lambda p, j: (0, p, 0, 0))] * n,
            scratch_shapes=[pltpu.VMEM((B, B), jnp.bfloat16)] + [pltpu.VMEM((B, B), jnp.float32)] * 3,
        ),
        out_shape=[jax.ShapeDtypeStruct((3, pairs, rows, w), jnp.bfloat16)] * n,
        compiler_params=params(),
        cost_estimate=cost(pairs * 8 * B**3, pairs * B * B * 2 * 8),
    )(js, *chunks)


def direct_body(n, rd, n_chunks, n_after, js, *refs):
    chunks, roots = refs[:n_chunks], refs[n_chunks : n_chunks + n]
    refs = refs[n_chunks + n + n_after :]
    outs, square_out = refs[:n_chunks], refs[n_chunks]
    g16, l32, r32 = refs[n_chunks + 1 :]
    for q in range(2):
        assemble(chunks, q, g16)
        for k in range(n):
            for kind, full in enumerate((l32, r32)):
                part = roots[k][kind, 0, :, q * B : q * B + B].astype(jnp.float32)
                for h in range(2):
                    full[own_rows(js[k], h, rd), :] = part[h * rd : h * rd + rd]
        inner = dot(l32[...].astype(jnp.bfloat16), g16[...], ((1,), (0,))).astype(jnp.bfloat16)
        direction = dot(inner, r32[...].astype(jnp.bfloat16), ((1,), (0,)))
        square_out[0, q : q + 1, :] = jnp.full((1, LANES), jnp.sum(direction * direction))
        direction = direction.astype(jnp.bfloat16)
        base = 0
        for out in outs:
            size = out.shape[1]
            for h in range(2):
                for side in range(2):
                    start = h * (B // 2) + base + side * size
                    out[2 * q + h, :, side * B : side * B + B] = direction[start : start + size]
            base += 2 * size


def direct(js, chunks, roots, rd, after):
    n = js.shape[0]
    count, _, w = chunks[0].shape
    pairs, rows = roots[0].shape[1], roots[0].shape[2]
    chunk_specs = [pl.BlockSpec((4,) + chunk.shape[1:], lambda p, j: (p, 0, 0)) for chunk in chunks]
    return pl.pallas_call(
        functools.partial(direct_body, n, rd, len(chunks), len(after)),
        grid_spec=pltpu.PrefetchScalarGridSpec(
            num_scalar_prefetch=1,
            grid=(pairs,),
            in_specs=chunk_specs
            + [pl.BlockSpec((2, 1, rows, w), lambda p, j: (0, p, 0, 0))] * n
            + [ANY] * len(after),
            out_specs=chunk_specs + [pl.BlockSpec((1, 8, LANES), lambda p, j: (p, 0, 0))],
            scratch_shapes=[pltpu.VMEM((B, B), jnp.bfloat16)] + [pltpu.VMEM((B, B), jnp.float32)] * 2,
        ),
        out_shape=[jax.ShapeDtypeStruct(chunk.shape, jnp.bfloat16) for chunk in chunks]
        + [jax.ShapeDtypeStruct((pairs, 8, LANES), jnp.float32)],
        compiler_params=params(),
        cost_estimate=cost(pairs * 8 * B**3, pairs * B * B * 2 * 8),
    )(js, *chunks, *roots, *after)


def statistics_body(n, js, *refs):
    received = refs[:n]
    left, right, moment, left_out, right_out, moment_out, square_out = refs[n:]
    m = pl.program_id(0)
    for k in range(n):

        @pl.when(m == k)
        def _():
            for q in range(2):
                lanes = slice(q * B, q * B + B)
                g, left_gram, right_gram = (
                    received[k][kind, 0, :, lanes].astype(jnp.float32) for kind in range(3)
                )
                left_out[q, 0] = 0.95 * left[q, 0] + 0.05 * left_gram
                right_out[q, 0] = 0.95 * right[q, 0] + 0.05 * right_gram
                second = 0.95 * moment[q, 0] + 0.05 * g * g
                moment_out[q, 0] = second
                adam = g / (jnp.sqrt(second) + 1e-08)
                square_out[0, 0, q : q + 1, :] = jnp.full((1, LANES), jnp.sum(adam * adam))


def statistics(js, received, olds):
    n = js.shape[0]
    blocks, _, rows, _ = olds[0].shape
    kinds, pairs, _, w = received[0].shape
    own = pl.BlockSpec((2, 1, rows, B), lambda m, p, j: (p, j[m], 0, 0))
    return pl.pallas_call(
        functools.partial(statistics_body, n),
        grid_spec=pltpu.PrefetchScalarGridSpec(
            num_scalar_prefetch=1,
            grid=(n, pairs),
            in_specs=[
                pl.BlockSpec(
                    (kinds, 1, rows, w),
                    lambda m, p, j, k=k: (0, visit(k, m, p, pairs - 1), 0, 0),
                )
                for k in range(n)
            ]
            + [own] * len(olds),
            out_specs=[own] * len(olds)
            + [pl.BlockSpec((1, 1, 8, LANES), lambda m, p, j: (m, p, 0, 0))],
        ),
        out_shape=[jax.ShapeDtypeStruct(old.shape, jnp.float32) for old in olds]
        + [jax.ShapeDtypeStruct((n, pairs, 8, LANES), jnp.float32)],
        compiler_params=params(),
        cost_estimate=cost(0, olds[0].size * 10 * len(olds)),
    )(js, *received, *olds)


def restore_body(item, scale, source, out, buffer, result, in_sems, out_sems):
    columns, n, w = buffer.shape
    slots = result.shape[0]

    def fetch(c, _):
        pltpu.make_async_copy(source.at[item[c]], buffer.at[c], in_sems.at[c]).start()
        return 0

    def store(p, slot):
        start = pl.multiple_of(p * w, LANES)
        return pltpu.make_async_copy(
            result.at[slot], out.at[:, pl.ds(start, w)], out_sems.at[slot]
        )

    def step(p, _):
        slot = lax.rem(p, slots)

        @pl.when(p >= slots)
        def _():
            store(p - slots, slot).wait()

        for e in range(2):
            c = 2 * p + e
            pltpu.make_async_copy(source.at[item[c]], buffer.at[c], in_sems.at[c]).wait()
            scaled = (buffer[c].astype(jnp.float32) * scale[c]).astype(result.dtype)
            result[slot, :n, e * B : e * B + B] = scaled[:, :B]
            result[slot, n:, e * B : e * B + B] = scaled[:, B:]
        store(p, slot).start()
        return 0

    pairs = columns // 2
    lax.fori_loop(0, columns, fetch, 0)
    lax.fori_loop(0, pairs, step, 0)
    for p in range(pairs - slots, pairs):
        store(p, p % slots).wait()


def restore(item, scale, source):
    columns, n, w = source.shape
    slots = 4
    return pl.pallas_call(
        restore_body,
        in_specs=[SCALARS, SCALARS, ANY],
        out_specs=ANY,
        out_shape=jax.ShapeDtypeStruct((2 * n, columns * B), jnp.bfloat16),
        scratch_shapes=[
            pltpu.VMEM((columns, n, w), jnp.bfloat16),
            pltpu.VMEM((slots, 2 * n, w), jnp.bfloat16),
            pltpu.SemaphoreType.DMA((columns,)),
            pltpu.SemaphoreType.DMA((slots,)),
        ],
        compiler_params=params(),
        cost_estimate=cost(0, columns * n * w * 4),
    )(item, scale, source)


def hold(arrays):
    return pl.pallas_call(
        lambda *refs: None,
        in_specs=[ANY] * len(arrays),
        out_specs=[ANY] * len(arrays),
        out_shape=[jax.ShapeDtypeStruct(x.shape, x.dtype) for x in arrays],
        input_output_aliases={k: k for k in range(len(arrays))},
        compiler_params=params(),
        cost_estimate=cost(0, 0),
    )(*arrays)


def owner_local(grads, slots, stats_left, stats_right, root_left, root_right, second_moment):
    owners = lax.axis_size("fsdp")
    replicas = lax.axis_size("replica")
    grad = grads[0]
    rows, full_width = grad.shape
    columns = full_width // B
    row_blocks = slots.shape[0]
    sub_count = B // rows
    rd = rows // replicas
    half = owners // 2
    f = lax.axis_index("fsdp")
    r = lax.axis_index("replica")
    js = r ^ jnp.arange(replicas, dtype=jnp.int32)
    row_slots = lax.dynamic_index_in_dim(slots, f // sub_count, 0, keepdims=False)
    column_ids = jnp.arange(columns, dtype=jnp.int32)
    owner_ids = replicas * jnp.arange(owners, dtype=jnp.int32)

    def columns_of(low, high):
        ids = jnp.arange(owners, dtype=jnp.int32)
        wanted = owner_ids + (r ^ jnp.where(ids < half, low, high))
        return jnp.sum(jnp.where(row_slots == wanted[:, None], column_ids, 0), axis=1)

    far, near, cross, own = (columns_of(*k) for k in ((3, 3), (1, 2), (2, 1), (0, 0)))

    def swap(x, k):
        return lax.ppermute(x, "replica", [(i, i ^ k) for i in range(replicas)])

    def as_rows(x):
        return x.reshape(row_blocks, -1, sub_count * rd, B)

    def exchange(x):
        return lax.all_to_all(x, "fsdp", split_axis=0, concat_axis=0, tiled=True)

    n = rows // 2
    far_a, far_b = arrange(far, grad, 0, n)
    by_far = (swap(far_a, 1), swap(far_b, 2))
    x_a, y_b = arrange(near, grad, 0, n, after=(far_a,))
    from_x_a, from_y_b = swap(x_a, 1), swap(y_b, 2)
    roots = pack_roots(js, as_rows(root_left), as_rows(root_right), (x_a,))
    y_a, x_b = arrange(cross, grad, 0, n, (by_far,), after=(roots[0],))
    terms = ((from_x_a, swap(x_b, 1)), (swap(y_a, 2), from_y_b))
    owned, *sent = arrange(own, grad, 0, n, terms, halves=False, through=tuple(roots[1:]))
    blocks = exchange(owned)
    roots = [roots[0]] + [swap(x, k) for k, x in zip((1, 2, 3), sent)]

    products = gram(js, [blocks], rd)
    received = [products[0]] + [swap(products[k], k) for k in (1, 2, 3)]
    direction, direction_square = direct(js, [blocks], roots, rd, (products[0],))
    returned, *received[1:] = hold((exchange(direction), *received[1:]))
    gathered = lax.all_gather(returned, "replica").reshape(columns, n, 2 * B)

    left_new, right_new, moment, adam_square = statistics(
        js, received, [as_rows(x) for x in (stats_left, stats_right, second_moment)]
    )

    adam_square = adam_square[:, :, :2, 0].reshape(replicas, row_blocks)
    slot_ids = jnp.arange(replicas, dtype=jnp.int32)
    adam_square = jnp.sum(
        jnp.where((js[:, None] == slot_ids)[:, :, None], adam_square[:, None, :], 0.0), axis=0
    )
    direction_square = direction_square[:, :2, 0].reshape(row_blocks)
    owner_place = jnp.arange(owners, dtype=jnp.int32)[:, None, None, None] == f
    slot_place = (slot_ids == r)[:, None]
    squares = jnp.stack([adam_square, jnp.where(slot_place, direction_square, 0.0)])
    squares = lax.psum(jnp.where(owner_place, squares, 0.0), ("fsdp", "replica"))
    ratio = jnp.sqrt(squares[:, 0]) / jnp.sqrt(squares[:, 1] + 1e-06)
    row_ratio = lax.dynamic_index_in_dim(
        ratio.reshape(columns, row_blocks), f // sub_count, 1, keepdims=False
    )
    scale = jnp.sum(jnp.where(row_slots[:, None] == column_ids, row_ratio, 0.0), axis=1)

    item = lax.rem(row_slots, replicas) * owners + row_slots // replicas
    update = restore(item, scale, gathered)
    return (
        update,
        left_new.reshape(stats_left.shape),
        right_new.reshape(stats_right.shape),
        moment.reshape(second_moment.shape),
    )


def slot_columns(row_slots, row_count):
    column_ids = jnp.arange(row_count, dtype=jnp.int32)
    matches = row_slots[None, :] == column_ids[:, None]
    return jnp.sum(jnp.where(matches, column_ids[None, :], 0), axis=1)


def row_local(grads, slots, stats_left, stats_right, root_left, root_right, second_moment):
    fsdp_count = lax.axis_size("fsdp")
    replica_count = lax.axis_size("replica")
    local_grad = grads[0]
    shard_rows, full_width = local_grad.shape
    columns = full_width // B
    row_blocks = slots.shape[0]
    per_owner = columns // fsdp_count
    sub_count = B // shard_rows
    part_rows = shard_rows // replica_count
    mine_rows = sub_count * part_rows
    fsdp_index = lax.axis_index("fsdp")
    replica_index = lax.axis_index("replica")
    row_slots = lax.dynamic_index_in_dim(slots, fsdp_index // sub_count, 0, keepdims=False)
    slot_cols = slot_columns(row_slots, columns)
    summed = lax.psum_scatter(
        local_grad.astype(jnp.float32).astype(jnp.bfloat16),
        "replica",
        scatter_dimension=0,
        tiled=True,
    )
    row_count = summed.shape[0]
    ordered = jnp.take(summed.reshape(row_count, columns, B), slot_cols, axis=1)
    arrived = lax.all_to_all(
        ordered.reshape(row_count, fsdp_count, per_owner * B).transpose(1, 0, 2),
        "fsdp",
        split_axis=0,
        concat_axis=0,
        tiled=True,
    )
    own_split = arrived.reshape(row_blocks, sub_count, part_rows, per_owner, B).transpose(
        0, 3, 1, 2, 4
    )
    gathered = lax.all_gather(own_split[:, :, :, None], "replica", axis=3, tiled=True)
    full_grad = gathered.reshape(row_blocks, per_owner, B, B)
    own_rows = own_split.reshape(row_blocks, per_owner, mine_rows, B)

    def as_rows(array_in):
        return array_in.reshape(row_blocks, per_owner, mine_rows, B)

    column_split = full_grad.reshape(row_blocks, per_owner, B, sub_count, replica_count, part_rows)
    column_part = lax.dynamic_index_in_dim(column_split, replica_index, 4, keepdims=False).reshape(
        row_blocks, per_owner, B, mine_rows
    )
    left_gram = jnp.einsum(
        "abmk,abnk->abmn", own_rows, full_grad, preferred_element_type=jnp.float32
    )
    right_gram = jnp.einsum(
        "abkm,abkn->abmn", column_part, full_grad, preferred_element_type=jnp.float32
    )
    left_new = 0.95 * as_rows(stats_left) + 0.05 * left_gram
    right_new = 0.95 * as_rows(stats_right) + 0.05 * right_gram
    right_full = lax.all_gather(root_right, "replica", axis=3, tiled=True).reshape(
        row_blocks, per_owner, B, B
    )
    inner_left = jnp.einsum(
        "abmk,abkn->abmn", as_rows(root_left), full_grad, preferred_element_type=jnp.float32
    ).astype(jnp.bfloat16)
    direction = jnp.einsum(
        "abmk,abkn->abmn", inner_left, right_full, preferred_element_type=jnp.float32
    )
    grad_float = own_rows.astype(jnp.float32)
    moment = 0.95 * as_rows(second_moment) + 0.05 * grad_float * grad_float
    adam_step = grad_float / (jnp.sqrt(moment) + 1e-08)
    adam_square, shampoo_square = lax.psum(
        (jnp.sum(adam_step * adam_step, axis=(2, 3)), jnp.sum(direction * direction, axis=(2, 3))),
        "replica",
    )
    graft_scale = jnp.sqrt(adam_square) / jnp.sqrt(shampoo_square + 1e-06)
    update_part = (direction * graft_scale[:, :, None, None]).astype(jnp.bfloat16)
    outgoing = (
        update_part.reshape(row_blocks, per_owner, sub_count, part_rows, B)
        .transpose(0, 2, 3, 1, 4)
        .reshape(fsdp_count, part_rows, per_owner * B)
    )
    returned = lax.all_to_all(outgoing, "fsdp", split_axis=0, concat_axis=0, tiled=True)
    ordered = returned.transpose(1, 0, 2).reshape(part_rows, columns, B)
    update = lax.all_gather(
        jnp.take(ordered, row_slots, axis=1).reshape(part_rows, full_width),
        "replica",
        axis=0,
        tiled=True,
    )
    return (
        update,
        left_new.reshape(stats_left.shape),
        right_new.reshape(stats_right.shape),
        moment.reshape(second_moment.shape),
    )


def local(*arrays):
    replicas = lax.axis_size("replica")
    rows, full_width = arrays[0].shape[1:]
    per_owner = full_width // B // lax.axis_size("fsdp")
    if replicas == 4 and per_owner == replicas and 2 * rows == B:
        return owner_local(*arrays)
    return row_local(*arrays)


def solution(mesh):
    placed = (
        P("replica", "fsdp", None),
        P(),
        P(None, "fsdp", None, "replica", None, None),
        P(None, "fsdp", None, "replica", None, None),
        P(None, "fsdp", None, "replica", None, None),
        P(None, "fsdp", None, "replica", None, None),
        P(None, "fsdp", None, "replica", None, None),
    )
    return jax.shard_map(
        local,
        mesh=mesh,
        in_specs=placed,
        out_specs=(
            P("fsdp", None),
            P(None, "fsdp", None, "replica", None, None),
            P(None, "fsdp", None, "replica", None, None),
            P(None, "fsdp", None, "replica", None, None),
        ),
        check_vma=False,
    )
```

```python
import functools

import jax
import jax.numpy as jnp
from jax import lax
from jax.experimental import pallas as pl
from jax.experimental.pallas import tpu as pltpu
from jax.sharding import PartitionSpec as P

B = 576
LANES = 128
WINDOW = -(-B // LANES) * LANES
VMEM = 64 * 1024 * 1024 - 4096
ANY = pl.BlockSpec(memory_space=pl.ANY)
WHOLE = pl.BlockSpec(memory_space=pltpu.VMEM)
SCALARS = pl.BlockSpec(memory_space=pltpu.SMEM)


def params():
    return pltpu.CompilerParams(vmem_limit_bytes=VMEM)


def cost(flops, moved):
    return pl.CostEstimate(flops=flops, bytes_accessed=moved, transcendentals=0)


def arrange_body(n_add, offsets, n_after, base, halves, cols, grad, *refs):
    adds, refs = refs[: 2 * n_add], refs[2 * n_add + n_after :]
    outs, (buffer, sems) = refs[:-2], refs[-2:]
    n = outs[0].shape[1]
    count = buffer.shape[0]
    half = count // 2

    def copy(i):
        start = pl.multiple_of(cols[i] * B // LANES * LANES, LANES)
        return pltpu.make_async_copy(
            grad.at[pl.ds(base, 2 * n), pl.ds(start, WINDOW)], buffer.at[i], sems.at[i]
        )

    for i in range(count):
        copy(i).start()
    for i in range(count):
        copy(i).wait()
        out, at = (outs[i // half], i % half) if halves else (outs[0], i)
        for shift in (0, B % LANES):

            @pl.when(lax.rem(cols[i] * B, LANES) == shift)
            def _():
                part = buffer[i, :, shift : shift + B]
                out[at, :, :B] = part[:n]
                out[at, :, B:] = part[n:]

        if n_add:
            total = out[at].astype(jnp.float32)
            for k in range(i // half, 2 * n_add, 2):
                total = total + adds[k][offsets[k] + i % half].astype(jnp.float32)
            out[at] = total.astype(out.dtype)


def arrange(cols, grad, base, n, adds=(), halves=True, after=()):
    count = cols.shape[0]
    w = 2 * B
    adds = [part for pair in adds for part in pair]
    shapes = [(count // 2, n, w)] * 2 if halves else [(count, n, w)]
    return pl.pallas_call(
        functools.partial(
            arrange_body, len(adds) // 2, [part[1] for part in adds], len(after), base, halves
        ),
        in_specs=[SCALARS, ANY] + [WHOLE] * len(adds) + [ANY] * len(after),
        out_specs=[WHOLE] * len(shapes),
        out_shape=[jax.ShapeDtypeStruct(s, grad.dtype) for s in shapes],
        scratch_shapes=[
            pltpu.VMEM((count, 2 * n, WINDOW), grad.dtype),
            pltpu.SemaphoreType.DMA((count,)),
        ],
        compiler_params=params(),
        cost_estimate=cost(0, count * n * w * (4 + len(adds))),
    )(cols, grad, *[part[0] for part in adds], *after)


def visit(k, m, p, last):
    return jnp.where(m == k, p, jnp.where(m < k, 0, last))


def pack_roots_body(n, js, left, right, *refs):
    m = pl.program_id(0)
    for k, out in enumerate(refs[-n:]):

        @pl.when(m == k)
        def _():
            for kind, ref in enumerate((left, right)):
                for q in range(2):
                    out[kind, 0, :, q * B : q * B + B] = ref[q, 0]


def pack_roots(js, left, right, after):
    blocks, _, rows, _ = left.shape
    pairs, n, w = blocks // 2, js.shape[0], 2 * B
    source = pl.BlockSpec((2, 1, rows, B), lambda m, p, j: (p, j[m], 0, 0))
    return pl.pallas_call(
        functools.partial(pack_roots_body, n),
        grid_spec=pltpu.PrefetchScalarGridSpec(
            num_scalar_prefetch=1,
            grid=(n, pairs),
            in_specs=[source, source] + [ANY] * len(after),
            out_specs=[
                pl.BlockSpec(
                    (2, 1, rows, w),
                    lambda m, p, j, k=k: (0, visit(k, m, p, pairs - 1), 0, 0),
                )
                for k in range(n)
            ],
        ),
        out_shape=[jax.ShapeDtypeStruct((2, pairs, rows, w), left.dtype)] * n,
        compiler_params=params(),
        cost_estimate=cost(0, 4 * left.size * 2),
    )(js, left, right, *after)


def dot(x, y, dims):
    return lax.dot_general(x, y, (dims, ((), ())), preferred_element_type=jnp.float32)


def assemble(chunks, q, full):
    base = 0
    for chunk in chunks:
        n = chunk.shape[1]
        for h in range(2):
            for side in range(2):
                start = h * (B // 2) + base + side * n
                full[start : start + n, :] = chunk[2 * q + h, :, side * B : side * B + B]
        base += 2 * n


def own_rows(j, h, rd):
    return pl.ds(pl.multiple_of(h * (B // 2) + j * rd, 8), rd)


def gram_body(n, rd, n_chunks, js, *refs):
    chunks, refs = refs[:n_chunks], refs[n_chunks:]
    outs, (g16, g32, l32, r32) = refs[:n], refs[n:]
    for q in range(2):
        assemble(chunks, q, g16)
        g = g16[...]
        g32[...] = g.astype(jnp.float32)
        l32[...] = dot(g, g, ((1,), (1,)))
        r32[...] = dot(g, g, ((0,), (0,)))
        lanes = slice(q * B, q * B + B)
        for k in range(n):
            for kind, full in enumerate((g32, l32, r32)):
                parts = [full[own_rows(js[k], h, rd), :] for h in range(2)]
                outs[k][kind, 0, :, lanes] = jnp.concatenate(parts, axis=0).astype(jnp.bfloat16)


def gram(js, chunks, rd):
    n = js.shape[0]
    count, _, w = chunks[0].shape
    pairs, rows = count // 4, 2 * rd

    return pl.pallas_call(
        functools.partial(gram_body, n, rd, len(chunks)),
        grid_spec=pltpu.PrefetchScalarGridSpec(
            num_scalar_prefetch=1,
            grid=(pairs,),
            in_specs=[
                pl.BlockSpec((4,) + chunk.shape[1:], lambda p, j: (p, 0, 0)) for chunk in chunks
            ],
            out_specs=[pl.BlockSpec((3, 1, rows, w), lambda p, j: (0, p, 0, 0))] * n,
            scratch_shapes=[pltpu.VMEM((B, B), jnp.bfloat16)] + [pltpu.VMEM((B, B), jnp.float32)] * 3,
        ),
        out_shape=[jax.ShapeDtypeStruct((3, pairs, rows, w), jnp.bfloat16)] * n,
        compiler_params=params(),
        cost_estimate=cost(pairs * 8 * B**3, pairs * B * B * 2 * 8),
    )(js, *chunks)


def direct_body(n, rd, n_chunks, n_after, js, place, *refs):
    chunks, roots, refs = refs[:n_chunks], refs[n_chunks : n_chunks + n], refs[n_chunks + n :]
    outs, (square_out, g16, l32, r32, result, sems) = refs[n_after:-6], refs[-6:]
    p = pl.program_id(0)
    f = place[0]
    hr = result.shape[1]

    def send(k):
        return pltpu.make_async_copy(result.at[f ^ k], outs[k], sems.at[k])

    for q in range(2):
        assemble(chunks, q, g16)
        for k in range(n):
            for kind, full in enumerate((l32, r32)):
                part = roots[k][kind, 0, :, q * B : q * B + B].astype(jnp.float32)
                for h in range(2):
                    full[own_rows(js[k], h, rd), :] = part[h * rd : h * rd + rd]
        inner = dot(l32[...].astype(jnp.bfloat16), g16[...], ((1,), (0,))).astype(jnp.bfloat16)
        direction = dot(inner, r32[...].astype(jnp.bfloat16), ((1,), (0,)))
        square_out[0, q : q + 1, :] = jnp.full((1, LANES), jnp.sum(direction * direction))
        direction = direction.astype(jnp.bfloat16)
        for h in range(2):
            for side in range(2):
                start = h * (B // 2) + side * hr
                result[4 * p + 2 * q + h, :, side * B : side * B + B] = direction[start : start + hr]
    for k in range(len(outs)):

        @pl.when((f ^ k) // 4 == p)
        def _():
            send(k).start()

    @pl.when(p == pl.num_programs(0) - 1)
    def _():
        for k in range(len(outs)):
            send(k).wait()


def direct(js, place, chunks, roots, rd, after):
    n = js.shape[0]
    owners, _, w = chunks[0].shape
    hr = sum(chunk.shape[1] for chunk in chunks)
    pairs, rows = roots[0].shape[1], roots[0].shape[2]
    return pl.pallas_call(
        functools.partial(direct_body, n, rd, len(chunks), len(after)),
        grid_spec=pltpu.PrefetchScalarGridSpec(
            num_scalar_prefetch=2,
            grid=(pairs,),
            in_specs=[pl.BlockSpec((4,) + chunk.shape[1:], lambda p, j, f: (p, 0, 0)) for chunk in chunks]
            + [pl.BlockSpec((2, 1, rows, w), lambda p, j, f: (0, p, 0, 0))] * n
            + [ANY] * len(after),
            out_specs=[ANY] * owners + [pl.BlockSpec((1, 8, LANES), lambda p, j, f: (p, 0, 0))],
            scratch_shapes=[pltpu.VMEM((B, B), jnp.bfloat16)]
            + [pltpu.VMEM((B, B), jnp.float32)] * 2
            + [pltpu.VMEM((owners, hr, w), jnp.bfloat16), pltpu.SemaphoreType.DMA((owners,))],
        ),
        out_shape=[jax.ShapeDtypeStruct((hr, w), jnp.bfloat16)] * owners
        + [jax.ShapeDtypeStruct((pairs, 8, LANES), jnp.float32)],
        compiler_params=params(),
        cost_estimate=cost(pairs * 8 * B**3, pairs * B * B * 2 * 8),
    )(js, place, *chunks, *roots, *after)


def follow(arrays, after):
    return pl.pallas_call(
        lambda *refs: None,
        in_specs=[ANY] * (len(arrays) + len(after)),
        out_specs=[ANY] * len(arrays),
        out_shape=[jax.ShapeDtypeStruct(x.shape, x.dtype) for x in arrays],
        input_output_aliases={k: k for k in range(len(arrays))},
        compiler_params=params(),
        cost_estimate=cost(0, 0),
    )(*arrays, *after)


def collect_body(count, n_through, *refs):
    half = count // 2
    parts, low, high, sems = refs[:count], *refs[count + n_through : count + n_through + 2], refs[-1]
    copies = [
        pltpu.make_async_copy(part, (low, high)[k // half].at[k % half], sems.at[k])
        for k, part in enumerate(parts)
    ]
    for copy in copies:
        copy.start()
    for copy in copies:
        copy.wait()


def collect(parts, through):
    count = len(parts)
    halves = jax.ShapeDtypeStruct((count // 2,) + parts[0].shape, parts[0].dtype)
    return pl.pallas_call(
        functools.partial(collect_body, count, len(through)),
        in_specs=[ANY] * (count + len(through)),
        out_specs=[ANY] * (2 + len(through)),
        out_shape=[halves] * 2 + [jax.ShapeDtypeStruct(x.shape, x.dtype) for x in through],
        scratch_shapes=[pltpu.SemaphoreType.DMA((count,))],
        input_output_aliases={count + k: 2 + k for k in range(len(through))},
        compiler_params=params(),
        cost_estimate=cost(0, 2 * count * parts[0].size * 2),
    )(*parts, *through)


def statistics_body(n, js, *refs):
    received = refs[:n]
    left, right, moment, left_out, right_out, moment_out, square_out = refs[n:]
    m = pl.program_id(0)
    for k in range(n):

        @pl.when(m == k)
        def _():
            for q in range(2):
                lanes = slice(q * B, q * B + B)
                g, left_gram, right_gram = (
                    received[k][kind, 0, :, lanes].astype(jnp.float32) for kind in range(3)
                )
                left_out[q, 0] = 0.95 * left[q, 0] + 0.05 * left_gram
                right_out[q, 0] = 0.95 * right[q, 0] + 0.05 * right_gram
                second = 0.95 * moment[q, 0] + 0.05 * g * g
                moment_out[q, 0] = second
                adam = g / (jnp.sqrt(second) + 1e-08)
                square_out[0, 0, q : q + 1, :] = jnp.full((1, LANES), jnp.sum(adam * adam))


def statistics(js, received, olds):
    n = js.shape[0]
    blocks, _, rows, _ = olds[0].shape
    kinds, pairs, _, w = received[0].shape
    own = pl.BlockSpec((2, 1, rows, B), lambda m, p, j: (p, j[m], 0, 0))
    return pl.pallas_call(
        functools.partial(statistics_body, n),
        grid_spec=pltpu.PrefetchScalarGridSpec(
            num_scalar_prefetch=1,
            grid=(n, pairs),
            in_specs=[
                pl.BlockSpec(
                    (kinds, 1, rows, w),
                    lambda m, p, j, k=k: (0, visit(k, m, p, pairs - 1), 0, 0),
                )
                for k in range(n)
            ]
            + [own] * len(olds),
            out_specs=[own] * len(olds)
            + [pl.BlockSpec((1, 1, 8, LANES), lambda m, p, j: (m, p, 0, 0))],
        ),
        out_shape=[jax.ShapeDtypeStruct(old.shape, jnp.float32) for old in olds]
        + [jax.ShapeDtypeStruct((n, pairs, 8, LANES), jnp.float32)],
        compiler_params=params(),
        cost_estimate=cost(0, olds[0].size * 10 * len(olds)),
    )(js, *received, *olds)


def restore_body(src, item, scale, *refs):
    sources, (out, buffer, result, in_sems, out_sems) = refs[:-5], refs[-5:]
    columns, n, w = buffer.shape
    slots = result.shape[0]

    def fetch(c, _):
        for k, source in enumerate(sources):

            @pl.when(src[c] == k)
            def _():
                pltpu.make_async_copy(source.at[item[c]], buffer.at[c], in_sems.at[c]).start()

        return 0

    def store(p, slot):
        start = pl.multiple_of(p * w, LANES)
        return pltpu.make_async_copy(
            result.at[slot], out.at[:, pl.ds(start, w)], out_sems.at[slot]
        )

    def step(p, _):
        slot = lax.rem(p, slots)

        @pl.when(p >= slots)
        def _():
            store(p - slots, slot).wait()

        for e in range(2):
            c = 2 * p + e
            pltpu.make_async_copy(sources[0].at[0], buffer.at[c], in_sems.at[c]).wait()
            scaled = (buffer[c].astype(jnp.float32) * scale[c]).astype(result.dtype)
            result[slot, :n, e * B : e * B + B] = scaled[:, :B]
            result[slot, n:, e * B : e * B + B] = scaled[:, B:]
        store(p, slot).start()
        return 0

    pairs = columns // 2
    lax.fori_loop(0, columns, fetch, 0)
    lax.fori_loop(0, pairs, step, 0)
    for p in range(pairs - slots, pairs):
        store(p, p % slots).wait()


def restore(src, item, scale, sources):
    columns = src.shape[0]
    _, n, w = sources[0].shape
    slots = 4
    return pl.pallas_call(
        restore_body,
        in_specs=[SCALARS] * 3 + [ANY] * len(sources),
        out_specs=ANY,
        out_shape=jax.ShapeDtypeStruct((2 * n, columns * B), jnp.bfloat16),
        scratch_shapes=[
            pltpu.VMEM((columns, n, w), jnp.bfloat16),
            pltpu.VMEM((slots, 2 * n, w), jnp.bfloat16),
            pltpu.SemaphoreType.DMA((columns,)),
            pltpu.SemaphoreType.DMA((slots,)),
        ],
        compiler_params=params(),
        cost_estimate=cost(0, columns * n * w * 4),
    )(src, item, scale, *sources)


def owner_local(grads, slots, stats_left, stats_right, root_left, root_right, second_moment):
    owners = lax.axis_size("fsdp")
    replicas = lax.axis_size("replica")
    grad = grads[0]
    rows, full_width = grad.shape
    columns = full_width // B
    row_blocks = slots.shape[0]
    sub_count = B // rows
    rd = rows // replicas
    half = owners // 2
    f = lax.axis_index("fsdp")
    r = lax.axis_index("replica")
    js = r ^ jnp.arange(replicas, dtype=jnp.int32)
    row_slots = lax.dynamic_index_in_dim(slots, f // sub_count, 0, keepdims=False)
    column_ids = jnp.arange(columns, dtype=jnp.int32)
    owner_ids = jnp.arange(owners, dtype=jnp.int32)
    halves = (owner_ids[:half], owner_ids[half:])
    wanted = jnp.stack(
        [
            replicas * jnp.concatenate([halves[low], halves[high]])
            + (r ^ jnp.where(owner_ids < half, low_step, high_step))
            for low, low_step, high, high_step in ((0, 3, 0, 1), (1, 3, 1, 2), (0, 2, 1, 1), (0, 0, 1, 0))
        ]
    )
    cols = jnp.sum(jnp.where(row_slots == wanted[:, :, None], column_ids, 0), axis=2)

    def swap(x, k):
        return lax.ppermute(x, "replica", [(i, i ^ k) for i in range(replicas)])

    def as_rows(x):
        return x.reshape(row_blocks, -1, sub_count * rd, B)

    first = rows // 64 * 16
    chunks = ((0, first), (2 * first, rows // 2 - first))
    after, early, blocks = (), [], []
    for chunk in chunks:
        x, y = arrange(cols[:2].reshape(-1), grad, *chunk, after=after)
        early.append((swap(x, 1), swap(y, 2)))
        after = (x,)
    roots = pack_roots(js, as_rows(root_left), as_rows(root_right), after)
    after = (roots[0],)
    for (x, y), chunk in zip(early, chunks):
        y_a, x_b = arrange(cols[2], grad, *chunk, [((x, 0), (y, 0))], after=after)
        terms = [((x, half), (y, half)), ((swap(y_a, 2), 0), (swap(x_b, 1), 0))]
        (owned,) = arrange(cols[3], grad, *chunk, terms, halves=False)
        blocks.append(lax.all_to_all(owned, "fsdp", split_axis=0, concat_axis=0, tiled=True))
        after = (owned,)
    sent = follow(roots[1:], after)
    roots = [roots[0]] + [swap(x, k) for k, x in zip((1, 2, 3), sent)]

    place = f.reshape(1)
    products = gram(js, blocks, rd)
    received = [products[0]] + [swap(products[k], k) for k in (1, 2, 3)]
    *direction, direction_square = direct(js, place, blocks, roots, rd, (products[0],))
    direction[1:] = [
        lax.ppermute(direction[k], "fsdp", [(i, i ^ k) for i in range(owners)])
        for k in range(1, owners)
    ]
    a, b, *received[1:] = collect(direction, received[1:])

    x_a, y_b, x_b, y_a = swap(a, 1), swap(b, 2), swap(b, 1), swap(a, 2)
    gathered = (a, b, x_a, x_b, y_a, y_b, swap(x_a, 2), swap(y_b, 1))

    left_new, right_new, moment, adam_square = statistics(
        js, received, [as_rows(x) for x in (stats_left, stats_right, second_moment)]
    )

    adam_square = adam_square[:, :, :2, 0].reshape(replicas, row_blocks)
    slot_ids = jnp.arange(replicas, dtype=jnp.int32)
    adam_square = jnp.sum(
        jnp.where((js[:, None] == slot_ids)[:, :, None], adam_square[:, None, :], 0.0), axis=0
    )
    direction_square = direction_square[:, :2, 0].reshape(row_blocks)
    owner_place = jnp.arange(owners, dtype=jnp.int32)[:, None, None, None] == f
    slot_place = (slot_ids == r)[:, None]
    squares = jnp.stack([adam_square, jnp.where(slot_place, direction_square, 0.0)])
    squares = lax.psum(jnp.where(owner_place, squares, 0.0), ("fsdp", "replica"))
    ratio = jnp.sqrt(squares[:, 0]) / jnp.sqrt(squares[:, 1] + 1e-06)
    row_ratio = lax.dynamic_index_in_dim(
        ratio.reshape(columns, row_blocks), f // sub_count, 1, keepdims=False
    )
    scale = jnp.sum(jnp.where(row_slots[:, None] == column_ids, row_ratio, 0.0), axis=1)

    part = (row_slots // replicas) ^ f
    src = 2 * (lax.rem(row_slots, replicas) ^ r) + part // half
    update = restore(src, lax.rem(part, half), scale, gathered)
    return (
        update,
        left_new.reshape(stats_left.shape),
        right_new.reshape(stats_right.shape),
        moment.reshape(second_moment.shape),
    )


def slot_columns(row_slots, row_count):
    column_ids = jnp.arange(row_count, dtype=jnp.int32)
    matches = row_slots[None, :] == column_ids[:, None]
    return jnp.sum(jnp.where(matches, column_ids[None, :], 0), axis=1)


def row_local(grads, slots, stats_left, stats_right, root_left, root_right, second_moment):
    fsdp_count = lax.axis_size("fsdp")
    replica_count = lax.axis_size("replica")
    local_grad = grads[0]
    shard_rows, full_width = local_grad.shape
    columns = full_width // B
    row_blocks = slots.shape[0]
    per_owner = columns // fsdp_count
    sub_count = B // shard_rows
    part_rows = shard_rows // replica_count
    mine_rows = sub_count * part_rows
    fsdp_index = lax.axis_index("fsdp")
    replica_index = lax.axis_index("replica")
    row_slots = lax.dynamic_index_in_dim(slots, fsdp_index // sub_count, 0, keepdims=False)
    slot_cols = slot_columns(row_slots, columns)
    summed = lax.psum_scatter(
        local_grad.astype(jnp.float32).astype(jnp.bfloat16),
        "replica",
        scatter_dimension=0,
        tiled=True,
    )
    row_count = summed.shape[0]
    ordered = jnp.take(summed.reshape(row_count, columns, B), slot_cols, axis=1)
    arrived = lax.all_to_all(
        ordered.reshape(row_count, fsdp_count, per_owner * B).transpose(1, 0, 2),
        "fsdp",
        split_axis=0,
        concat_axis=0,
        tiled=True,
    )
    own_split = arrived.reshape(row_blocks, sub_count, part_rows, per_owner, B).transpose(
        0, 3, 1, 2, 4
    )
    gathered = lax.all_gather(own_split[:, :, :, None], "replica", axis=3, tiled=True)
    full_grad = gathered.reshape(row_blocks, per_owner, B, B)
    own_rows = own_split.reshape(row_blocks, per_owner, mine_rows, B)

    def as_rows(array_in):
        return array_in.reshape(row_blocks, per_owner, mine_rows, B)

    column_split = full_grad.reshape(row_blocks, per_owner, B, sub_count, replica_count, part_rows)
    column_part = lax.dynamic_index_in_dim(column_split, replica_index, 4, keepdims=False).reshape(
        row_blocks, per_owner, B, mine_rows
    )
    left_gram = jnp.einsum(
        "abmk,abnk->abmn", own_rows, full_grad, preferred_element_type=jnp.float32
    )
    right_gram = jnp.einsum(
        "abkm,abkn->abmn", column_part, full_grad, preferred_element_type=jnp.float32
    )
    left_new = 0.95 * as_rows(stats_left) + 0.05 * left_gram
    right_new = 0.95 * as_rows(stats_right) + 0.05 * right_gram
    right_full = lax.all_gather(root_right, "replica", axis=3, tiled=True).reshape(
        row_blocks, per_owner, B, B
    )
    inner_left = jnp.einsum(
        "abmk,abkn->abmn", as_rows(root_left), full_grad, preferred_element_type=jnp.float32
    ).astype(jnp.bfloat16)
    direction = jnp.einsum(
        "abmk,abkn->abmn", inner_left, right_full, preferred_element_type=jnp.float32
    )
    grad_float = own_rows.astype(jnp.float32)
    moment = 0.95 * as_rows(second_moment) + 0.05 * grad_float * grad_float
    adam_step = grad_float / (jnp.sqrt(moment) + 1e-08)
    adam_square, shampoo_square = lax.psum(
        (jnp.sum(adam_step * adam_step, axis=(2, 3)), jnp.sum(direction * direction, axis=(2, 3))),
        "replica",
    )
    graft_scale = jnp.sqrt(adam_square) / jnp.sqrt(shampoo_square + 1e-06)
    update_part = (direction * graft_scale[:, :, None, None]).astype(jnp.bfloat16)
    outgoing = (
        update_part.reshape(row_blocks, per_owner, sub_count, part_rows, B)
        .transpose(0, 2, 3, 1, 4)
        .reshape(fsdp_count, part_rows, per_owner * B)
    )
    returned = lax.all_to_all(outgoing, "fsdp", split_axis=0, concat_axis=0, tiled=True)
    ordered = returned.transpose(1, 0, 2).reshape(part_rows, columns, B)
    update = lax.all_gather(
        jnp.take(ordered, row_slots, axis=1).reshape(part_rows, full_width),
        "replica",
        axis=0,
        tiled=True,
    )
    return (
        update,
        left_new.reshape(stats_left.shape),
        right_new.reshape(stats_right.shape),
        moment.reshape(second_moment.shape),
    )


def local(*arrays):
    replicas = lax.axis_size("replica")
    rows, full_width = arrays[0].shape[1:]
    owners = lax.axis_size("fsdp")
    per_owner = full_width // B // owners
    if replicas == 4 and per_owner == replicas and 2 * rows == B and owners == 8:
        return owner_local(*arrays)
    return row_local(*arrays)


def solution(mesh):
    placed = (
        P("replica", "fsdp", None),
        P(),
        P(None, "fsdp", None, "replica", None, None),
        P(None, "fsdp", None, "replica", None, None),
        P(None, "fsdp", None, "replica", None, None),
        P(None, "fsdp", None, "replica", None, None),
        P(None, "fsdp", None, "replica", None, None),
    )
    return jax.shard_map(
        local,
        mesh=mesh,
        in_specs=placed,
        out_specs=(
            P("fsdp", None),
            P(None, "fsdp", None, "replica", None, None),
            P(None, "fsdp", None, "replica", None, None),
            P(None, "fsdp", None, "replica", None, None),
        ),
        check_vma=False,
    )
```

```python
import functools

import jax
import jax.numpy as jnp
from jax import lax
from jax.experimental import pallas as pl
from jax.experimental.pallas import tpu as pltpu
from jax.sharding import PartitionSpec as P

B = 576
LANES = 128
WINDOW = -(-B // LANES) * LANES
VMEM = 64 * 1024 * 1024 - 4096
ANY = pl.BlockSpec(memory_space=pl.ANY)
WHOLE = pl.BlockSpec(memory_space=pltpu.VMEM)
SCALARS = pl.BlockSpec(memory_space=pltpu.SMEM)


def params():
    return pltpu.CompilerParams(vmem_limit_bytes=VMEM)


def cost(flops, moved):
    return pl.CostEstimate(flops=flops, bytes_accessed=moved, transcendentals=0)


def arrange_body(n_add, offsets, n_after, base, halves, cols, grad, *refs):
    adds, refs = refs[: 2 * n_add], refs[2 * n_add + n_after :]
    outs, (buffer, sems) = refs[:-2], refs[-2:]
    n = outs[0].shape[1]
    count = buffer.shape[0]
    half = count // 2

    def copy(i):
        start = pl.multiple_of(cols[i] * B // LANES * LANES, LANES)
        return pltpu.make_async_copy(
            grad.at[pl.ds(base, 2 * n), pl.ds(start, WINDOW)], buffer.at[i], sems.at[i]
        )

    for i in range(count):
        copy(i).start()
    for i in range(count):
        copy(i).wait()
        out, at = (outs[i // half], i % half) if halves else (outs[0], i)
        for shift in (0, B % LANES):

            @pl.when(lax.rem(cols[i] * B, LANES) == shift)
            def _():
                part = buffer[i, :, shift : shift + B]
                out[at, :, :B] = part[:n]
                out[at, :, B:] = part[n:]

        if n_add:
            total = out[at].astype(jnp.float32)
            for k in range(i // half, 2 * n_add, 2):
                total = total + adds[k][offsets[k] + i % half].astype(jnp.float32)
            out[at] = total.astype(out.dtype)


def arrange(cols, grad, base, n, adds=(), halves=True, after=()):
    count = cols.shape[0]
    w = 2 * B
    adds = [part for pair in adds for part in pair]
    shapes = [(count // 2, n, w)] * 2 if halves else [(count, n, w)]
    return pl.pallas_call(
        functools.partial(
            arrange_body, len(adds) // 2, [part[1] for part in adds], len(after), base, halves
        ),
        in_specs=[SCALARS, ANY] + [WHOLE] * len(adds) + [ANY] * len(after),
        out_specs=[WHOLE] * len(shapes),
        out_shape=[jax.ShapeDtypeStruct(s, grad.dtype) for s in shapes],
        scratch_shapes=[
            pltpu.VMEM((count, 2 * n, WINDOW), grad.dtype),
            pltpu.SemaphoreType.DMA((count,)),
        ],
        compiler_params=params(),
        cost_estimate=cost(0, count * n * w * (4 + len(adds))),
    )(cols, grad, *[part[0] for part in adds], *after)


def visit(k, m, p, last):
    return jnp.where(m == k, p, jnp.where(m < k, 0, last))


def pack_roots_body(n, js, left, right, *refs):
    m = pl.program_id(0)
    for k, out in enumerate(refs[-n:]):

        @pl.when(m == k)
        def _():
            for kind, ref in enumerate((left, right)):
                for q in range(2):
                    out[kind, 0, :, q * B : q * B + B] = ref[q, 0]


def pack_roots(js, left, right, after):
    blocks, _, rows, _ = left.shape
    pairs, n, w = blocks // 2, js.shape[0], 2 * B
    source = pl.BlockSpec((2, 1, rows, B), lambda m, p, j: (p, j[m], 0, 0))
    return pl.pallas_call(
        functools.partial(pack_roots_body, n),
        grid_spec=pltpu.PrefetchScalarGridSpec(
            num_scalar_prefetch=1,
            grid=(n, pairs),
            in_specs=[source, source] + [ANY] * len(after),
            out_specs=[
                pl.BlockSpec(
                    (2, 1, rows, w),
                    lambda m, p, j, k=k: (0, visit(k, m, p, pairs - 1), 0, 0),
                )
                for k in range(n)
            ],
        ),
        out_shape=[jax.ShapeDtypeStruct((2, pairs, rows, w), left.dtype)] * n,
        compiler_params=params(),
        cost_estimate=cost(0, 4 * left.size * 2),
    )(js, left, right, *after)


def dot(x, y, dims):
    return lax.dot_general(x, y, (dims, ((), ())), preferred_element_type=jnp.float32)


def assemble(chunks, q, full):
    base = 0
    for chunk in chunks:
        n = chunk.shape[1]
        for h in range(2):
            for side in range(2):
                start = h * (B // 2) + base + side * n
                full[start : start + n, :] = chunk[2 * q + h, :, side * B : side * B + B]
        base += 2 * n


def own_rows(j, h, rd):
    return pl.ds(pl.multiple_of(h * (B // 2) + j * rd, 8), rd)


def gram_body(n, rd, n_chunks, js, *refs):
    chunks, refs = refs[:n_chunks], refs[n_chunks:]
    outs, (g16, g32, l32, r32) = refs[:n], refs[n:]
    for q in range(2):
        assemble(chunks, q, g16)
        g = g16[...]
        g32[...] = g.astype(jnp.float32)
        l32[...] = dot(g, g, ((1,), (1,)))
        r32[...] = dot(g, g, ((0,), (0,)))
        lanes = slice(q * B, q * B + B)
        for k in range(n):
            for kind, full in enumerate((g32, l32, r32)):
                parts = [full[own_rows(js[k], h, rd), :] for h in range(2)]
                outs[k][kind, 0, :, lanes] = jnp.concatenate(parts, axis=0).astype(jnp.bfloat16)


def gram(js, chunks, rd):
    n = js.shape[0]
    count, _, w = chunks[0].shape
    pairs, rows = count // 4, 2 * rd

    return pl.pallas_call(
        functools.partial(gram_body, n, rd, len(chunks)),
        grid_spec=pltpu.PrefetchScalarGridSpec(
            num_scalar_prefetch=1,
            grid=(pairs,),
            in_specs=[
                pl.BlockSpec((4,) + chunk.shape[1:], lambda p, j: (p, 0, 0)) for chunk in chunks
            ],
            out_specs=[pl.BlockSpec((3, 1, rows, w), lambda p, j: (0, p, 0, 0))] * n,
            scratch_shapes=[pltpu.VMEM((B, B), jnp.bfloat16)] + [pltpu.VMEM((B, B), jnp.float32)] * 3,
        ),
        out_shape=[jax.ShapeDtypeStruct((3, pairs, rows, w), jnp.bfloat16)] * n,
        compiler_params=params(),
        cost_estimate=cost(pairs * 8 * B**3, pairs * B * B * 2 * 8),
    )(js, *chunks)


def direct_body(n, rd, n_chunks, n_after, js, place, *refs):
    chunks, roots, refs = refs[:n_chunks], refs[n_chunks : n_chunks + n], refs[n_chunks + n :]
    outs, (square_out, g16, l32, r32, result, sems) = refs[n_after:-6], refs[-6:]
    p = pl.program_id(0)
    f = place[0]
    hr = result.shape[1]

    def send(k):
        return pltpu.make_async_copy(result.at[f ^ k], outs[k], sems.at[k])

    for q in range(2):
        assemble(chunks, q, g16)
        for k in range(n):
            for kind, full in enumerate((l32, r32)):
                part = roots[k][kind, 0, :, q * B : q * B + B].astype(jnp.float32)
                for h in range(2):
                    full[own_rows(js[k], h, rd), :] = part[h * rd : h * rd + rd]
        inner = dot(l32[...].astype(jnp.bfloat16), g16[...], ((1,), (0,))).astype(jnp.bfloat16)
        direction = dot(inner, r32[...].astype(jnp.bfloat16), ((1,), (0,)))
        square_out[0, q : q + 1, :] = jnp.full((1, LANES), jnp.sum(direction * direction))
        direction = direction.astype(jnp.bfloat16)
        for h in range(2):
            for side in range(2):
                start = h * (B // 2) + side * hr
                result[4 * p + 2 * q + h, :, side * B : side * B + B] = direction[start : start + hr]
    for k in range(len(outs)):

        @pl.when((f ^ k) // 4 == p)
        def _():
            send(k).start()

    @pl.when(p == pl.num_programs(0) - 1)
    def _():
        for k in range(len(outs)):
            send(k).wait()


def direct(js, place, chunks, roots, rd, after):
    n = js.shape[0]
    owners, _, w = chunks[0].shape
    hr = sum(chunk.shape[1] for chunk in chunks)
    pairs, rows = roots[0].shape[1], roots[0].shape[2]
    return pl.pallas_call(
        functools.partial(direct_body, n, rd, len(chunks), len(after)),
        grid_spec=pltpu.PrefetchScalarGridSpec(
            num_scalar_prefetch=2,
            grid=(pairs,),
            in_specs=[pl.BlockSpec((4,) + chunk.shape[1:], lambda p, j, f: (p, 0, 0)) for chunk in chunks]
            + [pl.BlockSpec((2, 1, rows, w), lambda p, j, f: (0, p, 0, 0))] * n
            + [ANY] * len(after),
            out_specs=[ANY] * owners + [pl.BlockSpec((1, 8, LANES), lambda p, j, f: (p, 0, 0))],
            scratch_shapes=[pltpu.VMEM((B, B), jnp.bfloat16)]
            + [pltpu.VMEM((B, B), jnp.float32)] * 2
            + [pltpu.VMEM((owners, hr, w), jnp.bfloat16), pltpu.SemaphoreType.DMA((owners,))],
        ),
        out_shape=[jax.ShapeDtypeStruct((hr, w), jnp.bfloat16)] * owners
        + [jax.ShapeDtypeStruct((pairs, 8, LANES), jnp.float32)],
        compiler_params=params(),
        cost_estimate=cost(pairs * 8 * B**3, pairs * B * B * 2 * 8),
    )(js, place, *chunks, *roots, *after)


def follow(arrays, after):
    return pl.pallas_call(
        lambda *refs: None,
        in_specs=[ANY] * (len(arrays) + len(after)),
        out_specs=[ANY] * len(arrays),
        out_shape=[jax.ShapeDtypeStruct(x.shape, x.dtype) for x in arrays],
        input_output_aliases={k: k for k in range(len(arrays))},
        compiler_params=params(),
        cost_estimate=cost(0, 0),
    )(*arrays, *after)


def collect_body(*refs):
    *parts, low, high, buffer, in_sems, out_sems = refs
    half = len(parts) // 2

    def arrive(k):
        return pltpu.make_async_copy(parts[k], buffer.at[k], in_sems.at[k])

    def leave(k):
        return pltpu.make_async_copy(
            buffer.at[k], (low, high)[k // half].at[k % half], out_sems.at[k]
        )

    for k in range(len(parts)):
        arrive(k).start()
    for k in range(len(parts)):
        arrive(k).wait()
        leave(k).start()
    for k in range(len(parts)):
        leave(k).wait()


def collect(parts):
    count = len(parts)
    halves = jax.ShapeDtypeStruct((count // 2,) + parts[0].shape, parts[0].dtype)
    return pl.pallas_call(
        collect_body,
        in_specs=[ANY] * count,
        out_specs=[ANY] * 2,
        out_shape=[halves] * 2,
        scratch_shapes=[pltpu.VMEM((count,) + parts[0].shape, parts[0].dtype)]
        + [pltpu.SemaphoreType.DMA((count,))] * 2,
        compiler_params=params(),
        cost_estimate=cost(0, 2 * count * parts[0].size * 2),
    )(*parts)


def moment_body(q, received, moment, moment_out, square_out):
    g = received[0, 0, :, q * B : q * B + B].astype(jnp.float32)
    second = 0.95 * moment[q, 0] + 0.05 * g * g
    moment_out[q, 0] = second
    adam = g / (jnp.sqrt(second) + 1e-08)
    square_out[0, 0, q : q + 1, :] = jnp.full((1, LANES), jnp.sum(adam * adam))


def gram_update_body(q, received, left, right, left_out, right_out):
    for kind, old, new in ((1, left, left_out), (2, right, right_out)):
        product = received[kind, 0, :, q * B : q * B + B].astype(jnp.float32)
        new[q, 0] = 0.95 * old[q, 0] + 0.05 * product


def by_rows_body(body, n, js, *refs):
    m = pl.program_id(0)
    for k in range(n):

        @pl.when(m == k)
        def _():
            for q in range(2):
                body(q, refs[k], *refs[n:])


def by_rows(body, kinds, js, received, olds, squares):
    n = js.shape[0]
    blocks, _, rows, _ = olds[0].shape
    pairs, w = received[0].shape[1], received[0].shape[3]
    own = pl.BlockSpec((2, 1, rows, B), lambda m, p, j: (p, j[m], 0, 0))
    out_specs = [own] * len(olds)
    out_shape = [jax.ShapeDtypeStruct(old.shape, jnp.float32) for old in olds]
    if squares:
        out_specs.append(pl.BlockSpec((1, 1, 8, LANES), lambda m, p, j: (m, p, 0, 0)))
        out_shape.append(jax.ShapeDtypeStruct((n, pairs, 8, LANES), jnp.float32))
    return pl.pallas_call(
        functools.partial(by_rows_body, body, n),
        grid_spec=pltpu.PrefetchScalarGridSpec(
            num_scalar_prefetch=1,
            grid=(n, pairs),
            in_specs=[
                pl.BlockSpec(
                    (kinds, 1, rows, w),
                    lambda m, p, j, k=k: (0, visit(k, m, p, pairs - 1), 0, 0),
                )
                for k in range(n)
            ]
            + [own] * len(olds),
            out_specs=out_specs,
        ),
        out_shape=out_shape,
        compiler_params=params(),
        cost_estimate=cost(0, olds[0].size * 10 * len(olds)),
    )(js, *received, *olds)


def restore_body(src, item, scale, *refs):
    sources, (out, buffer, result, in_sems, out_sems) = refs[:-5], refs[-5:]
    columns, n, w = buffer.shape
    slots = result.shape[0]

    def fetch(c, _):
        for k, source in enumerate(sources):

            @pl.when(src[c] == k)
            def _():
                pltpu.make_async_copy(source.at[item[c]], buffer.at[c], in_sems.at[c]).start()

        return 0

    def store(p, slot):
        start = pl.multiple_of(p * w, LANES)
        return pltpu.make_async_copy(
            result.at[slot], out.at[:, pl.ds(start, w)], out_sems.at[slot]
        )

    def step(p, _):
        slot = lax.rem(p, slots)

        @pl.when(p >= slots)
        def _():
            store(p - slots, slot).wait()

        for e in range(2):
            c = 2 * p + e
            pltpu.make_async_copy(sources[0].at[0], buffer.at[c], in_sems.at[c]).wait()
            scaled = (buffer[c].astype(jnp.float32) * scale[c]).astype(result.dtype)
            result[slot, :n, e * B : e * B + B] = scaled[:, :B]
            result[slot, n:, e * B : e * B + B] = scaled[:, B:]
        store(p, slot).start()
        return 0

    pairs = columns // 2
    lax.fori_loop(0, columns, fetch, 0)
    lax.fori_loop(0, pairs, step, 0)
    for p in range(pairs - slots, pairs):
        store(p, p % slots).wait()


def restore(src, item, scale, sources):
    columns = src.shape[0]
    _, n, w = sources[0].shape
    slots = 4
    return pl.pallas_call(
        restore_body,
        in_specs=[SCALARS] * 3 + [ANY] * len(sources),
        out_specs=ANY,
        out_shape=jax.ShapeDtypeStruct((2 * n, columns * B), jnp.bfloat16),
        scratch_shapes=[
            pltpu.VMEM((columns, n, w), jnp.bfloat16),
            pltpu.VMEM((slots, 2 * n, w), jnp.bfloat16),
            pltpu.SemaphoreType.DMA((columns,)),
            pltpu.SemaphoreType.DMA((slots,)),
        ],
        compiler_params=params(),
        cost_estimate=cost(0, columns * n * w * 4),
    )(src, item, scale, *sources)


def owner_local(grads, slots, stats_left, stats_right, root_left, root_right, second_moment):
    owners = lax.axis_size("fsdp")
    replicas = lax.axis_size("replica")
    grad = grads[0]
    rows, full_width = grad.shape
    columns = full_width // B
    row_blocks = slots.shape[0]
    sub_count = B // rows
    rd = rows // replicas
    half = owners // 2
    f = lax.axis_index("fsdp")
    r = lax.axis_index("replica")
    js = r ^ jnp.arange(replicas, dtype=jnp.int32)
    row_slots = lax.dynamic_index_in_dim(slots, f // sub_count, 0, keepdims=False)
    column_ids = jnp.arange(columns, dtype=jnp.int32)
    owner_ids = jnp.arange(owners, dtype=jnp.int32)
    halves = (owner_ids[:half], owner_ids[half:])
    wanted = jnp.stack(
        [
            replicas * jnp.concatenate([halves[low], halves[high]])
            + (r ^ jnp.where(owner_ids < half, low_step, high_step))
            for low, low_step, high, high_step in ((0, 3, 0, 1), (1, 3, 1, 2), (0, 2, 1, 1), (0, 0, 1, 0))
        ]
    )
    cols = jnp.sum(jnp.where(row_slots == wanted[:, :, None], column_ids, 0), axis=2)

    def swap(x, k):
        return lax.ppermute(x, "replica", [(i, i ^ k) for i in range(replicas)])

    def as_rows(x):
        return x.reshape(row_blocks, -1, sub_count * rd, B)

    first = rows // 64 * 16
    lower, upper = (0, first), (2 * first, rows // 2 - first)

    def exchange(x):
        return lax.all_to_all(x, "fsdp", split_axis=0, concat_axis=0, tiled=True)

    x, y = arrange(cols[:2].reshape(-1), grad, *lower)
    early = (swap(x, 1), swap(y, 2))
    far_a, far_b = arrange(cols[:2, :half].reshape(-1), grad, *upper, after=(x,))
    far = (swap(far_a, 1), swap(far_b, 2))
    x_a, y_b = arrange(cols[:2, half:].reshape(-1), grad, *upper, after=(far_a,))
    near = (swap(x_a, 1), swap(y_b, 2))
    roots = pack_roots(js, as_rows(root_left), as_rows(root_right), (x_a,))
    y_a, x_b = arrange(cols[2], grad, *lower, [[(x, 0) for x in early]], after=(roots[0],))
    cross = (swap(y_a, 2), swap(x_b, 1))
    y_a, x_b = arrange(cols[2], grad, *upper, [[(x, 0) for x in far]], after=(y_a,))
    late = (swap(y_a, 2), swap(x_b, 1))
    terms = [[(x, half) for x in early], [(x, 0) for x in cross]]
    (owned,) = arrange(cols[3], grad, *lower, terms, halves=False, after=(y_a,))
    blocks = [exchange(owned)]
    terms = [[(x, 0) for x in near], [(x, 0) for x in late]]
    (owned,) = arrange(cols[3], grad, *upper, terms, halves=False, after=(owned,))
    blocks.append(exchange(owned))
    after = (owned,)
    sent = follow(roots[1:], after)
    roots = [roots[0]] + [swap(x, k) for k, x in zip((1, 2, 3), sent)]

    place = f.reshape(1)
    products = gram(js, blocks, rd)
    received = [products[0]] + [swap(products[k], k) for k in (1, 2, 3)]
    *direction, direction_square = direct(js, place, blocks, roots, rd, (products[0],))
    direction[1:] = [
        lax.ppermute(direction[k], "fsdp", [(i, i ^ k) for i in range(owners)])
        for k in range(1, owners)
    ]
    a, b = collect(direction)

    x_a, y_b = swap(a, 1), swap(b, 2)
    late_a, late_b = follow((a, b), received[1:])
    x_b, y_a = swap(late_b, 1), swap(late_a, 2)

    moment, adam_square = by_rows(
        moment_body, 1, js, received, [as_rows(second_moment)], True
    )
    adam_square = adam_square[:, :, :2, 0].reshape(replicas, row_blocks)
    slot_ids = jnp.arange(replicas, dtype=jnp.int32)
    adam_square = jnp.sum(
        jnp.where((js[:, None] == slot_ids)[:, :, None], adam_square[:, None, :], 0.0), axis=0
    )
    direction_square = direction_square[:, :2, 0].reshape(row_blocks)
    owner_place = jnp.arange(owners, dtype=jnp.int32)[:, None, None, None] == f
    slot_place = (slot_ids == r)[:, None]
    squares = jnp.stack([adam_square, jnp.where(slot_place, direction_square, 0.0)])
    squares = lax.psum(jnp.where(owner_place, squares, 0.0), ("fsdp", "replica"))
    ratio = jnp.sqrt(squares[:, 0]) / jnp.sqrt(squares[:, 1] + 1e-06)
    row_ratio = lax.dynamic_index_in_dim(
        ratio.reshape(columns, row_blocks), f // sub_count, 1, keepdims=False
    )
    scale = jnp.sum(jnp.where(row_slots[:, None] == column_ids, row_ratio, 0.0), axis=1)

    x_a, y_b = follow((x_a, y_b), (scale, x_b, y_a))
    left_new, right_new = by_rows(
        gram_update_body, 3, js, received, [as_rows(stats_left), as_rows(stats_right)], False
    )
    part = (row_slots // replicas) ^ f
    src = 2 * (lax.rem(row_slots, replicas) ^ r) + part // half
    gathered = (late_a, late_b, x_a, x_b, y_a, y_b, swap(x_a, 2), swap(y_b, 1))
    update = restore(src, lax.rem(part, half), scale, gathered)
    return (
        update,
        left_new.reshape(stats_left.shape),
        right_new.reshape(stats_right.shape),
        moment.reshape(second_moment.shape),
    )


def slot_columns(row_slots, row_count):
    column_ids = jnp.arange(row_count, dtype=jnp.int32)
    matches = row_slots[None, :] == column_ids[:, None]
    return jnp.sum(jnp.where(matches, column_ids[None, :], 0), axis=1)


def row_local(grads, slots, stats_left, stats_right, root_left, root_right, second_moment):
    fsdp_count = lax.axis_size("fsdp")
    replica_count = lax.axis_size("replica")
    local_grad = grads[0]
    shard_rows, full_width = local_grad.shape
    columns = full_width // B
    row_blocks = slots.shape[0]
    per_owner = columns // fsdp_count
    sub_count = B // shard_rows
    part_rows = shard_rows // replica_count
    mine_rows = sub_count * part_rows
    fsdp_index = lax.axis_index("fsdp")
    replica_index = lax.axis_index("replica")
    row_slots = lax.dynamic_index_in_dim(slots, fsdp_index // sub_count, 0, keepdims=False)
    slot_cols = slot_columns(row_slots, columns)
    summed = lax.psum_scatter(
        local_grad.astype(jnp.float32).astype(jnp.bfloat16),
        "replica",
        scatter_dimension=0,
        tiled=True,
    )
    row_count = summed.shape[0]
    ordered = jnp.take(summed.reshape(row_count, columns, B), slot_cols, axis=1)
    arrived = lax.all_to_all(
        ordered.reshape(row_count, fsdp_count, per_owner * B).transpose(1, 0, 2),
        "fsdp",
        split_axis=0,
        concat_axis=0,
        tiled=True,
    )
    own_split = arrived.reshape(row_blocks, sub_count, part_rows, per_owner, B).transpose(
        0, 3, 1, 2, 4
    )
    gathered = lax.all_gather(own_split[:, :, :, None], "replica", axis=3, tiled=True)
    full_grad = gathered.reshape(row_blocks, per_owner, B, B)
    own_rows = own_split.reshape(row_blocks, per_owner, mine_rows, B)

    def as_rows(array_in):
        return array_in.reshape(row_blocks, per_owner, mine_rows, B)

    column_split = full_grad.reshape(row_blocks, per_owner, B, sub_count, replica_count, part_rows)
    column_part = lax.dynamic_index_in_dim(column_split, replica_index, 4, keepdims=False).reshape(
        row_blocks, per_owner, B, mine_rows
    )
    left_gram = jnp.einsum(
        "abmk,abnk->abmn", own_rows, full_grad, preferred_element_type=jnp.float32
    )
    right_gram = jnp.einsum(
        "abkm,abkn->abmn", column_part, full_grad, preferred_element_type=jnp.float32
    )
    left_new = 0.95 * as_rows(stats_left) + 0.05 * left_gram
    right_new = 0.95 * as_rows(stats_right) + 0.05 * right_gram
    right_full = lax.all_gather(root_right, "replica", axis=3, tiled=True).reshape(
        row_blocks, per_owner, B, B
    )
    inner_left = jnp.einsum(
        "abmk,abkn->abmn", as_rows(root_left), full_grad, preferred_element_type=jnp.float32
    ).astype(jnp.bfloat16)
    direction = jnp.einsum(
        "abmk,abkn->abmn", inner_left, right_full, preferred_element_type=jnp.float32
    )
    grad_float = own_rows.astype(jnp.float32)
    moment = 0.95 * as_rows(second_moment) + 0.05 * grad_float * grad_float
    adam_step = grad_float / (jnp.sqrt(moment) + 1e-08)
    adam_square, shampoo_square = lax.psum(
        (jnp.sum(adam_step * adam_step, axis=(2, 3)), jnp.sum(direction * direction, axis=(2, 3))),
        "replica",
    )
    graft_scale = jnp.sqrt(adam_square) / jnp.sqrt(shampoo_square + 1e-06)
    update_part = (direction * graft_scale[:, :, None, None]).astype(jnp.bfloat16)
    outgoing = (
        update_part.reshape(row_blocks, per_owner, sub_count, part_rows, B)
        .transpose(0, 2, 3, 1, 4)
        .reshape(fsdp_count, part_rows, per_owner * B)
    )
    returned = lax.all_to_all(outgoing, "fsdp", split_axis=0, concat_axis=0, tiled=True)
    ordered = returned.transpose(1, 0, 2).reshape(part_rows, columns, B)
    update = lax.all_gather(
        jnp.take(ordered, row_slots, axis=1).reshape(part_rows, full_width),
        "replica",
        axis=0,
        tiled=True,
    )
    return (
        update,
        left_new.reshape(stats_left.shape),
        right_new.reshape(stats_right.shape),
        moment.reshape(second_moment.shape),
    )


def local(*arrays):
    replicas = lax.axis_size("replica")
    rows, full_width = arrays[0].shape[1:]
    owners = lax.axis_size("fsdp")
    per_owner = full_width // B // owners
    if replicas == 4 and per_owner == replicas and 2 * rows == B and owners == 8:
        return owner_local(*arrays)
    return row_local(*arrays)


def solution(mesh):
    placed = (
        P("replica", "fsdp", None),
        P(),
        P(None, "fsdp", None, "replica", None, None),
        P(None, "fsdp", None, "replica", None, None),
        P(None, "fsdp", None, "replica", None, None),
        P(None, "fsdp", None, "replica", None, None),
        P(None, "fsdp", None, "replica", None, None),
    )
    return jax.shard_map(
        local,
        mesh=mesh,
        in_specs=placed,
        out_specs=(
            P("fsdp", None),
            P(None, "fsdp", None, "replica", None, None),
            P(None, "fsdp", None, "replica", None, None),
            P(None, "fsdp", None, "replica", None, None),
        ),
        check_vma=False,
    )
```

```python
import functools

import jax
import jax.numpy as jnp
from jax import lax
from jax.experimental import pallas as pl
from jax.experimental.pallas import tpu as pltpu
from jax.sharding import PartitionSpec as P

B = 576
LANES = 128
WINDOW = -(-B // LANES) * LANES
VMEM = 64 * 1024 * 1024 - 4096
ANY = pl.BlockSpec(memory_space=pl.ANY)
WHOLE = pl.BlockSpec(memory_space=pltpu.VMEM)
SCALARS = pl.BlockSpec(memory_space=pltpu.SMEM)


def params():
    return pltpu.CompilerParams(vmem_limit_bytes=VMEM)


def cost(flops, moved):
    return pl.CostEstimate(flops=flops, bytes_accessed=moved, transcendentals=0)


def arrange_body(n_add, offsets, n_after, base, halves, cols, grad, *refs):
    adds, refs = refs[: 2 * n_add], refs[2 * n_add + n_after :]
    outs, (buffer, sems) = refs[:-2], refs[-2:]
    n = outs[0].shape[1]
    count = buffer.shape[0]
    half = count // 2

    def copy(i):
        start = pl.multiple_of(cols[i] * B // LANES * LANES, LANES)
        return pltpu.make_async_copy(
            grad.at[pl.ds(base, 2 * n), pl.ds(start, WINDOW)], buffer.at[i], sems.at[i]
        )

    for i in range(count):
        copy(i).start()
    for i in range(count):
        copy(i).wait()
        out, at = (outs[i // half], i % half) if halves else (outs[0], i)
        for shift in (0, B % LANES):

            @pl.when(lax.rem(cols[i] * B, LANES) == shift)
            def _():
                part = buffer[i, :, shift : shift + B]
                out[at, :, :B] = part[:n]
                out[at, :, B:] = part[n:]

        if n_add:
            total = out[at].astype(jnp.float32)
            for k in range(i // half, 2 * n_add, 2):
                total = total + adds[k][offsets[k] + i % half].astype(jnp.float32)
            out[at] = total.astype(out.dtype)


def arrange(cols, grad, base, n, adds=(), halves=True, after=()):
    count = cols.shape[0]
    w = 2 * B
    adds = [part for pair in adds for part in pair]
    shapes = [(count // 2, n, w)] * 2 if halves else [(count, n, w)]
    return pl.pallas_call(
        functools.partial(
            arrange_body, len(adds) // 2, [part[1] for part in adds], len(after), base, halves
        ),
        in_specs=[SCALARS, ANY] + [WHOLE] * len(adds) + [ANY] * len(after),
        out_specs=[WHOLE] * len(shapes),
        out_shape=[jax.ShapeDtypeStruct(s, grad.dtype) for s in shapes],
        scratch_shapes=[
            pltpu.VMEM((count, 2 * n, WINDOW), grad.dtype),
            pltpu.SemaphoreType.DMA((count,)),
        ],
        compiler_params=params(),
        cost_estimate=cost(0, count * n * w * (4 + len(adds))),
    )(cols, grad, *[part[0] for part in adds], *after)


def visit(k, m, p, last):
    return jnp.where(m == k, p, jnp.where(m < k, 0, last))


def pack_roots_body(n, js, left, right, *refs):
    m = pl.program_id(0)
    for k, out in enumerate(refs[-n:]):

        @pl.when(m == k)
        def _():
            for kind, ref in enumerate((left, right)):
                for q in range(2):
                    out[kind, 0, :, q * B : q * B + B] = ref[q, 0]


def pack_roots(js, left, right, after):
    blocks, _, rows, _ = left.shape
    pairs, n, w = blocks // 2, js.shape[0], 2 * B
    source = pl.BlockSpec((2, 1, rows, B), lambda m, p, j: (p, j[m], 0, 0))
    return pl.pallas_call(
        functools.partial(pack_roots_body, n),
        grid_spec=pltpu.PrefetchScalarGridSpec(
            num_scalar_prefetch=1,
            grid=(n, pairs),
            in_specs=[source, source] + [ANY] * len(after),
            out_specs=[
                pl.BlockSpec(
                    (2, 1, rows, w),
                    lambda m, p, j, k=k: (0, visit(k, m, p, pairs - 1), 0, 0),
                )
                for k in range(n)
            ],
        ),
        out_shape=[jax.ShapeDtypeStruct((2, pairs, rows, w), left.dtype)] * n,
        compiler_params=params(),
        cost_estimate=cost(0, 4 * left.size * 2),
    )(js, left, right, *after)


def dot(x, y, dims):
    return lax.dot_general(x, y, (dims, ((), ())), preferred_element_type=jnp.float32)


def assemble(chunks, q, full):
    base = 0
    for chunk in chunks:
        n = chunk.shape[1]
        for h in range(2):
            for side in range(2):
                start = h * (B // 2) + base + side * n
                full[start : start + n, :] = chunk[2 * q + h, :, side * B : side * B + B]
        base += 2 * n


def own_rows(j, h, rd):
    return pl.ds(pl.multiple_of(h * (B // 2) + j * rd, 8), rd)


def gram_body(n, rd, n_chunks, js, *refs):
    chunks, refs = refs[:n_chunks], refs[n_chunks:]
    outs, (g16, g32, l32, r32) = refs[:n], refs[n:]
    for q in range(2):
        assemble(chunks, q, g16)
        g = g16[...]
        g32[...] = g.astype(jnp.float32)
        l32[...] = dot(g, g, ((1,), (1,)))
        r32[...] = dot(g, g, ((0,), (0,)))
        lanes = slice(q * B, q * B + B)
        for k in range(n):
            for kind, full in enumerate((g32, l32, r32)):
                parts = [full[own_rows(js[k], h, rd), :] for h in range(2)]
                outs[k][kind, 0, :, lanes] = jnp.concatenate(parts, axis=0).astype(jnp.bfloat16)


def gram(js, chunks, rd):
    n = js.shape[0]
    count, _, w = chunks[0].shape
    pairs, rows = count // 4, 2 * rd

    return pl.pallas_call(
        functools.partial(gram_body, n, rd, len(chunks)),
        grid_spec=pltpu.PrefetchScalarGridSpec(
            num_scalar_prefetch=1,
            grid=(pairs,),
            in_specs=[
                pl.BlockSpec((4,) + chunk.shape[1:], lambda p, j: (p, 0, 0)) for chunk in chunks
            ],
            out_specs=[pl.BlockSpec((3, 1, rows, w), lambda p, j: (0, p, 0, 0))] * n,
            scratch_shapes=[pltpu.VMEM((B, B), jnp.bfloat16)] + [pltpu.VMEM((B, B), jnp.float32)] * 3,
        ),
        out_shape=[jax.ShapeDtypeStruct((3, pairs, rows, w), jnp.bfloat16)] * n,
        compiler_params=params(),
        cost_estimate=cost(pairs * 8 * B**3, pairs * B * B * 2 * 8),
    )(js, *chunks)


def direct_body(n, rd, n_chunks, n_after, js, place, *refs):
    chunks, roots, refs = refs[:n_chunks], refs[n_chunks : n_chunks + n], refs[n_chunks + n :]
    outs, (square_out, g16, l32, r32, result, sems) = refs[n_after:-6], refs[-6:]
    p = pl.program_id(0)
    f = place[0]
    hr = result.shape[1]

    def send(k):
        return pltpu.make_async_copy(result.at[f ^ k], outs[k], sems.at[k])

    for q in range(2):
        assemble(chunks, q, g16)
        for k in range(n):
            for kind, full in enumerate((l32, r32)):
                part = roots[k][kind, 0, :, q * B : q * B + B].astype(jnp.float32)
                for h in range(2):
                    full[own_rows(js[k], h, rd), :] = part[h * rd : h * rd + rd]
        inner = dot(l32[...].astype(jnp.bfloat16), g16[...], ((1,), (0,))).astype(jnp.bfloat16)
        direction = dot(inner, r32[...].astype(jnp.bfloat16), ((1,), (0,)))
        square_out[0, q : q + 1, :] = jnp.full((1, LANES), jnp.sum(direction * direction))
        direction = direction.astype(jnp.bfloat16)
        for h in range(2):
            for side in range(2):
                start = h * (B // 2) + side * hr
                result[4 * p + 2 * q + h, :, side * B : side * B + B] = direction[start : start + hr]
    for k in range(len(outs)):

        @pl.when((f ^ k) // 4 == p)
        def _():
            send(k).start()

    @pl.when(p == pl.num_programs(0) - 1)
    def _():
        for k in range(len(outs)):
            send(k).wait()


def direct(js, place, chunks, roots, rd, after):
    n = js.shape[0]
    owners, _, w = chunks[0].shape
    hr = sum(chunk.shape[1] for chunk in chunks)
    pairs, rows = roots[0].shape[1], roots[0].shape[2]
    return pl.pallas_call(
        functools.partial(direct_body, n, rd, len(chunks), len(after)),
        grid_spec=pltpu.PrefetchScalarGridSpec(
            num_scalar_prefetch=2,
            grid=(pairs,),
            in_specs=[pl.BlockSpec((4,) + chunk.shape[1:], lambda p, j, f: (p, 0, 0)) for chunk in chunks]
            + [pl.BlockSpec((2, 1, rows, w), lambda p, j, f: (0, p, 0, 0))] * n
            + [ANY] * len(after),
            out_specs=[ANY] * owners + [pl.BlockSpec((1, 8, LANES), lambda p, j, f: (p, 0, 0))],
            scratch_shapes=[pltpu.VMEM((B, B), jnp.bfloat16)]
            + [pltpu.VMEM((B, B), jnp.float32)] * 2
            + [pltpu.VMEM((owners, hr, w), jnp.bfloat16), pltpu.SemaphoreType.DMA((owners,))],
        ),
        out_shape=[jax.ShapeDtypeStruct((hr, w), jnp.bfloat16)] * owners
        + [jax.ShapeDtypeStruct((pairs, 8, LANES), jnp.float32)],
        compiler_params=params(),
        cost_estimate=cost(pairs * 8 * B**3, pairs * B * B * 2 * 8),
    )(js, place, *chunks, *roots, *after)


def follow(arrays, after):
    return pl.pallas_call(
        lambda *refs: None,
        in_specs=[ANY] * (len(arrays) + len(after)),
        out_specs=[ANY] * len(arrays),
        out_shape=[jax.ShapeDtypeStruct(x.shape, x.dtype) for x in arrays],
        input_output_aliases={k: k for k in range(len(arrays))},
        compiler_params=params(),
        cost_estimate=cost(0, 0),
    )(*arrays, *after)


def collect_body(count, n_through, *refs):
    parts, half = refs[:count], count // 2
    low, high = refs[count + n_through : count + n_through + 2]
    buffer, in_sems, out_sems = refs[-3:]

    def arrive(k):
        return pltpu.make_async_copy(parts[k], buffer.at[k], in_sems.at[k])

    def leave(k):
        return pltpu.make_async_copy(
            buffer.at[k], (low, high)[k // half].at[k % half], out_sems.at[k]
        )

    for k in range(len(parts)):
        arrive(k).start()
    for k in range(len(parts)):
        arrive(k).wait()
        leave(k).start()
    for k in range(len(parts)):
        leave(k).wait()


def collect(parts, through):
    count = len(parts)
    halves = jax.ShapeDtypeStruct((count // 2,) + parts[0].shape, parts[0].dtype)
    return pl.pallas_call(
        functools.partial(collect_body, count, len(through)),
        in_specs=[ANY] * (count + len(through)),
        out_specs=[ANY] * (2 + len(through)),
        out_shape=[halves] * 2 + [jax.ShapeDtypeStruct(x.shape, x.dtype) for x in through],
        scratch_shapes=[pltpu.VMEM((count,) + parts[0].shape, parts[0].dtype)]
        + [pltpu.SemaphoreType.DMA((count,))] * 2,
        input_output_aliases={count + k: 2 + k for k in range(len(through))},
        compiler_params=params(),
        cost_estimate=cost(0, 2 * count * parts[0].size * 2),
    )(*parts, *through)


def moment_body(q, received, moment, moment_out, square_out):
    g = received[0, 0, :, q * B : q * B + B].astype(jnp.float32)
    second = 0.95 * moment[q, 0] + 0.05 * g * g
    moment_out[q, 0] = second
    adam = g / (jnp.sqrt(second) + 1e-08)
    square_out[0, 0, q : q + 1, :] = jnp.full((1, LANES), jnp.sum(adam * adam))


def gram_update_body(q, received, left, right, left_out, right_out):
    for kind, old, new in ((1, left, left_out), (2, right, right_out)):
        product = received[kind, 0, :, q * B : q * B + B].astype(jnp.float32)
        new[q, 0] = 0.95 * old[q, 0] + 0.05 * product


def by_rows_body(body, n, js, *refs):
    m = pl.program_id(0)
    for k in range(n):

        @pl.when(m == k)
        def _():
            for q in range(2):
                body(q, refs[k], *refs[n:])


def by_rows(body, kinds, js, received, olds, squares):
    n = js.shape[0]
    blocks, _, rows, _ = olds[0].shape
    pairs, w = received[0].shape[1], received[0].shape[3]
    own = pl.BlockSpec((2, 1, rows, B), lambda m, p, j: (p, j[m], 0, 0))
    out_specs = [own] * len(olds)
    out_shape = [jax.ShapeDtypeStruct(old.shape, jnp.float32) for old in olds]
    if squares:
        out_specs.append(pl.BlockSpec((1, 1, 8, LANES), lambda m, p, j: (m, p, 0, 0)))
        out_shape.append(jax.ShapeDtypeStruct((n, pairs, 8, LANES), jnp.float32))
    return pl.pallas_call(
        functools.partial(by_rows_body, body, n),
        grid_spec=pltpu.PrefetchScalarGridSpec(
            num_scalar_prefetch=1,
            grid=(n, pairs),
            in_specs=[
                pl.BlockSpec(
                    (kinds, 1, rows, w),
                    lambda m, p, j, k=k: (0, visit(k, m, p, pairs - 1), 0, 0),
                )
                for k in range(n)
            ]
            + [own] * len(olds),
            out_specs=out_specs,
        ),
        out_shape=out_shape,
        compiler_params=params(),
        cost_estimate=cost(0, olds[0].size * 10 * len(olds)),
    )(js, *received, *olds)


def restore_body(src, item, scale, *refs):
    sources, (out, buffer, result, in_sems, out_sems) = refs[:-5], refs[-5:]
    columns, n, w = buffer.shape
    slots = result.shape[0]

    def fetch(c, _):
        for k, source in enumerate(sources):

            @pl.when(src[c] == k)
            def _():
                pltpu.make_async_copy(source.at[item[c]], buffer.at[c], in_sems.at[c]).start()

        return 0

    def store(p, slot):
        start = pl.multiple_of(p * w, LANES)
        return pltpu.make_async_copy(
            result.at[slot], out.at[:, pl.ds(start, w)], out_sems.at[slot]
        )

    def step(p, _):
        slot = lax.rem(p, slots)

        @pl.when(p >= slots)
        def _():
            store(p - slots, slot).wait()

        for e in range(2):
            c = 2 * p + e
            pltpu.make_async_copy(sources[0].at[0], buffer.at[c], in_sems.at[c]).wait()
            scaled = (buffer[c].astype(jnp.float32) * scale[c]).astype(result.dtype)
            result[slot, :n, e * B : e * B + B] = scaled[:, :B]
            result[slot, n:, e * B : e * B + B] = scaled[:, B:]
        store(p, slot).start()
        return 0

    pairs = columns // 2
    lax.fori_loop(0, columns, fetch, 0)
    lax.fori_loop(0, pairs, step, 0)
    for p in range(pairs - slots, pairs):
        store(p, p % slots).wait()


def restore(src, item, scale, sources):
    columns = src.shape[0]
    _, n, w = sources[0].shape
    slots = 4
    return pl.pallas_call(
        restore_body,
        in_specs=[SCALARS] * 3 + [ANY] * len(sources),
        out_specs=ANY,
        out_shape=jax.ShapeDtypeStruct((2 * n, columns * B), jnp.bfloat16),
        scratch_shapes=[
            pltpu.VMEM((columns, n, w), jnp.bfloat16),
            pltpu.VMEM((slots, 2 * n, w), jnp.bfloat16),
            pltpu.SemaphoreType.DMA((columns,)),
            pltpu.SemaphoreType.DMA((slots,)),
        ],
        compiler_params=params(),
        cost_estimate=cost(0, columns * n * w * 4),
    )(src, item, scale, *sources)


def owner_local(grads, slots, stats_left, stats_right, root_left, root_right, second_moment):
    owners = lax.axis_size("fsdp")
    replicas = lax.axis_size("replica")
    grad = grads[0]
    rows, full_width = grad.shape
    columns = full_width // B
    row_blocks = slots.shape[0]
    sub_count = B // rows
    rd = rows // replicas
    half = owners // 2
    f = lax.axis_index("fsdp")
    r = lax.axis_index("replica")
    js = r ^ jnp.arange(replicas, dtype=jnp.int32)
    row_slots = lax.dynamic_index_in_dim(slots, f // sub_count, 0, keepdims=False)
    column_ids = jnp.arange(columns, dtype=jnp.int32)
    owner_ids = jnp.arange(owners, dtype=jnp.int32)
    halves = (owner_ids[:half], owner_ids[half:])
    wanted = jnp.stack(
        [
            replicas * jnp.concatenate([halves[low], halves[high]])
            + (r ^ jnp.where(owner_ids < half, low_step, high_step))
            for low, low_step, high, high_step in ((0, 3, 0, 1), (1, 3, 1, 2), (0, 2, 1, 1), (0, 0, 1, 0))
        ]
    )
    cols = jnp.sum(jnp.where(row_slots == wanted[:, :, None], column_ids, 0), axis=2)

    def swap(x, k):
        return lax.ppermute(x, "replica", [(i, i ^ k) for i in range(replicas)])

    def as_rows(x):
        return x.reshape(row_blocks, -1, sub_count * rd, B)

    first = rows // 64 * 16
    chunks = ((0, first), (2 * first, rows // 2 - first))
    after, early, blocks = (), [], []
    for chunk in chunks:
        x, y = arrange(cols[:2].reshape(-1), grad, *chunk, after=after)
        early.append((swap(x, 1), swap(y, 2)))
        after = (x,)
    roots = pack_roots(js, as_rows(root_left), as_rows(root_right), after)
    after = (roots[0],)
    for (x, y), chunk in zip(early, chunks):
        y_a, x_b = arrange(cols[2], grad, *chunk, [((x, 0), (y, 0))], after=after)
        terms = [((x, half), (y, half)), ((swap(y_a, 2), 0), (swap(x_b, 1), 0))]
        (owned,) = arrange(cols[3], grad, *chunk, terms, halves=False)
        blocks.append(lax.all_to_all(owned, "fsdp", split_axis=0, concat_axis=0, tiled=True))
        after = (owned,)
    sent = follow(roots[1:], after)
    roots = [roots[0]] + [swap(x, k) for k, x in zip((1, 2, 3), sent)]

    place = f.reshape(1)
    products = gram(js, blocks, rd)
    received = [products[0]] + [swap(products[k], k) for k in (1, 2, 3)]
    *direction, direction_square = direct(js, place, blocks, roots, rd, (products[0],))
    direction[1:] = [
        lax.ppermute(direction[k], "fsdp", [(i, i ^ k) for i in range(owners)])
        for k in range(1, owners)
    ]
    a, b, *received[1:] = collect(direction, received[1:])

    x_a, y_b, x_b, y_a = swap(a, 1), swap(b, 2), swap(b, 1), swap(a, 2)

    moment, adam_square = by_rows(
        moment_body, 1, js, received, [as_rows(second_moment)], True
    )
    adam_square = adam_square[:, :, :2, 0].reshape(replicas, row_blocks)
    slot_ids = jnp.arange(replicas, dtype=jnp.int32)
    adam_square = jnp.sum(
        jnp.where((js[:, None] == slot_ids)[:, :, None], adam_square[:, None, :], 0.0), axis=0
    )
    direction_square = direction_square[:, :2, 0].reshape(row_blocks)
    slot_place = (slot_ids == r)[:, None]
    squares = jnp.stack([adam_square, jnp.where(slot_place, direction_square, 0.0)])
    squares = lax.psum(squares, "replica")
    squares = lax.psum(jnp.where(owner_ids[:, None, None, None] == f, squares, 0.0), "fsdp")
    ratio = jnp.sqrt(squares[:, 0]) / jnp.sqrt(squares[:, 1] + 1e-06)
    row_ratio = lax.dynamic_index_in_dim(
        ratio.reshape(columns, row_blocks), f // sub_count, 1, keepdims=False
    )
    scale = jnp.sum(jnp.where(row_slots[:, None] == column_ids, row_ratio, 0.0), axis=1)

    x_a, y_b = follow((x_a, y_b), (scale, x_b, y_a))
    left_new, right_new = by_rows(
        gram_update_body, 3, js, received, [as_rows(stats_left), as_rows(stats_right)], False
    )
    part = (row_slots // replicas) ^ f
    src = 2 * (lax.rem(row_slots, replicas) ^ r) + part // half
    gathered = (a, b, x_a, x_b, y_a, y_b, swap(x_a, 2), swap(y_b, 1))
    update = restore(src, lax.rem(part, half), scale, gathered)
    return (
        update,
        left_new.reshape(stats_left.shape),
        right_new.reshape(stats_right.shape),
        moment.reshape(second_moment.shape),
    )


def slot_columns(row_slots, row_count):
    column_ids = jnp.arange(row_count, dtype=jnp.int32)
    matches = row_slots[None, :] == column_ids[:, None]
    return jnp.sum(jnp.where(matches, column_ids[None, :], 0), axis=1)


def row_local(grads, slots, stats_left, stats_right, root_left, root_right, second_moment):
    fsdp_count = lax.axis_size("fsdp")
    replica_count = lax.axis_size("replica")
    local_grad = grads[0]
    shard_rows, full_width = local_grad.shape
    columns = full_width // B
    row_blocks = slots.shape[0]
    per_owner = columns // fsdp_count
    sub_count = B // shard_rows
    part_rows = shard_rows // replica_count
    mine_rows = sub_count * part_rows
    fsdp_index = lax.axis_index("fsdp")
    replica_index = lax.axis_index("replica")
    row_slots = lax.dynamic_index_in_dim(slots, fsdp_index // sub_count, 0, keepdims=False)
    slot_cols = slot_columns(row_slots, columns)
    summed = lax.psum_scatter(
        local_grad.astype(jnp.float32).astype(jnp.bfloat16),
        "replica",
        scatter_dimension=0,
        tiled=True,
    )
    row_count = summed.shape[0]
    ordered = jnp.take(summed.reshape(row_count, columns, B), slot_cols, axis=1)
    arrived = lax.all_to_all(
        ordered.reshape(row_count, fsdp_count, per_owner * B).transpose(1, 0, 2),
        "fsdp",
        split_axis=0,
        concat_axis=0,
        tiled=True,
    )
    own_split = arrived.reshape(row_blocks, sub_count, part_rows, per_owner, B).transpose(
        0, 3, 1, 2, 4
    )
    gathered = lax.all_gather(own_split[:, :, :, None], "replica", axis=3, tiled=True)
    full_grad = gathered.reshape(row_blocks, per_owner, B, B)
    own_rows = own_split.reshape(row_blocks, per_owner, mine_rows, B)

    def as_rows(array_in):
        return array_in.reshape(row_blocks, per_owner, mine_rows, B)

    column_split = full_grad.reshape(row_blocks, per_owner, B, sub_count, replica_count, part_rows)
    column_part = lax.dynamic_index_in_dim(column_split, replica_index, 4, keepdims=False).reshape(
        row_blocks, per_owner, B, mine_rows
    )
    left_gram = jnp.einsum(
        "abmk,abnk->abmn", own_rows, full_grad, preferred_element_type=jnp.float32
    )
    right_gram = jnp.einsum(
        "abkm,abkn->abmn", column_part, full_grad, preferred_element_type=jnp.float32
    )
    left_new = 0.95 * as_rows(stats_left) + 0.05 * left_gram
    right_new = 0.95 * as_rows(stats_right) + 0.05 * right_gram
    right_full = lax.all_gather(root_right, "replica", axis=3, tiled=True).reshape(
        row_blocks, per_owner, B, B
    )
    inner_left = jnp.einsum(
        "abmk,abkn->abmn", as_rows(root_left), full_grad, preferred_element_type=jnp.float32
    ).astype(jnp.bfloat16)
    direction = jnp.einsum(
        "abmk,abkn->abmn", inner_left, right_full, preferred_element_type=jnp.float32
    )
    grad_float = own_rows.astype(jnp.float32)
    moment = 0.95 * as_rows(second_moment) + 0.05 * grad_float * grad_float
    adam_step = grad_float / (jnp.sqrt(moment) + 1e-08)
    adam_square, shampoo_square = lax.psum(
        (jnp.sum(adam_step * adam_step, axis=(2, 3)), jnp.sum(direction * direction, axis=(2, 3))),
        "replica",
    )
    graft_scale = jnp.sqrt(adam_square) / jnp.sqrt(shampoo_square + 1e-06)
    update_part = (direction * graft_scale[:, :, None, None]).astype(jnp.bfloat16)
    outgoing = (
        update_part.reshape(row_blocks, per_owner, sub_count, part_rows, B)
        .transpose(0, 2, 3, 1, 4)
        .reshape(fsdp_count, part_rows, per_owner * B)
    )
    returned = lax.all_to_all(outgoing, "fsdp", split_axis=0, concat_axis=0, tiled=True)
    ordered = returned.transpose(1, 0, 2).reshape(part_rows, columns, B)
    update = lax.all_gather(
        jnp.take(ordered, row_slots, axis=1).reshape(part_rows, full_width),
        "replica",
        axis=0,
        tiled=True,
    )
    return (
        update,
        left_new.reshape(stats_left.shape),
        right_new.reshape(stats_right.shape),
        moment.reshape(second_moment.shape),
    )


def local(*arrays):
    replicas = lax.axis_size("replica")
    rows, full_width = arrays[0].shape[1:]
    owners = lax.axis_size("fsdp")
    per_owner = full_width // B // owners
    if replicas == 4 and per_owner == replicas and 2 * rows == B and owners == 8:
        return owner_local(*arrays)
    return row_local(*arrays)


def solution(mesh):
    placed = (
        P("replica", "fsdp", None),
        P(),
        P(None, "fsdp", None, "replica", None, None),
        P(None, "fsdp", None, "replica", None, None),
        P(None, "fsdp", None, "replica", None, None),
        P(None, "fsdp", None, "replica", None, None),
        P(None, "fsdp", None, "replica", None, None),
    )
    return jax.shard_map(
        local,
        mesh=mesh,
        in_specs=placed,
        out_specs=(
            P("fsdp", None),
            P(None, "fsdp", None, "replica", None, None),
            P(None, "fsdp", None, "replica", None, None),
            P(None, "fsdp", None, "replica", None, None),
        ),
        check_vma=False,
    )
```

```python
import functools

import jax
import jax.numpy as jnp
from jax import lax
from jax.experimental import pallas as pl
from jax.experimental.pallas import tpu as pltpu
from jax.sharding import PartitionSpec as P

B = 576
LANES = 128
WINDOW = -(-B // LANES) * LANES
VMEM = 64 * 1024 * 1024 - 4096
ANY = pl.BlockSpec(memory_space=pl.ANY)
WHOLE = pl.BlockSpec(memory_space=pltpu.VMEM)
SCALARS = pl.BlockSpec(memory_space=pltpu.SMEM)


def params():
    return pltpu.CompilerParams(vmem_limit_bytes=VMEM)


def cost(flops, moved):
    return pl.CostEstimate(flops=flops, bytes_accessed=moved, transcendentals=0)


def arrange_body(n_add, offsets, n_after, base, halves, cols, grad, *refs):
    adds, refs = refs[: 2 * n_add], refs[2 * n_add + n_after :]
    outs, (buffer, sems) = refs[:-2], refs[-2:]
    n = outs[0].shape[1]
    count = buffer.shape[0]
    half = count // 2

    def copy(i):
        start = pl.multiple_of(cols[i] * B // LANES * LANES, LANES)
        return pltpu.make_async_copy(
            grad.at[pl.ds(base, 2 * n), pl.ds(start, WINDOW)], buffer.at[i], sems.at[i]
        )

    for i in range(count):
        copy(i).start()
    for i in range(count):
        copy(i).wait()
        out, at = (outs[i // half], i % half) if halves else (outs[0], i)
        for shift in (0, B % LANES):

            @pl.when(lax.rem(cols[i] * B, LANES) == shift)
            def _():
                part = buffer[i, :, shift : shift + B]
                out[at, :, :B] = part[:n]
                out[at, :, B:] = part[n:]

        if n_add:
            total = out[at].astype(jnp.float32)
            for k in range(i // half, 2 * n_add, 2):
                total = total + adds[k][offsets[k] + i % half].astype(jnp.float32)
            out[at] = total.astype(out.dtype)


def arrange(cols, grad, base, n, adds=(), halves=True, after=()):
    count = cols.shape[0]
    w = 2 * B
    adds = [part for pair in adds for part in pair]
    shapes = [(count // 2, n, w)] * 2 if halves else [(count, n, w)]
    return pl.pallas_call(
        functools.partial(
            arrange_body, len(adds) // 2, [part[1] for part in adds], len(after), base, halves
        ),
        in_specs=[SCALARS, ANY] + [WHOLE] * len(adds) + [ANY] * len(after),
        out_specs=[WHOLE] * len(shapes),
        out_shape=[jax.ShapeDtypeStruct(s, grad.dtype) for s in shapes],
        scratch_shapes=[
            pltpu.VMEM((count, 2 * n, WINDOW), grad.dtype),
            pltpu.SemaphoreType.DMA((count,)),
        ],
        compiler_params=params(),
        cost_estimate=cost(0, count * n * w * (4 + len(adds))),
    )(cols, grad, *[part[0] for part in adds], *after)


def visit(k, m, p, last):
    return jnp.where(m == k, p, jnp.where(m < k, 0, last))


def pack_roots_body(n, js, left, right, *refs):
    m = pl.program_id(0)
    for k, out in enumerate(refs[-n:]):

        @pl.when(m == k)
        def _():
            for kind, ref in enumerate((left, right)):
                for q in range(2):
                    out[kind, 0, :, q * B : q * B + B] = ref[q, 0]


def pack_roots(js, left, right, after):
    blocks, _, rows, _ = left.shape
    pairs, n, w = blocks // 2, js.shape[0], 2 * B
    source = pl.BlockSpec((2, 1, rows, B), lambda m, p, j: (p, j[m], 0, 0))
    return pl.pallas_call(
        functools.partial(pack_roots_body, n),
        grid_spec=pltpu.PrefetchScalarGridSpec(
            num_scalar_prefetch=1,
            grid=(n, pairs),
            in_specs=[source, source] + [ANY] * len(after),
            out_specs=[
                pl.BlockSpec(
                    (2, 1, rows, w),
                    lambda m, p, j, k=k: (0, visit(k, m, p, pairs - 1), 0, 0),
                )
                for k in range(n)
            ],
        ),
        out_shape=[jax.ShapeDtypeStruct((2, pairs, rows, w), left.dtype)] * n,
        compiler_params=params(),
        cost_estimate=cost(0, 4 * left.size * 2),
    )(js, left, right, *after)


def dot(x, y, dims):
    return lax.dot_general(x, y, (dims, ((), ())), preferred_element_type=jnp.float32)


def assemble(chunks, q, full):
    base = 0
    for chunk in chunks:
        n = chunk.shape[1]
        for h in range(2):
            for side in range(2):
                start = h * (B // 2) + base + side * n
                full[start : start + n, :] = chunk[2 * q + h, :, side * B : side * B + B]
        base += 2 * n


def own_rows(j, h, rd):
    return pl.ds(pl.multiple_of(h * (B // 2) + j * rd, 8), rd)


def gram_body(n, rd, n_chunks, js, *refs):
    chunks, refs = refs[:n_chunks], refs[n_chunks:]
    outs, (g16, g32, l32, r32) = refs[:n], refs[n:]
    for q in range(2):
        assemble(chunks, q, g16)
        g = g16[...]
        g32[...] = g.astype(jnp.float32)
        l32[...] = dot(g, g, ((1,), (1,)))
        r32[...] = dot(g, g, ((0,), (0,)))
        lanes = slice(q * B, q * B + B)
        for k in range(n):
            for kind, full in enumerate((g32, l32, r32)):
                parts = [full[own_rows(js[k], h, rd), :] for h in range(2)]
                outs[k][kind, 0, :, lanes] = jnp.concatenate(parts, axis=0).astype(jnp.bfloat16)


def gram(js, chunks, rd):
    n = js.shape[0]
    count, _, w = chunks[0].shape
    pairs, rows = count // 4, 2 * rd

    return pl.pallas_call(
        functools.partial(gram_body, n, rd, len(chunks)),
        grid_spec=pltpu.PrefetchScalarGridSpec(
            num_scalar_prefetch=1,
            grid=(pairs,),
            in_specs=[
                pl.BlockSpec((4,) + chunk.shape[1:], lambda p, j: (p, 0, 0)) for chunk in chunks
            ],
            out_specs=[pl.BlockSpec((3, 1, rows, w), lambda p, j: (0, p, 0, 0))] * n,
            scratch_shapes=[pltpu.VMEM((B, B), jnp.bfloat16)] + [pltpu.VMEM((B, B), jnp.float32)] * 3,
        ),
        out_shape=[jax.ShapeDtypeStruct((3, pairs, rows, w), jnp.bfloat16)] * n,
        compiler_params=params(),
        cost_estimate=cost(pairs * 8 * B**3, pairs * B * B * 2 * 8),
    )(js, *chunks)


def direct_body(n, rd, n_chunks, n_after, js, place, *refs):
    chunks, roots, refs = refs[:n_chunks], refs[n_chunks : n_chunks + n], refs[n_chunks + n :]
    outs, (square_out, g16, l32, r32, result, sems) = refs[n_after:-6], refs[-6:]
    p = pl.program_id(0)
    f = place[0]
    hr = result.shape[1]

    def send(k):
        return pltpu.make_async_copy(result.at[f ^ k], outs[k], sems.at[k])

    for q in range(2):
        assemble(chunks, q, g16)
        for k in range(n):
            for kind, full in enumerate((l32, r32)):
                part = roots[k][kind, 0, :, q * B : q * B + B].astype(jnp.float32)
                for h in range(2):
                    full[own_rows(js[k], h, rd), :] = part[h * rd : h * rd + rd]
        inner = dot(l32[...].astype(jnp.bfloat16), g16[...], ((1,), (0,))).astype(jnp.bfloat16)
        direction = dot(inner, r32[...].astype(jnp.bfloat16), ((1,), (0,)))
        square_out[0, q : q + 1, :] = jnp.full((1, LANES), jnp.sum(direction * direction))
        direction = direction.astype(jnp.bfloat16)
        for h in range(2):
            for side in range(2):
                start = h * (B // 2) + side * hr
                result[4 * p + 2 * q + h, :, side * B : side * B + B] = direction[start : start + hr]
    for k in range(len(outs)):

        @pl.when((f ^ k) // 4 == p)
        def _():
            send(k).start()

    @pl.when(p == pl.num_programs(0) - 1)
    def _():
        for k in range(len(outs)):
            send(k).wait()


def direct(js, place, chunks, roots, rd, after):
    n = js.shape[0]
    owners, _, w = chunks[0].shape
    hr = sum(chunk.shape[1] for chunk in chunks)
    pairs, rows = roots[0].shape[1], roots[0].shape[2]
    return pl.pallas_call(
        functools.partial(direct_body, n, rd, len(chunks), len(after)),
        grid_spec=pltpu.PrefetchScalarGridSpec(
            num_scalar_prefetch=2,
            grid=(pairs,),
            in_specs=[pl.BlockSpec((4,) + chunk.shape[1:], lambda p, j, f: (p, 0, 0)) for chunk in chunks]
            + [pl.BlockSpec((2, 1, rows, w), lambda p, j, f: (0, p, 0, 0))] * n
            + [ANY] * len(after),
            out_specs=[ANY] * owners + [pl.BlockSpec((1, 8, LANES), lambda p, j, f: (p, 0, 0))],
            scratch_shapes=[pltpu.VMEM((B, B), jnp.bfloat16)]
            + [pltpu.VMEM((B, B), jnp.float32)] * 2
            + [pltpu.VMEM((owners, hr, w), jnp.bfloat16), pltpu.SemaphoreType.DMA((owners,))],
        ),
        out_shape=[jax.ShapeDtypeStruct((hr, w), jnp.bfloat16)] * owners
        + [jax.ShapeDtypeStruct((pairs, 8, LANES), jnp.float32)],
        compiler_params=params(),
        cost_estimate=cost(pairs * 8 * B**3, pairs * B * B * 2 * 8),
    )(js, place, *chunks, *roots, *after)


def follow(arrays, after):
    return pl.pallas_call(
        lambda *refs: None,
        in_specs=[ANY] * (len(arrays) + len(after)),
        out_specs=[ANY] * len(arrays),
        out_shape=[jax.ShapeDtypeStruct(x.shape, x.dtype) for x in arrays],
        input_output_aliases={k: k for k in range(len(arrays))},
        compiler_params=params(),
        cost_estimate=cost(0, 0),
    )(*arrays, *after)


def collect_body(count, n_through, *refs):
    parts, half = refs[:count], count // 2
    low, high = refs[count + n_through : count + n_through + 2]
    buffer, in_sems, out_sems = refs[-3:]

    def arrive(k):
        return pltpu.make_async_copy(parts[k], buffer.at[k], in_sems.at[k])

    def leave(k):
        return pltpu.make_async_copy(
            buffer.at[k], (low, high)[k // half].at[k % half], out_sems.at[k]
        )

    for k in range(len(parts)):
        arrive(k).start()
    for k in range(len(parts)):
        arrive(k).wait()
        leave(k).start()
    for k in range(len(parts)):
        leave(k).wait()


def collect(parts, through):
    count = len(parts)
    halves = jax.ShapeDtypeStruct((count // 2,) + parts[0].shape, parts[0].dtype)
    return pl.pallas_call(
        functools.partial(collect_body, count, len(through)),
        in_specs=[ANY] * (count + len(through)),
        out_specs=[ANY] * (2 + len(through)),
        out_shape=[halves] * 2 + [jax.ShapeDtypeStruct(x.shape, x.dtype) for x in through],
        scratch_shapes=[pltpu.VMEM((count,) + parts[0].shape, parts[0].dtype)]
        + [pltpu.SemaphoreType.DMA((count,))] * 2,
        input_output_aliases={count + k: 2 + k for k in range(len(through))},
        compiler_params=params(),
        cost_estimate=cost(0, 2 * count * parts[0].size * 2),
    )(*parts, *through)


def moment_body(q, received, moment, moment_out, square_out):
    g = received[0, 0, :, q * B : q * B + B].astype(jnp.float32)
    second = 0.95 * moment[q, 0] + 0.05 * g * g
    moment_out[q, 0] = second
    adam = g / (jnp.sqrt(second) + 1e-08)
    square_out[0, 0, q : q + 1, :] = jnp.full((1, LANES), jnp.sum(adam * adam))


def gram_update_body(q, received, left, right, left_out, right_out):
    for kind, old, new in ((1, left, left_out), (2, right, right_out)):
        product = received[kind, 0, :, q * B : q * B + B].astype(jnp.float32)
        new[q, 0] = 0.95 * old[q, 0] + 0.05 * product


def by_rows_body(body, n, js, *refs):
    m = pl.program_id(0)
    for k in range(n):

        @pl.when(m == k)
        def _():
            for q in range(2):
                body(q, refs[k], *refs[n:])


def by_rows(body, kinds, js, received, olds, squares):
    n = js.shape[0]
    blocks, _, rows, _ = olds[0].shape
    pairs, w = received[0].shape[1], received[0].shape[3]
    own = pl.BlockSpec((2, 1, rows, B), lambda m, p, j: (p, j[m], 0, 0))
    out_specs = [own] * len(olds)
    out_shape = [jax.ShapeDtypeStruct(old.shape, jnp.float32) for old in olds]
    if squares:
        out_specs.append(pl.BlockSpec((1, 1, 8, LANES), lambda m, p, j: (m, p, 0, 0)))
        out_shape.append(jax.ShapeDtypeStruct((n, pairs, 8, LANES), jnp.float32))
    return pl.pallas_call(
        functools.partial(by_rows_body, body, n),
        grid_spec=pltpu.PrefetchScalarGridSpec(
            num_scalar_prefetch=1,
            grid=(n, pairs),
            in_specs=[
                pl.BlockSpec(
                    (kinds, 1, rows, w),
                    lambda m, p, j, k=k: (0, visit(k, m, p, pairs - 1), 0, 0),
                )
                for k in range(n)
            ]
            + [own] * len(olds),
            out_specs=out_specs,
        ),
        out_shape=out_shape,
        compiler_params=params(),
        cost_estimate=cost(0, olds[0].size * 10 * len(olds)),
    )(js, *received, *olds)


def restore_body(src, item, scale, *refs):
    sources, (out, buffer, result, in_sems, out_sems) = refs[:-5], refs[-5:]
    columns, n, w = buffer.shape
    slots = result.shape[0]

    def fetch(c, _):
        for k, source in enumerate(sources):

            @pl.when(src[c] == k)
            def _():
                pltpu.make_async_copy(source.at[item[c]], buffer.at[c], in_sems.at[c]).start()

        return 0

    def store(p, slot):
        start = pl.multiple_of(p * w, LANES)
        return pltpu.make_async_copy(
            result.at[slot], out.at[:, pl.ds(start, w)], out_sems.at[slot]
        )

    def step(p, _):
        slot = lax.rem(p, slots)

        @pl.when(p >= slots)
        def _():
            store(p - slots, slot).wait()

        for e in range(2):
            c = 2 * p + e
            pltpu.make_async_copy(sources[0].at[0], buffer.at[c], in_sems.at[c]).wait()
            scaled = (buffer[c].astype(jnp.float32) * scale[c]).astype(result.dtype)
            result[slot, :n, e * B : e * B + B] = scaled[:, :B]
            result[slot, n:, e * B : e * B + B] = scaled[:, B:]
        store(p, slot).start()
        return 0

    pairs = columns // 2
    lax.fori_loop(0, columns, fetch, 0)
    lax.fori_loop(0, pairs, step, 0)
    for p in range(pairs - slots, pairs):
        store(p, p % slots).wait()


def restore(src, item, scale, sources):
    columns = src.shape[0]
    _, n, w = sources[0].shape
    slots = 4
    return pl.pallas_call(
        restore_body,
        in_specs=[SCALARS] * 3 + [ANY] * len(sources),
        out_specs=ANY,
        out_shape=jax.ShapeDtypeStruct((2 * n, columns * B), jnp.bfloat16),
        scratch_shapes=[
            pltpu.VMEM((columns, n, w), jnp.bfloat16),
            pltpu.VMEM((slots, 2 * n, w), jnp.bfloat16),
            pltpu.SemaphoreType.DMA((columns,)),
            pltpu.SemaphoreType.DMA((slots,)),
        ],
        compiler_params=params(),
        cost_estimate=cost(0, columns * n * w * 4),
    )(src, item, scale, *sources)


def owner_local(grads, slots, stats_left, stats_right, root_left, root_right, second_moment):
    owners = lax.axis_size("fsdp")
    replicas = lax.axis_size("replica")
    grad = grads[0]
    rows, full_width = grad.shape
    columns = full_width // B
    row_blocks = slots.shape[0]
    sub_count = B // rows
    rd = rows // replicas
    half = owners // 2
    f = lax.axis_index("fsdp")
    r = lax.axis_index("replica")
    js = r ^ jnp.arange(replicas, dtype=jnp.int32)
    row_slots = lax.dynamic_index_in_dim(slots, f // sub_count, 0, keepdims=False)
    column_ids = jnp.arange(columns, dtype=jnp.int32)
    owner_ids = jnp.arange(owners, dtype=jnp.int32)
    halves = (owner_ids[:half], owner_ids[half:])
    wanted = jnp.stack(
        [
            replicas * jnp.concatenate([halves[low], halves[high]])
            + (r ^ jnp.where(owner_ids < half, low_step, high_step))
            for low, low_step, high, high_step in ((0, 3, 0, 1), (1, 3, 1, 2), (0, 2, 1, 1), (0, 0, 1, 0))
        ]
    )
    cols = jnp.sum(jnp.where(row_slots == wanted[:, :, None], column_ids, 0), axis=2)

    def swap(x, k):
        return lax.ppermute(x, "replica", [(i, i ^ k) for i in range(replicas)])

    def as_rows(x):
        return x.reshape(row_blocks, -1, sub_count * rd, B)

    first = -(-rows // 64) * 16
    chunks = ((0, first), (2 * first, rows // 2 - first))
    after, early, blocks = (), [], []
    for chunk in chunks:
        x, y = arrange(cols[:2].reshape(-1), grad, *chunk, after=after)
        early.append((swap(x, 1), swap(y, 2)))
        after = (x,)
    roots = pack_roots(js, as_rows(root_left), as_rows(root_right), after)
    after = (roots[0],)
    for (x, y), chunk in zip(early, chunks):
        y_a, x_b = arrange(cols[2], grad, *chunk, [((x, 0), (y, 0))], after=after)
        terms = [((x, half), (y, half)), ((swap(y_a, 2), 0), (swap(x_b, 1), 0))]
        (owned,) = arrange(cols[3], grad, *chunk, terms, halves=False)
        blocks.append(lax.all_to_all(owned, "fsdp", split_axis=0, concat_axis=0, tiled=True))
        after = (owned,)
    sent = follow(roots[1:], (y_a,))
    roots = [roots[0]] + [swap(x, k) for k, x in zip((1, 2, 3), sent)]

    place = f.reshape(1)
    products = gram(js, blocks, rd)
    received = [products[0]] + [swap(products[k], k) for k in (1, 2, 3)]
    *direction, direction_square = direct(js, place, blocks, roots, rd, (products[0],))
    direction[1:] = [
        lax.ppermute(direction[k], "fsdp", [(i, i ^ k) for i in range(owners)])
        for k in range(1, owners)
    ]
    a, b, *received[1:] = collect(direction, received[1:])

    x_a, y_b, x_b, y_a = swap(a, 1), swap(b, 2), swap(b, 1), swap(a, 2)

    moment, adam_square = by_rows(
        moment_body, 1, js, received, [as_rows(second_moment)], True
    )
    adam_square = adam_square[:, :, :2, 0].reshape(replicas, row_blocks)
    slot_ids = jnp.arange(replicas, dtype=jnp.int32)
    adam_square = jnp.sum(
        jnp.where((js[:, None] == slot_ids)[:, :, None], adam_square[:, None, :], 0.0), axis=0
    )
    direction_square = direction_square[:, :2, 0].reshape(row_blocks)
    slot_place = (slot_ids == r)[:, None]
    squares = jnp.stack([adam_square, jnp.where(slot_place, direction_square, 0.0)])
    squares = lax.psum(jnp.where(owner_ids[:, None, None, None] == f, squares, 0.0), "fsdp")
    squares = lax.psum(squares, "replica")
    ratio = jnp.sqrt(squares[:, 0]) / jnp.sqrt(squares[:, 1] + 1e-06)
    row_ratio = lax.dynamic_index_in_dim(
        ratio.reshape(columns, row_blocks), f // sub_count, 1, keepdims=False
    )
    scale = jnp.sum(jnp.where(row_slots[:, None] == column_ids, row_ratio, 0.0), axis=1)

    x_a, y_b = follow((x_a, y_b), (scale, x_b, y_a))
    left_new, right_new = by_rows(
        gram_update_body, 3, js, received, [as_rows(stats_left), as_rows(stats_right)], False
    )
    part = (row_slots // replicas) ^ f
    src = 2 * (lax.rem(row_slots, replicas) ^ r) + part // half
    gathered = (a, b, x_a, x_b, y_a, y_b, swap(x_a, 2), swap(y_b, 1))
    update = restore(src, lax.rem(part, half), scale, gathered)
    return (
        update,
        left_new.reshape(stats_left.shape),
        right_new.reshape(stats_right.shape),
        moment.reshape(second_moment.shape),
    )


def slot_columns(row_slots, row_count):
    column_ids = jnp.arange(row_count, dtype=jnp.int32)
    matches = row_slots[None, :] == column_ids[:, None]
    return jnp.sum(jnp.where(matches, column_ids[None, :], 0), axis=1)


def row_local(grads, slots, stats_left, stats_right, root_left, root_right, second_moment):
    fsdp_count = lax.axis_size("fsdp")
    replica_count = lax.axis_size("replica")
    local_grad = grads[0]
    shard_rows, full_width = local_grad.shape
    columns = full_width // B
    row_blocks = slots.shape[0]
    per_owner = columns // fsdp_count
    sub_count = B // shard_rows
    part_rows = shard_rows // replica_count
    mine_rows = sub_count * part_rows
    fsdp_index = lax.axis_index("fsdp")
    replica_index = lax.axis_index("replica")
    row_slots = lax.dynamic_index_in_dim(slots, fsdp_index // sub_count, 0, keepdims=False)
    slot_cols = slot_columns(row_slots, columns)
    summed = lax.psum_scatter(
        local_grad.astype(jnp.float32).astype(jnp.bfloat16),
        "replica",
        scatter_dimension=0,
        tiled=True,
    )
    row_count = summed.shape[0]
    ordered = jnp.take(summed.reshape(row_count, columns, B), slot_cols, axis=1)
    arrived = lax.all_to_all(
        ordered.reshape(row_count, fsdp_count, per_owner * B).transpose(1, 0, 2),
        "fsdp",
        split_axis=0,
        concat_axis=0,
        tiled=True,
    )
    own_split = arrived.reshape(row_blocks, sub_count, part_rows, per_owner, B).transpose(
        0, 3, 1, 2, 4
    )
    gathered = lax.all_gather(own_split[:, :, :, None], "replica", axis=3, tiled=True)
    full_grad = gathered.reshape(row_blocks, per_owner, B, B)
    own_rows = own_split.reshape(row_blocks, per_owner, mine_rows, B)

    def as_rows(array_in):
        return array_in.reshape(row_blocks, per_owner, mine_rows, B)

    column_split = full_grad.reshape(row_blocks, per_owner, B, sub_count, replica_count, part_rows)
    column_part = lax.dynamic_index_in_dim(column_split, replica_index, 4, keepdims=False).reshape(
        row_blocks, per_owner, B, mine_rows
    )
    left_gram = jnp.einsum(
        "abmk,abnk->abmn", own_rows, full_grad, preferred_element_type=jnp.float32
    )
    right_gram = jnp.einsum(
        "abkm,abkn->abmn", column_part, full_grad, preferred_element_type=jnp.float32
    )
    left_new = 0.95 * as_rows(stats_left) + 0.05 * left_gram
    right_new = 0.95 * as_rows(stats_right) + 0.05 * right_gram
    right_full = lax.all_gather(root_right, "replica", axis=3, tiled=True).reshape(
        row_blocks, per_owner, B, B
    )
    inner_left = jnp.einsum(
        "abmk,abkn->abmn", as_rows(root_left), full_grad, preferred_element_type=jnp.float32
    ).astype(jnp.bfloat16)
    direction = jnp.einsum(
        "abmk,abkn->abmn", inner_left, right_full, preferred_element_type=jnp.float32
    )
    grad_float = own_rows.astype(jnp.float32)
    moment = 0.95 * as_rows(second_moment) + 0.05 * grad_float * grad_float
    adam_step = grad_float / (jnp.sqrt(moment) + 1e-08)
    adam_square, shampoo_square = lax.psum(
        (jnp.sum(adam_step * adam_step, axis=(2, 3)), jnp.sum(direction * direction, axis=(2, 3))),
        "replica",
    )
    graft_scale = jnp.sqrt(adam_square) / jnp.sqrt(shampoo_square + 1e-06)
    update_part = (direction * graft_scale[:, :, None, None]).astype(jnp.bfloat16)
    outgoing = (
        update_part.reshape(row_blocks, per_owner, sub_count, part_rows, B)
        .transpose(0, 2, 3, 1, 4)
        .reshape(fsdp_count, part_rows, per_owner * B)
    )
    returned = lax.all_to_all(outgoing, "fsdp", split_axis=0, concat_axis=0, tiled=True)
    ordered = returned.transpose(1, 0, 2).reshape(part_rows, columns, B)
    update = lax.all_gather(
        jnp.take(ordered, row_slots, axis=1).reshape(part_rows, full_width),
        "replica",
        axis=0,
        tiled=True,
    )
    return (
        update,
        left_new.reshape(stats_left.shape),
        right_new.reshape(stats_right.shape),
        moment.reshape(second_moment.shape),
    )


def local(*arrays):
    replicas = lax.axis_size("replica")
    rows, full_width = arrays[0].shape[1:]
    owners = lax.axis_size("fsdp")
    per_owner = full_width // B // owners
    if replicas == 4 and per_owner == replicas and 2 * rows == B and owners == 8:
        return owner_local(*arrays)
    return row_local(*arrays)


def solution(mesh):
    placed = (
        P("replica", "fsdp", None),
        P(),
        P(None, "fsdp", None, "replica", None, None),
        P(None, "fsdp", None, "replica", None, None),
        P(None, "fsdp", None, "replica", None, None),
        P(None, "fsdp", None, "replica", None, None),
        P(None, "fsdp", None, "replica", None, None),
    )
    return jax.shard_map(
        local,
        mesh=mesh,
        in_specs=placed,
        out_specs=(
            P("fsdp", None),
            P(None, "fsdp", None, "replica", None, None),
            P(None, "fsdp", None, "replica", None, None),
            P(None, "fsdp", None, "replica", None, None),
        ),
        check_vma=False,
    )
```

```python
import functools

import jax
import jax.numpy as jnp
from jax import lax
from jax.experimental import pallas as pl
from jax.experimental.pallas import tpu as pltpu
from jax.sharding import PartitionSpec as P

B = 576
LANES = 128
WINDOW = -(-B // LANES) * LANES
VMEM = 64 * 1024 * 1024 - 4096
ANY = pl.BlockSpec(memory_space=pl.ANY)
WHOLE = pl.BlockSpec(memory_space=pltpu.VMEM)
SCALARS = pl.BlockSpec(memory_space=pltpu.SMEM)


def params():
    return pltpu.CompilerParams(vmem_limit_bytes=VMEM)


def cost(flops, moved):
    return pl.CostEstimate(flops=flops, bytes_accessed=moved, transcendentals=0)


def arrange_body(n_add, offsets, n_after, base, halves, cols, grad, *refs):
    adds, refs = refs[: 2 * n_add], refs[2 * n_add + n_after :]
    outs, (buffer, sems) = refs[:-2], refs[-2:]
    n = outs[0].shape[1]
    count = buffer.shape[0]
    half = count // 2

    def copy(i):
        start = pl.multiple_of(cols[i] * B // LANES * LANES, LANES)
        return pltpu.make_async_copy(
            grad.at[pl.ds(base, 2 * n), pl.ds(start, WINDOW)], buffer.at[i], sems.at[i]
        )

    for i in range(count):
        copy(i).start()
    for i in range(count):
        copy(i).wait()
        out, at = (outs[i // half], i % half) if halves else (outs[0], i)
        for shift in (0, B % LANES):

            @pl.when(lax.rem(cols[i] * B, LANES) == shift)
            def _():
                part = buffer[i, :, shift : shift + B]
                out[at, :, :B] = part[:n]
                out[at, :, B:] = part[n:]

        if n_add:
            total = out[at].astype(jnp.float32)
            for k in range(i // half, 2 * n_add, 2):
                total = total + adds[k][offsets[k] + i % half].astype(jnp.float32)
            out[at] = total.astype(out.dtype)


def arrange(cols, grad, base, n, adds=(), halves=True, after=()):
    count = cols.shape[0]
    w = 2 * B
    adds = [part for pair in adds for part in pair]
    shapes = [(count // 2, n, w)] * 2 if halves else [(count, n, w)]
    return pl.pallas_call(
        functools.partial(
            arrange_body, len(adds) // 2, [part[1] for part in adds], len(after), base, halves
        ),
        in_specs=[SCALARS, ANY] + [WHOLE] * len(adds) + [ANY] * len(after),
        out_specs=[WHOLE] * len(shapes),
        out_shape=[jax.ShapeDtypeStruct(s, grad.dtype) for s in shapes],
        scratch_shapes=[
            pltpu.VMEM((count, 2 * n, WINDOW), grad.dtype),
            pltpu.SemaphoreType.DMA((count,)),
        ],
        compiler_params=params(),
        cost_estimate=cost(0, count * n * w * (4 + len(adds))),
    )(cols, grad, *[part[0] for part in adds], *after)


def visit(k, m, p, last):
    return jnp.where(m == k, p, jnp.where(m < k, 0, last))


def pack_roots_body(n, js, left, right, *refs):
    m = pl.program_id(0)
    for k, out in enumerate(refs[-n:]):

        @pl.when(m == k)
        def _():
            for kind, ref in enumerate((left, right)):
                for q in range(2):
                    out[kind, 0, :, q * B : q * B + B] = ref[q, 0]


def pack_roots(js, left, right, after):
    blocks, _, rows, _ = left.shape
    pairs, n, w = blocks // 2, js.shape[0], 2 * B
    source = pl.BlockSpec((2, 1, rows, B), lambda m, p, j: (p, j[m], 0, 0))
    return pl.pallas_call(
        functools.partial(pack_roots_body, n),
        grid_spec=pltpu.PrefetchScalarGridSpec(
            num_scalar_prefetch=1,
            grid=(n, pairs),
            in_specs=[source, source] + [ANY] * len(after),
            out_specs=[
                pl.BlockSpec(
                    (2, 1, rows, w),
                    lambda m, p, j, k=k: (0, visit(k, m, p, pairs - 1), 0, 0),
                )
                for k in range(n)
            ],
        ),
        out_shape=[jax.ShapeDtypeStruct((2, pairs, rows, w), left.dtype)] * n,
        compiler_params=params(),
        cost_estimate=cost(0, 4 * left.size * 2),
    )(js, left, right, *after)


def dot(x, y, dims):
    return lax.dot_general(x, y, (dims, ((), ())), preferred_element_type=jnp.float32)


def assemble(chunks, q, full):
    base = 0
    for chunk in chunks:
        n = chunk.shape[1]
        for h in range(2):
            for side in range(2):
                start = h * (B // 2) + base + side * n
                full[start : start + n, :] = chunk[2 * q + h, :, side * B : side * B + B]
        base += 2 * n


def own_rows(j, h, rd):
    return pl.ds(pl.multiple_of(h * (B // 2) + j * rd, 8), rd)


def gram_body(n, rd, n_chunks, js, *refs):
    chunks, refs = refs[:n_chunks], refs[n_chunks:]
    outs, (g16, g32, l32, r32) = refs[:n], refs[n:]
    for q in range(2):
        assemble(chunks, q, g16)
        g = g16[...]
        g32[...] = g.astype(jnp.float32)
        l32[...] = dot(g, g, ((1,), (1,)))
        r32[...] = dot(g, g, ((0,), (0,)))
        lanes = slice(q * B, q * B + B)
        for k in range(n):
            for kind, full in enumerate((g32, l32, r32)):
                parts = [full[own_rows(js[k], h, rd), :] for h in range(2)]
                outs[k][kind, 0, :, lanes] = jnp.concatenate(parts, axis=0).astype(jnp.bfloat16)


def gram(js, chunks, rd):
    n = js.shape[0]
    count, _, w = chunks[0].shape
    pairs, rows = count // 4, 2 * rd

    return pl.pallas_call(
        functools.partial(gram_body, n, rd, len(chunks)),
        grid_spec=pltpu.PrefetchScalarGridSpec(
            num_scalar_prefetch=1,
            grid=(pairs,),
            in_specs=[
                pl.BlockSpec((4,) + chunk.shape[1:], lambda p, j: (p, 0, 0)) for chunk in chunks
            ],
            out_specs=[pl.BlockSpec((3, 1, rows, w), lambda p, j: (0, p, 0, 0))] * n,
            scratch_shapes=[pltpu.VMEM((B, B), jnp.bfloat16)] + [pltpu.VMEM((B, B), jnp.float32)] * 3,
        ),
        out_shape=[jax.ShapeDtypeStruct((3, pairs, rows, w), jnp.bfloat16)] * n,
        compiler_params=params(),
        cost_estimate=cost(pairs * 8 * B**3, pairs * B * B * 2 * 8),
    )(js, *chunks)


def direct_body(n, rd, n_chunks, n_after, js, place, *refs):
    chunks, roots, refs = refs[:n_chunks], refs[n_chunks : n_chunks + n], refs[n_chunks + n :]
    outs, (square_out, g16, l32, r32, result, sems) = refs[n_after:-6], refs[-6:]
    p = pl.program_id(0)
    f = place[0]
    hr = result.shape[1]

    def send(k):
        return pltpu.make_async_copy(result.at[f ^ k], outs[k], sems.at[k])

    for q in range(2):
        assemble(chunks, q, g16)
        for k in range(n):
            for kind, full in enumerate((l32, r32)):
                part = roots[k][kind, 0, :, q * B : q * B + B].astype(jnp.float32)
                for h in range(2):
                    full[own_rows(js[k], h, rd), :] = part[h * rd : h * rd + rd]
        inner = dot(l32[...].astype(jnp.bfloat16), g16[...], ((1,), (0,))).astype(jnp.bfloat16)
        direction = dot(inner, r32[...].astype(jnp.bfloat16), ((1,), (0,)))
        square_out[0, q : q + 1, :] = jnp.full((1, LANES), jnp.sum(direction * direction))
        direction = direction.astype(jnp.bfloat16)
        for h in range(2):
            for side in range(2):
                start = h * (B // 2) + side * hr
                result[4 * p + 2 * q + h, :, side * B : side * B + B] = direction[start : start + hr]
    for k in range(len(outs)):

        @pl.when((f ^ k) // 4 == p)
        def _():
            send(k).start()

    @pl.when(p == pl.num_programs(0) - 1)
    def _():
        for k in range(len(outs)):
            send(k).wait()


def direct(js, place, chunks, roots, rd, after):
    n = js.shape[0]
    owners, _, w = chunks[0].shape
    hr = sum(chunk.shape[1] for chunk in chunks)
    pairs, rows = roots[0].shape[1], roots[0].shape[2]
    return pl.pallas_call(
        functools.partial(direct_body, n, rd, len(chunks), len(after)),
        grid_spec=pltpu.PrefetchScalarGridSpec(
            num_scalar_prefetch=2,
            grid=(pairs,),
            in_specs=[pl.BlockSpec((4,) + chunk.shape[1:], lambda p, j, f: (p, 0, 0)) for chunk in chunks]
            + [pl.BlockSpec((2, 1, rows, w), lambda p, j, f: (0, p, 0, 0))] * n
            + [ANY] * len(after),
            out_specs=[ANY] * owners + [pl.BlockSpec((1, 8, LANES), lambda p, j, f: (p, 0, 0))],
            scratch_shapes=[pltpu.VMEM((B, B), jnp.bfloat16)]
            + [pltpu.VMEM((B, B), jnp.float32)] * 2
            + [pltpu.VMEM((owners, hr, w), jnp.bfloat16), pltpu.SemaphoreType.DMA((owners,))],
        ),
        out_shape=[jax.ShapeDtypeStruct((hr, w), jnp.bfloat16)] * owners
        + [jax.ShapeDtypeStruct((pairs, 8, LANES), jnp.float32)],
        compiler_params=params(),
        cost_estimate=cost(pairs * 8 * B**3, pairs * B * B * 2 * 8),
    )(js, place, *chunks, *roots, *after)


def follow(arrays, after):
    return pl.pallas_call(
        lambda *refs: None,
        in_specs=[ANY] * (len(arrays) + len(after)),
        out_specs=[ANY] * len(arrays),
        out_shape=[jax.ShapeDtypeStruct(x.shape, x.dtype) for x in arrays],
        input_output_aliases={k: k for k in range(len(arrays))},
        compiler_params=params(),
        cost_estimate=cost(0, 0),
    )(*arrays, *after)


def collect_body(count, n_through, *refs):
    parts, half = refs[:count], count // 2
    low, high = refs[count + n_through : count + n_through + 2]
    buffer, in_sems, out_sems = refs[-3:]

    def arrive(k):
        return pltpu.make_async_copy(parts[k], buffer.at[k], in_sems.at[k])

    def leave(k):
        return pltpu.make_async_copy(
            buffer.at[k], (low, high)[k // half].at[k % half], out_sems.at[k]
        )

    for k in range(len(parts)):
        arrive(k).start()
    for k in range(len(parts)):
        arrive(k).wait()
        leave(k).start()
    for k in range(len(parts)):
        leave(k).wait()


def collect(parts, through):
    count = len(parts)
    halves = jax.ShapeDtypeStruct((count // 2,) + parts[0].shape, parts[0].dtype)
    return pl.pallas_call(
        functools.partial(collect_body, count, len(through)),
        in_specs=[ANY] * (count + len(through)),
        out_specs=[ANY] * (2 + len(through)),
        out_shape=[halves] * 2 + [jax.ShapeDtypeStruct(x.shape, x.dtype) for x in through],
        scratch_shapes=[pltpu.VMEM((count,) + parts[0].shape, parts[0].dtype)]
        + [pltpu.SemaphoreType.DMA((count,))] * 2,
        input_output_aliases={count + k: 2 + k for k in range(len(through))},
        compiler_params=params(),
        cost_estimate=cost(0, 2 * count * parts[0].size * 2),
    )(*parts, *through)


def moment_body(p, q, received, moment, moment_out, square_out):
    a = 2 * p + q
    g = received[0, p, :, q * B : q * B + B].astype(jnp.float32)
    second = 0.95 * moment[a, 0] + 0.05 * g * g
    moment_out[a, 0] = second
    adam = g / (jnp.sqrt(second) + 1e-08)
    square_out[0, a : a + 1, :] = jnp.full((1, LANES), jnp.sum(adam * adam))


def gram_update_body(p, q, received, left, right, left_out, right_out):
    for kind, old, new in ((1, left, left_out), (2, right, right_out)):
        product = received[kind, p, :, q * B : q * B + B].astype(jnp.float32)
        new[2 * p + q, 0] = 0.95 * old[2 * p + q, 0] + 0.05 * product


def by_rows_body(body, n, pairs, js, *refs):
    m = pl.program_id(0)
    for k in range(n):

        @pl.when(m == k)
        def _():
            for p in range(pairs):
                for q in range(2):
                    body(p, q, refs[k], *refs[n:])


def by_rows(body, kinds, js, received, olds, squares):
    n = js.shape[0]
    blocks, _, rows, _ = olds[0].shape
    pairs, w = received[0].shape[1], received[0].shape[3]
    own = pl.BlockSpec((blocks, 1, rows, B), lambda m, j: (0, j[m], 0, 0))
    out_specs = [own] * len(olds)
    out_shape = [jax.ShapeDtypeStruct(old.shape, jnp.float32) for old in olds]
    if squares:
        out_specs.append(pl.BlockSpec((1, 8, LANES), lambda m, j: (m, 0, 0)))
        out_shape.append(jax.ShapeDtypeStruct((n, 8, LANES), jnp.float32))
    return pl.pallas_call(
        functools.partial(by_rows_body, body, n, pairs),
        grid_spec=pltpu.PrefetchScalarGridSpec(
            num_scalar_prefetch=1,
            grid=(n,),
            in_specs=[pl.BlockSpec((kinds, pairs, rows, w), lambda m, j: (0, 0, 0, 0))] * n
            + [own] * len(olds),
            out_specs=out_specs,
        ),
        out_shape=out_shape,
        compiler_params=params(),
        cost_estimate=cost(0, olds[0].size * 10 * len(olds)),
    )(js, *received, *olds)


def restore_body(src, item, scale, *refs):
    sources, (out, buffer, result, in_sems, out_sems) = refs[:-5], refs[-5:]
    columns, n, w = buffer.shape
    slots = result.shape[0]

    def fetch(c, _):
        for k, source in enumerate(sources):

            @pl.when(src[c] == k)
            def _():
                pltpu.make_async_copy(source.at[item[c]], buffer.at[c], in_sems.at[c]).start()

        return 0

    def store(p, slot):
        start = pl.multiple_of(p * w, LANES)
        return pltpu.make_async_copy(
            result.at[slot], out.at[:, pl.ds(start, w)], out_sems.at[slot]
        )

    def step(p, _):
        slot = lax.rem(p, slots)

        @pl.when(p >= slots)
        def _():
            store(p - slots, slot).wait()

        for e in range(2):
            c = 2 * p + e
            pltpu.make_async_copy(sources[0].at[0], buffer.at[c], in_sems.at[c]).wait()
            scaled = (buffer[c].astype(jnp.float32) * scale[c]).astype(result.dtype)
            result[slot, :n, e * B : e * B + B] = scaled[:, :B]
            result[slot, n:, e * B : e * B + B] = scaled[:, B:]
        store(p, slot).start()
        return 0

    pairs = columns // 2
    lax.fori_loop(0, columns, fetch, 0)
    lax.fori_loop(0, pairs, step, 0)
    for p in range(pairs - slots, pairs):
        store(p, p % slots).wait()


def restore(src, item, scale, sources):
    columns = src.shape[0]
    _, n, w = sources[0].shape
    slots = 4
    return pl.pallas_call(
        restore_body,
        in_specs=[SCALARS] * 3 + [ANY] * len(sources),
        out_specs=ANY,
        out_shape=jax.ShapeDtypeStruct((2 * n, columns * B), jnp.bfloat16),
        scratch_shapes=[
            pltpu.VMEM((columns, n, w), jnp.bfloat16),
            pltpu.VMEM((slots, 2 * n, w), jnp.bfloat16),
            pltpu.SemaphoreType.DMA((columns,)),
            pltpu.SemaphoreType.DMA((slots,)),
        ],
        compiler_params=params(),
        cost_estimate=cost(0, columns * n * w * 4),
    )(src, item, scale, *sources)


def owner_local(grads, slots, stats_left, stats_right, root_left, root_right, second_moment):
    owners = lax.axis_size("fsdp")
    replicas = lax.axis_size("replica")
    grad = grads[0]
    rows, full_width = grad.shape
    columns = full_width // B
    row_blocks = slots.shape[0]
    sub_count = B // rows
    rd = rows // replicas
    half = owners // 2
    f = lax.axis_index("fsdp")
    r = lax.axis_index("replica")
    js = r ^ jnp.arange(replicas, dtype=jnp.int32)
    row_slots = lax.dynamic_index_in_dim(slots, f // sub_count, 0, keepdims=False)
    column_ids = jnp.arange(columns, dtype=jnp.int32)
    owner_ids = jnp.arange(owners, dtype=jnp.int32)
    halves = (owner_ids[:half], owner_ids[half:])
    wanted = jnp.stack(
        [
            replicas * jnp.concatenate([halves[low], halves[high]])
            + (r ^ jnp.where(owner_ids < half, low_step, high_step))
            for low, low_step, high, high_step in ((0, 3, 0, 1), (1, 3, 1, 2), (0, 2, 1, 1), (0, 0, 1, 0))
        ]
    )
    cols = jnp.sum(jnp.where(row_slots == wanted[:, :, None], column_ids, 0), axis=2)

    def swap(x, k):
        return lax.ppermute(x, "replica", [(i, i ^ k) for i in range(replicas)])

    def as_rows(x):
        return x.reshape(row_blocks, -1, sub_count * rd, B)

    first = rows // 64 * 16
    chunks = ((0, first), (2 * first, rows // 2 - first))
    after, early, blocks = (), [], []
    for chunk in chunks:
        x, y = arrange(cols[:2].reshape(-1), grad, *chunk, after=after)
        early.append((swap(x, 1), swap(y, 2)))
        after = (x,)
    roots = pack_roots(js, as_rows(root_left), as_rows(root_right), after)
    after = (roots[0],)
    for (x, y), chunk in zip(early, chunks):
        y_a, x_b = arrange(cols[2], grad, *chunk, [((x, 0), (y, 0))], after=after)
        terms = [((x, half), (y, half)), ((swap(y_a, 2), 0), (swap(x_b, 1), 0))]
        (owned,) = arrange(cols[3], grad, *chunk, terms, halves=False)
        blocks.append(lax.all_to_all(owned, "fsdp", split_axis=0, concat_axis=0, tiled=True))
        after = (owned,)
    sent = follow(roots[1:], after)
    roots = [roots[0]] + [swap(x, k) for k, x in zip((1, 2, 3), sent)]

    place = f.reshape(1)
    products = gram(js, blocks, rd)
    received = [products[0]] + [swap(products[k], k) for k in (1, 2, 3)]
    *direction, direction_square = direct(js, place, blocks, roots, rd, (products[0],))
    direction[1:] = [
        lax.ppermute(direction[k], "fsdp", [(i, i ^ k) for i in range(owners)])
        for k in range(1, owners)
    ]
    a, b, *received[1:] = collect(direction, received[1:])

    x_a, y_b, x_b, y_a = swap(a, 1), swap(b, 2), swap(b, 1), swap(a, 2)

    moment, adam_square = by_rows(
        moment_body, 1, js, received, [as_rows(second_moment)], True
    )
    adam_square = adam_square[:, :row_blocks, 0]
    slot_ids = jnp.arange(replicas, dtype=jnp.int32)
    adam_square = jnp.sum(
        jnp.where((js[:, None] == slot_ids)[:, :, None], adam_square[:, None, :], 0.0), axis=0
    )
    direction_square = direction_square[:, :2, 0].reshape(row_blocks)
    slot_place = (slot_ids == r)[:, None]
    squares = jnp.stack([adam_square, jnp.where(slot_place, direction_square, 0.0)])
    squares = lax.psum(jnp.where(owner_ids[:, None, None, None] == f, squares, 0.0), "fsdp")
    squares = lax.psum(squares, "replica")
    ratio = jnp.sqrt(squares[:, 0]) / jnp.sqrt(squares[:, 1] + 1e-06)
    row_ratio = lax.dynamic_index_in_dim(
        ratio.reshape(columns, row_blocks), f // sub_count, 1, keepdims=False
    )
    scale = jnp.sum(jnp.where(row_slots[:, None] == column_ids, row_ratio, 0.0), axis=1)

    x_a, y_b = follow((x_a, y_b), (scale, x_b, y_a))
    left_new, right_new = by_rows(
        gram_update_body, 3, js, received, [as_rows(stats_left), as_rows(stats_right)], False
    )
    part = (row_slots // replicas) ^ f
    src = 2 * (lax.rem(row_slots, replicas) ^ r) + part // half
    gathered = (a, b, x_a, x_b, y_a, y_b, swap(x_a, 2), swap(y_b, 1))
    update = restore(src, lax.rem(part, half), scale, gathered)
    return (
        update,
        left_new.reshape(stats_left.shape),
        right_new.reshape(stats_right.shape),
        moment.reshape(second_moment.shape),
    )


def slot_columns(row_slots, row_count):
    column_ids = jnp.arange(row_count, dtype=jnp.int32)
    matches = row_slots[None, :] == column_ids[:, None]
    return jnp.sum(jnp.where(matches, column_ids[None, :], 0), axis=1)


def row_local(grads, slots, stats_left, stats_right, root_left, root_right, second_moment):
    fsdp_count = lax.axis_size("fsdp")
    replica_count = lax.axis_size("replica")
    local_grad = grads[0]
    shard_rows, full_width = local_grad.shape
    columns = full_width // B
    row_blocks = slots.shape[0]
    per_owner = columns // fsdp_count
    sub_count = B // shard_rows
    part_rows = shard_rows // replica_count
    mine_rows = sub_count * part_rows
    fsdp_index = lax.axis_index("fsdp")
    replica_index = lax.axis_index("replica")
    row_slots = lax.dynamic_index_in_dim(slots, fsdp_index // sub_count, 0, keepdims=False)
    slot_cols = slot_columns(row_slots, columns)
    summed = lax.psum_scatter(
        local_grad.astype(jnp.float32).astype(jnp.bfloat16),
        "replica",
        scatter_dimension=0,
        tiled=True,
    )
    row_count = summed.shape[0]
    ordered = jnp.take(summed.reshape(row_count, columns, B), slot_cols, axis=1)
    arrived = lax.all_to_all(
        ordered.reshape(row_count, fsdp_count, per_owner * B).transpose(1, 0, 2),
        "fsdp",
        split_axis=0,
        concat_axis=0,
        tiled=True,
    )
    own_split = arrived.reshape(row_blocks, sub_count, part_rows, per_owner, B).transpose(
        0, 3, 1, 2, 4
    )
    gathered = lax.all_gather(own_split[:, :, :, None], "replica", axis=3, tiled=True)
    full_grad = gathered.reshape(row_blocks, per_owner, B, B)
    own_rows = own_split.reshape(row_blocks, per_owner, mine_rows, B)

    def as_rows(array_in):
        return array_in.reshape(row_blocks, per_owner, mine_rows, B)

    column_split = full_grad.reshape(row_blocks, per_owner, B, sub_count, replica_count, part_rows)
    column_part = lax.dynamic_index_in_dim(column_split, replica_index, 4, keepdims=False).reshape(
        row_blocks, per_owner, B, mine_rows
    )
    left_gram = jnp.einsum(
        "abmk,abnk->abmn", own_rows, full_grad, preferred_element_type=jnp.float32
    )
    right_gram = jnp.einsum(
        "abkm,abkn->abmn", column_part, full_grad, preferred_element_type=jnp.float32
    )
    left_new = 0.95 * as_rows(stats_left) + 0.05 * left_gram
    right_new = 0.95 * as_rows(stats_right) + 0.05 * right_gram
    right_full = lax.all_gather(root_right, "replica", axis=3, tiled=True).reshape(
        row_blocks, per_owner, B, B
    )
    inner_left = jnp.einsum(
        "abmk,abkn->abmn", as_rows(root_left), full_grad, preferred_element_type=jnp.float32
    ).astype(jnp.bfloat16)
    direction = jnp.einsum(
        "abmk,abkn->abmn", inner_left, right_full, preferred_element_type=jnp.float32
    )
    grad_float = own_rows.astype(jnp.float32)
    moment = 0.95 * as_rows(second_moment) + 0.05 * grad_float * grad_float
    adam_step = grad_float / (jnp.sqrt(moment) + 1e-08)
    adam_square, shampoo_square = lax.psum(
        (jnp.sum(adam_step * adam_step, axis=(2, 3)), jnp.sum(direction * direction, axis=(2, 3))),
        "replica",
    )
    graft_scale = jnp.sqrt(adam_square) / jnp.sqrt(shampoo_square + 1e-06)
    update_part = (direction * graft_scale[:, :, None, None]).astype(jnp.bfloat16)
    outgoing = (
        update_part.reshape(row_blocks, per_owner, sub_count, part_rows, B)
        .transpose(0, 2, 3, 1, 4)
        .reshape(fsdp_count, part_rows, per_owner * B)
    )
    returned = lax.all_to_all(outgoing, "fsdp", split_axis=0, concat_axis=0, tiled=True)
    ordered = returned.transpose(1, 0, 2).reshape(part_rows, columns, B)
    update = lax.all_gather(
        jnp.take(ordered, row_slots, axis=1).reshape(part_rows, full_width),
        "replica",
        axis=0,
        tiled=True,
    )
    return (
        update,
        left_new.reshape(stats_left.shape),
        right_new.reshape(stats_right.shape),
        moment.reshape(second_moment.shape),
    )


def local(*arrays):
    replicas = lax.axis_size("replica")
    rows, full_width = arrays[0].shape[1:]
    owners = lax.axis_size("fsdp")
    per_owner = full_width // B // owners
    if replicas == 4 and per_owner == replicas and 2 * rows == B and owners == 8:
        return owner_local(*arrays)
    return row_local(*arrays)


def solution(mesh):
    placed = (
        P("replica", "fsdp", None),
        P(),
        P(None, "fsdp", None, "replica", None, None),
        P(None, "fsdp", None, "replica", None, None),
        P(None, "fsdp", None, "replica", None, None),
        P(None, "fsdp", None, "replica", None, None),
        P(None, "fsdp", None, "replica", None, None),
    )
    return jax.shard_map(
        local,
        mesh=mesh,
        in_specs=placed,
        out_specs=(
            P("fsdp", None),
            P(None, "fsdp", None, "replica", None, None),
            P(None, "fsdp", None, "replica", None, None),
            P(None, "fsdp", None, "replica", None, None),
        ),
        check_vma=False,
    )
```

```python
import functools

import jax
import jax.numpy as jnp
from jax import lax
from jax.experimental import pallas as pl
from jax.experimental.pallas import tpu as pltpu
from jax.sharding import PartitionSpec as P

B = 576
LANES = 128
WINDOW = -(-B // LANES) * LANES
VMEM = 64 * 1024 * 1024 - 4096
ANY = pl.BlockSpec(memory_space=pl.ANY)
WHOLE = pl.BlockSpec(memory_space=pltpu.VMEM)
SCALARS = pl.BlockSpec(memory_space=pltpu.SMEM)


def params():
    return pltpu.CompilerParams(vmem_limit_bytes=VMEM)


def cost(flops, moved):
    return pl.CostEstimate(flops=flops, bytes_accessed=moved, transcendentals=0)


def arrange_body(n_add, offsets, n_after, base, halves, cols, grad, *refs):
    adds, refs = refs[: 2 * n_add], refs[2 * n_add + n_after :]
    outs, (buffer, sems) = refs[:-2], refs[-2:]
    n = outs[0].shape[1]
    count = buffer.shape[0]
    half = count // 2

    def copy(i):
        start = pl.multiple_of(cols[i] * B // LANES * LANES, LANES)
        return pltpu.make_async_copy(
            grad.at[pl.ds(base, 2 * n), pl.ds(start, WINDOW)], buffer.at[i], sems.at[i]
        )

    for i in range(count):
        copy(i).start()
    for i in range(count):
        copy(i).wait()
        out, at = (outs[i // half], i % half) if halves else (outs[0], i)
        for shift in (0, B % LANES):

            @pl.when(lax.rem(cols[i] * B, LANES) == shift)
            def _():
                part = buffer[i, :, shift : shift + B]
                out[at, :, :B] = part[:n]
                out[at, :, B:] = part[n:]

        if n_add:
            total = out[at].astype(jnp.float32)
            for k in range(i // half, 2 * n_add, 2):
                total = total + adds[k][offsets[k] + i % half].astype(jnp.float32)
            out[at] = total.astype(out.dtype)


def arrange(cols, grad, base, n, adds=(), halves=True, after=()):
    count = cols.shape[0]
    w = 2 * B
    adds = [part for pair in adds for part in pair]
    shapes = [(count // 2, n, w)] * 2 if halves else [(count, n, w)]
    return pl.pallas_call(
        functools.partial(
            arrange_body, len(adds) // 2, [part[1] for part in adds], len(after), base, halves
        ),
        in_specs=[SCALARS, ANY] + [WHOLE] * len(adds) + [ANY] * len(after),
        out_specs=[WHOLE] * len(shapes),
        out_shape=[jax.ShapeDtypeStruct(s, grad.dtype) for s in shapes],
        scratch_shapes=[
            pltpu.VMEM((count, 2 * n, WINDOW), grad.dtype),
            pltpu.SemaphoreType.DMA((count,)),
        ],
        compiler_params=params(),
        cost_estimate=cost(0, count * n * w * (4 + len(adds))),
    )(cols, grad, *[part[0] for part in adds], *after)


def visit(k, m, p, last):
    return jnp.where(m == k, p, jnp.where(m < k, 0, last))


def pack_roots_body(n, js, left, right, *refs):
    m = pl.program_id(0)
    for k, out in enumerate(refs[-n:]):

        @pl.when(m == k)
        def _():
            for kind, ref in enumerate((left, right)):
                for q in range(2):
                    out[kind, 0, :, q * B : q * B + B] = ref[q, 0]


def pack_roots(js, left, right, after):
    blocks, _, rows, _ = left.shape
    pairs, n, w = blocks // 2, js.shape[0], 2 * B
    source = pl.BlockSpec((2, 1, rows, B), lambda m, p, j: (p, j[m], 0, 0))
    return pl.pallas_call(
        functools.partial(pack_roots_body, n),
        grid_spec=pltpu.PrefetchScalarGridSpec(
            num_scalar_prefetch=1,
            grid=(n, pairs),
            in_specs=[source, source] + [ANY] * len(after),
            out_specs=[
                pl.BlockSpec(
                    (2, 1, rows, w),
                    lambda m, p, j, k=k: (0, visit(k, m, p, pairs - 1), 0, 0),
                )
                for k in range(n)
            ],
        ),
        out_shape=[jax.ShapeDtypeStruct((2, pairs, rows, w), left.dtype)] * n,
        compiler_params=params(),
        cost_estimate=cost(0, 4 * left.size * 2),
    )(js, left, right, *after)


def dot(x, y, dims):
    return lax.dot_general(x, y, (dims, ((), ())), preferred_element_type=jnp.float32)


def assemble(chunks, q, full):
    base = 0
    for chunk in chunks:
        n = chunk.shape[1]
        for h in range(2):
            for side in range(2):
                start = h * (B // 2) + base + side * n
                full[start : start + n, :] = chunk[2 * q + h, :, side * B : side * B + B]
        base += 2 * n


def own_rows(j, h, rd):
    return pl.ds(pl.multiple_of(h * (B // 2) + j * rd, 8), rd)


def gram_body(n, rd, n_chunks, js, *refs):
    chunks, refs = refs[:n_chunks], refs[n_chunks:]
    outs, (g16, g32, l32, r32) = refs[:n], refs[n:]
    for q in range(2):
        assemble(chunks, q, g16)
        g = g16[...]
        g32[...] = g.astype(jnp.float32)
        l32[...] = dot(g, g, ((1,), (1,)))
        r32[...] = dot(g, g, ((0,), (0,)))
        lanes = slice(q * B, q * B + B)
        for k in range(n):
            for kind, full in enumerate((g32, l32, r32)):
                parts = [full[own_rows(js[k], h, rd), :] for h in range(2)]
                outs[k][kind, 0, :, lanes] = jnp.concatenate(parts, axis=0).astype(jnp.bfloat16)


def gram(js, chunks, rd):
    n = js.shape[0]
    count, _, w = chunks[0].shape
    pairs, rows = count // 4, 2 * rd

    return pl.pallas_call(
        functools.partial(gram_body, n, rd, len(chunks)),
        grid_spec=pltpu.PrefetchScalarGridSpec(
            num_scalar_prefetch=1,
            grid=(pairs,),
            in_specs=[
                pl.BlockSpec((4,) + chunk.shape[1:], lambda p, j: (p, 0, 0)) for chunk in chunks
            ],
            out_specs=[pl.BlockSpec((3, 1, rows, w), lambda p, j: (0, p, 0, 0))] * n,
            scratch_shapes=[pltpu.VMEM((B, B), jnp.bfloat16)] + [pltpu.VMEM((B, B), jnp.float32)] * 3,
        ),
        out_shape=[jax.ShapeDtypeStruct((3, pairs, rows, w), jnp.bfloat16)] * n,
        compiler_params=params(),
        cost_estimate=cost(pairs * 8 * B**3, pairs * B * B * 2 * 8),
    )(js, *chunks)


def direct_body(n, rd, n_chunks, n_after, js, place, *refs):
    chunks, roots, refs = refs[:n_chunks], refs[n_chunks : n_chunks + n], refs[n_chunks + n :]
    outs, (square_out, g16, l32, r32, result, sems) = refs[n_after:-6], refs[-6:]
    p = pl.program_id(0)
    f = place[0]
    hr = result.shape[1]

    def send(k):
        return pltpu.make_async_copy(result.at[f ^ k], outs[k], sems.at[k])

    for q in range(2):
        assemble(chunks, q, g16)
        for k in range(n):
            for kind, full in enumerate((l32, r32)):
                part = roots[k][kind, 0, :, q * B : q * B + B].astype(jnp.float32)
                for h in range(2):
                    full[own_rows(js[k], h, rd), :] = part[h * rd : h * rd + rd]
        inner = dot(l32[...].astype(jnp.bfloat16), g16[...], ((1,), (0,))).astype(jnp.bfloat16)
        direction = dot(inner, r32[...].astype(jnp.bfloat16), ((1,), (0,)))
        square_out[0, q : q + 1, :] = jnp.full((1, LANES), jnp.sum(direction * direction))
        direction = direction.astype(jnp.bfloat16)
        for h in range(2):
            for side in range(2):
                start = h * (B // 2) + side * hr
                result[4 * p + 2 * q + h, :, side * B : side * B + B] = direction[start : start + hr]
    for k in range(len(outs)):

        @pl.when((f ^ k) // 4 == p)
        def _():
            send(k).start()

    @pl.when(p == pl.num_programs(0) - 1)
    def _():
        for k in range(len(outs)):
            send(k).wait()


def direct(js, place, chunks, roots, rd, after):
    n = js.shape[0]
    owners, _, w = chunks[0].shape
    hr = sum(chunk.shape[1] for chunk in chunks)
    pairs, rows = roots[0].shape[1], roots[0].shape[2]
    return pl.pallas_call(
        functools.partial(direct_body, n, rd, len(chunks), len(after)),
        grid_spec=pltpu.PrefetchScalarGridSpec(
            num_scalar_prefetch=2,
            grid=(pairs,),
            in_specs=[pl.BlockSpec((4,) + chunk.shape[1:], lambda p, j, f: (p, 0, 0)) for chunk in chunks]
            + [pl.BlockSpec((2, 1, rows, w), lambda p, j, f: (0, p, 0, 0))] * n
            + [ANY] * len(after),
            out_specs=[ANY] * owners + [pl.BlockSpec((1, 8, LANES), lambda p, j, f: (p, 0, 0))],
            scratch_shapes=[pltpu.VMEM((B, B), jnp.bfloat16)]
            + [pltpu.VMEM((B, B), jnp.float32)] * 2
            + [pltpu.VMEM((owners, hr, w), jnp.bfloat16), pltpu.SemaphoreType.DMA((owners,))],
        ),
        out_shape=[jax.ShapeDtypeStruct((hr, w), jnp.bfloat16)] * owners
        + [jax.ShapeDtypeStruct((pairs, 8, LANES), jnp.float32)],
        compiler_params=params(),
        cost_estimate=cost(pairs * 8 * B**3, pairs * B * B * 2 * 8),
    )(js, place, *chunks, *roots, *after)


def follow(arrays, after):
    return pl.pallas_call(
        lambda *refs: None,
        in_specs=[ANY] * (len(arrays) + len(after)),
        out_specs=[ANY] * len(arrays),
        out_shape=[jax.ShapeDtypeStruct(x.shape, x.dtype) for x in arrays],
        input_output_aliases={k: k for k in range(len(arrays))},
        compiler_params=params(),
        cost_estimate=cost(0, 0),
    )(*arrays, *after)


def collect_body(count, n_through, *refs):
    parts, half = refs[:count], count // 2
    low, high = refs[count + n_through : count + n_through + 2]
    buffer, in_sems, out_sems = refs[-3:]

    def arrive(k):
        return pltpu.make_async_copy(parts[k], buffer.at[k], in_sems.at[k])

    def leave(k):
        return pltpu.make_async_copy(
            buffer.at[k], (low, high)[k // half].at[k % half], out_sems.at[k]
        )

    for k in range(len(parts)):
        arrive(k).start()
    for k in range(len(parts)):
        arrive(k).wait()
        leave(k).start()
    for k in range(len(parts)):
        leave(k).wait()


def collect(parts, through):
    count = len(parts)
    halves = jax.ShapeDtypeStruct((count // 2,) + parts[0].shape, parts[0].dtype)
    return pl.pallas_call(
        functools.partial(collect_body, count, len(through)),
        in_specs=[ANY] * (count + len(through)),
        out_specs=[ANY] * (2 + len(through)),
        out_shape=[halves] * 2 + [jax.ShapeDtypeStruct(x.shape, x.dtype) for x in through],
        scratch_shapes=[pltpu.VMEM((count,) + parts[0].shape, parts[0].dtype)]
        + [pltpu.SemaphoreType.DMA((count,))] * 2,
        input_output_aliases={count + k: 2 + k for k in range(len(through))},
        compiler_params=params(),
        cost_estimate=cost(0, 2 * count * parts[0].size * 2),
    )(*parts, *through)


def moment_body(p, q, received, moment, moment_out, square_out):
    a = 2 * p + q
    g = received[0, p, :, q * B : q * B + B].astype(jnp.float32)
    second = 0.95 * moment[a, 0] + 0.05 * g * g
    moment_out[a, 0] = second
    adam = g / (jnp.sqrt(second) + 1e-08)
    square_out[0, a : a + 1, :] = jnp.full((1, LANES), jnp.sum(adam * adam))


def gram_update_body(p, q, received, left, right, left_out, right_out):
    for kind, old, new in ((1, left, left_out), (2, right, right_out)):
        product = received[kind, p, :, q * B : q * B + B].astype(jnp.float32)
        new[2 * p + q, 0] = 0.95 * old[2 * p + q, 0] + 0.05 * product


def by_rows_body(body, n, pairs, js, *refs):
    m = pl.program_id(0)
    for k in range(n):

        @pl.when(m == k)
        def _():
            for p in range(pairs):
                for q in range(2):
                    body(p, q, refs[k], *refs[n:])


def by_rows(body, kinds, js, received, olds, squares):
    n = js.shape[0]
    blocks, _, rows, _ = olds[0].shape
    pairs, w = received[0].shape[1], received[0].shape[3]
    own = pl.BlockSpec((blocks, 1, rows, B), lambda m, j: (0, j[m], 0, 0))
    out_specs = [own] * len(olds)
    out_shape = [jax.ShapeDtypeStruct(old.shape, jnp.float32) for old in olds]
    if squares:
        out_specs.append(pl.BlockSpec((1, 8, LANES), lambda m, j: (m, 0, 0)))
        out_shape.append(jax.ShapeDtypeStruct((n, 8, LANES), jnp.float32))
    return pl.pallas_call(
        functools.partial(by_rows_body, body, n, pairs),
        grid_spec=pltpu.PrefetchScalarGridSpec(
            num_scalar_prefetch=1,
            grid=(n,),
            in_specs=[pl.BlockSpec((kinds, pairs, rows, w), lambda m, j: (0, 0, 0, 0))] * n
            + [own] * len(olds),
            out_specs=out_specs,
        ),
        out_shape=out_shape,
        compiler_params=params(),
        cost_estimate=cost(0, olds[0].size * 10 * len(olds)),
    )(js, *received, *olds)


def restore_body(src, item, scale, *refs):
    sources, (out, buffer, result, in_sems, out_sems) = refs[:-5], refs[-5:]
    columns, n, w = buffer.shape
    slots = result.shape[0]

    def fetch(c, _):
        for k, source in enumerate(sources):

            @pl.when(src[c] == k)
            def _():
                pltpu.make_async_copy(source.at[item[c]], buffer.at[c], in_sems.at[c]).start()

        return 0

    def store(p, slot):
        start = pl.multiple_of(p * w, LANES)
        return pltpu.make_async_copy(
            result.at[slot], out.at[:, pl.ds(start, w)], out_sems.at[slot]
        )

    def step(p, _):
        slot = lax.rem(p, slots)

        @pl.when(p >= slots)
        def _():
            store(p - slots, slot).wait()

        for e in range(2):
            c = 2 * p + e
            pltpu.make_async_copy(sources[0].at[0], buffer.at[c], in_sems.at[c]).wait()
            scaled = (buffer[c].astype(jnp.float32) * scale[c]).astype(result.dtype)
            result[slot, :n, e * B : e * B + B] = scaled[:, :B]
            result[slot, n:, e * B : e * B + B] = scaled[:, B:]
        store(p, slot).start()
        return 0

    pairs = columns // 2
    lax.fori_loop(0, columns, fetch, 0)
    lax.fori_loop(0, pairs, step, 0)
    for p in range(pairs - slots, pairs):
        store(p, p % slots).wait()


def restore(src, item, scale, sources):
    columns = src.shape[0]
    _, n, w = sources[0].shape
    slots = 4
    return pl.pallas_call(
        restore_body,
        in_specs=[SCALARS] * 3 + [ANY] * len(sources),
        out_specs=ANY,
        out_shape=jax.ShapeDtypeStruct((2 * n, columns * B), jnp.bfloat16),
        scratch_shapes=[
            pltpu.VMEM((columns, n, w), jnp.bfloat16),
            pltpu.VMEM((slots, 2 * n, w), jnp.bfloat16),
            pltpu.SemaphoreType.DMA((columns,)),
            pltpu.SemaphoreType.DMA((slots,)),
        ],
        compiler_params=params(),
        cost_estimate=cost(0, columns * n * w * 4),
    )(src, item, scale, *sources)


def owner_local(grads, slots, stats_left, stats_right, root_left, root_right, second_moment):
    owners = lax.axis_size("fsdp")
    replicas = lax.axis_size("replica")
    grad = grads[0]
    rows, full_width = grad.shape
    columns = full_width // B
    row_blocks = slots.shape[0]
    sub_count = B // rows
    rd = rows // replicas
    half = owners // 2
    f = lax.axis_index("fsdp")
    r = lax.axis_index("replica")
    js = r ^ jnp.arange(replicas, dtype=jnp.int32)
    row_slots = lax.dynamic_index_in_dim(slots, f // sub_count, 0, keepdims=False)
    column_ids = jnp.arange(columns, dtype=jnp.int32)
    owner_ids = jnp.arange(owners, dtype=jnp.int32)
    halves = (owner_ids[:half], owner_ids[half:])
    wanted = jnp.stack(
        [
            replicas * jnp.concatenate([halves[low], halves[high]])
            + (r ^ jnp.where(owner_ids < half, low_step, high_step))
            for low, low_step, high, high_step in ((0, 3, 0, 1), (1, 3, 1, 2), (0, 2, 1, 1), (0, 0, 1, 0))
        ]
    )
    cols = jnp.sum(jnp.where(row_slots == wanted[:, :, None], column_ids, 0), axis=2)

    def swap(x, k):
        return lax.ppermute(x, "replica", [(i, i ^ k) for i in range(replicas)])

    def plus(x, y):
        return (x.astype(jnp.float32) + y.astype(jnp.float32)).astype(x.dtype)

    def as_rows(x):
        return x.reshape(row_blocks, -1, sub_count * rd, B)

    first = rows // 64 * 16
    chunks = ((0, first), (2 * first, rows // 2 - first))
    after, early, blocks = (), [], []
    for chunk in chunks:
        x, y = arrange(cols[:2].reshape(-1), grad, *chunk, after=after)
        early.append((swap(x, 1), swap(y, 2)))
        after = (x,)
    roots = pack_roots(js, as_rows(root_left), as_rows(root_right), after)
    after = (roots[0],)
    for (x, y), chunk in zip(early, chunks):
        y_a, x_b = arrange(cols[2], grad, *chunk, after=after)
        y_a, x_b = plus(y_a, x[:half]), plus(x_b, y[:half])
        terms = [((x, half), (y, half)), ((swap(y_a, 2), 0), (swap(x_b, 1), 0))]
        (owned,) = arrange(cols[3], grad, *chunk, terms, halves=False)
        blocks.append(lax.all_to_all(owned, "fsdp", split_axis=0, concat_axis=0, tiled=True))
        after = (owned,)
    sent = follow(roots[1:], after)
    roots = [roots[0]] + [swap(x, k) for k, x in zip((1, 2, 3), sent)]

    place = f.reshape(1)
    products = gram(js, blocks, rd)
    received = [products[0]] + [swap(products[k], k) for k in (1, 2, 3)]
    *direction, direction_square = direct(js, place, blocks, roots, rd, (products[0],))
    direction[1:] = [
        lax.ppermute(direction[k], "fsdp", [(i, i ^ k) for i in range(owners)])
        for k in range(1, owners)
    ]
    a, b, *received[1:] = collect(direction, received[1:])

    x_a, y_b, x_b, y_a = swap(a, 1), swap(b, 2), swap(b, 1), swap(a, 2)

    moment, adam_square = by_rows(
        moment_body, 1, js, received, [as_rows(second_moment)], True
    )
    adam_square = adam_square[:, :row_blocks, 0]
    slot_ids = jnp.arange(replicas, dtype=jnp.int32)
    adam_square = jnp.sum(
        jnp.where((js[:, None] == slot_ids)[:, :, None], adam_square[:, None, :], 0.0), axis=0
    )
    direction_square = direction_square[:, :2, 0].reshape(row_blocks)
    slot_place = (slot_ids == r)[:, None]
    squares = jnp.stack([adam_square, jnp.where(slot_place, direction_square, 0.0)])
    squares = lax.psum(jnp.where(owner_ids[:, None, None, None] == f, squares, 0.0), "fsdp")
    squares = lax.psum(squares, "replica")
    ratio = jnp.sqrt(squares[:, 0]) / jnp.sqrt(squares[:, 1] + 1e-06)
    row_ratio = lax.dynamic_index_in_dim(
        ratio.reshape(columns, row_blocks), f // sub_count, 1, keepdims=False
    )
    scale = jnp.sum(jnp.where(row_slots[:, None] == column_ids, row_ratio, 0.0), axis=1)

    x_a, y_b = follow((x_a, y_b), (scale, x_b, y_a))
    left_new, right_new = by_rows(
        gram_update_body, 3, js, received, [as_rows(stats_left), as_rows(stats_right)], False
    )
    part = (row_slots // replicas) ^ f
    src = 2 * (lax.rem(row_slots, replicas) ^ r) + part // half
    gathered = (a, b, x_a, x_b, y_a, y_b, swap(x_a, 2), swap(y_b, 1))
    update = restore(src, lax.rem(part, half), scale, gathered)
    return (
        update,
        left_new.reshape(stats_left.shape),
        right_new.reshape(stats_right.shape),
        moment.reshape(second_moment.shape),
    )


def slot_columns(row_slots, row_count):
    column_ids = jnp.arange(row_count, dtype=jnp.int32)
    matches = row_slots[None, :] == column_ids[:, None]
    return jnp.sum(jnp.where(matches, column_ids[None, :], 0), axis=1)


def row_local(grads, slots, stats_left, stats_right, root_left, root_right, second_moment):
    fsdp_count = lax.axis_size("fsdp")
    replica_count = lax.axis_size("replica")
    local_grad = grads[0]
    shard_rows, full_width = local_grad.shape
    columns = full_width // B
    row_blocks = slots.shape[0]
    per_owner = columns // fsdp_count
    sub_count = B // shard_rows
    part_rows = shard_rows // replica_count
    mine_rows = sub_count * part_rows
    fsdp_index = lax.axis_index("fsdp")
    replica_index = lax.axis_index("replica")
    row_slots = lax.dynamic_index_in_dim(slots, fsdp_index // sub_count, 0, keepdims=False)
    slot_cols = slot_columns(row_slots, columns)
    summed = lax.psum_scatter(
        local_grad.astype(jnp.float32).astype(jnp.bfloat16),
        "replica",
        scatter_dimension=0,
        tiled=True,
    )
    row_count = summed.shape[0]
    ordered = jnp.take(summed.reshape(row_count, columns, B), slot_cols, axis=1)
    arrived = lax.all_to_all(
        ordered.reshape(row_count, fsdp_count, per_owner * B).transpose(1, 0, 2),
        "fsdp",
        split_axis=0,
        concat_axis=0,
        tiled=True,
    )
    own_split = arrived.reshape(row_blocks, sub_count, part_rows, per_owner, B).transpose(
        0, 3, 1, 2, 4
    )
    gathered = lax.all_gather(own_split[:, :, :, None], "replica", axis=3, tiled=True)
    full_grad = gathered.reshape(row_blocks, per_owner, B, B)
    own_rows = own_split.reshape(row_blocks, per_owner, mine_rows, B)

    def as_rows(array_in):
        return array_in.reshape(row_blocks, per_owner, mine_rows, B)

    column_split = full_grad.reshape(row_blocks, per_owner, B, sub_count, replica_count, part_rows)
    column_part = lax.dynamic_index_in_dim(column_split, replica_index, 4, keepdims=False).reshape(
        row_blocks, per_owner, B, mine_rows
    )
    left_gram = jnp.einsum(
        "abmk,abnk->abmn", own_rows, full_grad, preferred_element_type=jnp.float32
    )
    right_gram = jnp.einsum(
        "abkm,abkn->abmn", column_part, full_grad, preferred_element_type=jnp.float32
    )
    left_new = 0.95 * as_rows(stats_left) + 0.05 * left_gram
    right_new = 0.95 * as_rows(stats_right) + 0.05 * right_gram
    right_full = lax.all_gather(root_right, "replica", axis=3, tiled=True).reshape(
        row_blocks, per_owner, B, B
    )
    inner_left = jnp.einsum(
        "abmk,abkn->abmn", as_rows(root_left), full_grad, preferred_element_type=jnp.float32
    ).astype(jnp.bfloat16)
    direction = jnp.einsum(
        "abmk,abkn->abmn", inner_left, right_full, preferred_element_type=jnp.float32
    )
    grad_float = own_rows.astype(jnp.float32)
    moment = 0.95 * as_rows(second_moment) + 0.05 * grad_float * grad_float
    adam_step = grad_float / (jnp.sqrt(moment) + 1e-08)
    adam_square, shampoo_square = lax.psum(
        (jnp.sum(adam_step * adam_step, axis=(2, 3)), jnp.sum(direction * direction, axis=(2, 3))),
        "replica",
    )
    graft_scale = jnp.sqrt(adam_square) / jnp.sqrt(shampoo_square + 1e-06)
    update_part = (direction * graft_scale[:, :, None, None]).astype(jnp.bfloat16)
    outgoing = (
        update_part.reshape(row_blocks, per_owner, sub_count, part_rows, B)
        .transpose(0, 2, 3, 1, 4)
        .reshape(fsdp_count, part_rows, per_owner * B)
    )
    returned = lax.all_to_all(outgoing, "fsdp", split_axis=0, concat_axis=0, tiled=True)
    ordered = returned.transpose(1, 0, 2).reshape(part_rows, columns, B)
    update = lax.all_gather(
        jnp.take(ordered, row_slots, axis=1).reshape(part_rows, full_width),
        "replica",
        axis=0,
        tiled=True,
    )
    return (
        update,
        left_new.reshape(stats_left.shape),
        right_new.reshape(stats_right.shape),
        moment.reshape(second_moment.shape),
    )


def local(*arrays):
    replicas = lax.axis_size("replica")
    rows, full_width = arrays[0].shape[1:]
    owners = lax.axis_size("fsdp")
    per_owner = full_width // B // owners
    if replicas == 4 and per_owner == replicas and 2 * rows == B and owners == 8:
        return owner_local(*arrays)
    return row_local(*arrays)


def solution(mesh):
    placed = (
        P("replica", "fsdp", None),
        P(),
        P(None, "fsdp", None, "replica", None, None),
        P(None, "fsdp", None, "replica", None, None),
        P(None, "fsdp", None, "replica", None, None),
        P(None, "fsdp", None, "replica", None, None),
        P(None, "fsdp", None, "replica", None, None),
    )
    return jax.shard_map(
        local,
        mesh=mesh,
        in_specs=placed,
        out_specs=(
            P("fsdp", None),
            P(None, "fsdp", None, "replica", None, None),
            P(None, "fsdp", None, "replica", None, None),
            P(None, "fsdp", None, "replica", None, None),
        ),
        check_vma=False,
    )
```
